32 devices in a mesh: ctx: 8 (over z, x), head: 4 (over y, core).
Axes of the slice: x: 2, y: 2, z: 4, core: 2. Of those that a mesh axis runs over, the one named last changes fastest.
Arguments:
- hidden: bfloat16 [1024, 8192], P('ctx', 'head'), may hold values from -6 to 6
- frozen_query_rows: bfloat16 [1024, 3072], P('ctx', 'head'), may hold values from -101 to 101
- frozen_key_rows: bfloat16 [1024, 256], P('ctx'), may hold values from -5 to 5
- frozen_value_rows: bfloat16 [1024, 256], P('ctx'), may hold values from -6 to 6
- adapter_down_factors: bfloat16 [8192, 64], P('head'), may hold values from -0.0625 to 0.0625
- query_up_factor: bfloat16 [32, 3072], P(None, 'head'), may hold values from -1 to 1
- value_up_factor: bfloat16 [32, 256], replicated, may hold values from -1 to 1
- slot_span_order: int32 [16], replicated, may hold values from 0 to 15, each once
Outputs:
- attended: bfloat16 [1024, 3072], P('ctx', 'head')
- log_normalizer: float32 [24, 1024], P('head', 'ctx')
The draws below stay inside these ranges and needn't reach their ends.
Inputs may be any that keep to these rules, and one draw needn't show every extreme that they name: `slot_span_order`: every span number appears once.
All inputs are finite; a program needn't handle non-finite values.
Results may differ from the reference program's by a relative error of at most 0.018.
Values may be sent and summed in bfloat16 or wider, within the bound.
No kernel may reach another device: no remote copies, remote signals or barrier semaphores. Data moves between devices by JAX's collectives and lax.ppermute only.
A program may use at most 64 MiB of HBM per device.

```python
import math
import jax
import jax.numpy as jnp
from jax import lax

MODEL_WIDTH = 8192
HEAD_SIZE = 128
QUERY_HEADS = 24
KEY_VALUE_HEADS = 2
ADAPTER_RANK = 32
CH = 64
SPANS = 16
TOKENS = 1024


def joint_fields(key):
    key_source = jax.random.fold_in(key, 17)
    query_source = jax.random.fold_in(key, 29)
    key_field = jnp.clip(jax.random.normal(key_source, (TOKENS, KEY_VALUE_HEADS * HEAD_SIZE), jnp.float32), -5.0, 5.0)
    query_field = jnp.clip(jax.random.normal(query_source, (TOKENS, QUERY_HEADS * HEAD_SIZE), jnp.float32), -5.0, 5.0)
    return (query_field, key_field)


def draw_frozen_query_rows(key, part):
    return joint_fields(key)[0].astype(jnp.bfloat16)


def draw_frozen_key_rows(key, part):
    return joint_fields(key)[1].astype(jnp.bfloat16)


def level_of(key, dims, pieces, least, high):
    gain = 1.0
    for dim, blocks in pieces:
        draws = jax.random.uniform(jax.random.fold_in(jax.random.fold_in(key, 6), dim), (blocks,), jnp.float32, least / len(pieces), high / len(pieces))
        gain = gain * jnp.repeat(jnp.exp(draws), dims[dim] // blocks).reshape((-1,) + (1,) * (len(dims) - 1 - dim))
    return gain


def gaussian(key, shape, width, bound, shards=(), kind=jnp.bfloat16):
    gain = level_of(key, shape, shards, -0.22, 0.18) if shards else 1.0
    values = jax.random.normal(key, shape, jnp.float32) * width * gain
    return jnp.minimum(jnp.maximum(values, -bound), bound).astype(kind)


def setup_inputs(seed: int = 0) -> dict:
    arg_keys = jax.random.split(jax.random.key(seed), 9)
    hidden = gaussian(arg_keys[0], (TOKENS, MODEL_WIDTH), 1.0, 6.0, ((0, 8), (1, 4)))
    frozen_query_rows = draw_frozen_query_rows(jax.random.fold_in(arg_keys[8], 71), 0)
    frozen_key_rows = draw_frozen_key_rows(jax.random.fold_in(arg_keys[8], 71), 0)
    frozen_value_rows = gaussian(arg_keys[3], (TOKENS, KEY_VALUE_HEADS * HEAD_SIZE), 1.0, 6.0, ((0, 8),))
    adapter_down_factors = gaussian(arg_keys[4], (MODEL_WIDTH, 2 * ADAPTER_RANK), MODEL_WIDTH ** -0.5, 0.0625, ((0, 4),))
    query_up_factor = gaussian(arg_keys[5], (ADAPTER_RANK, QUERY_HEADS * HEAD_SIZE), ADAPTER_RANK ** -0.5, 1.0, ((1, 4),))
    value_up_factor = gaussian(arg_keys[6], (ADAPTER_RANK, KEY_VALUE_HEADS * HEAD_SIZE), ADAPTER_RANK ** -0.5, 1.0)
    slot_span_order = jax.random.permutation(arg_keys[7], SPANS).astype(jnp.int32)
    return dict(hidden=hidden, frozen_query_rows=frozen_query_rows, frozen_key_rows=frozen_key_rows, frozen_value_rows=frozen_value_rows, adapter_down_factors=adapter_down_factors, query_up_factor=query_up_factor, value_up_factor=value_up_factor, slot_span_order=slot_span_order)


adapter_scale = 0.5

def spread_positions(span_ids, span_len):
    return (span_ids[:, None] * span_len + jnp.arange(span_len, dtype=jnp.int32)[None, :]).reshape(-1)

def reference(hidden, frozen_query_rows, frozen_key_rows, frozen_value_rows, adapter_down_factors, query_up_factor, value_up_factor, slot_span_order):
    adapter_bottleneck = jnp.dot(hidden, adapter_down_factors, preferred_element_type=jnp.float32).astype(jnp.bfloat16)
    query_matrix = (frozen_query_rows.astype(jnp.float32) + adapter_scale * jnp.dot(adapter_bottleneck[:, :ADAPTER_RANK], query_up_factor, preferred_element_type=jnp.float32)).astype(jnp.bfloat16)
    value_matrix = (frozen_value_rows.astype(jnp.float32) + adapter_scale * jnp.dot(adapter_bottleneck[:, ADAPTER_RANK:], value_up_factor, preferred_element_type=jnp.float32)).astype(jnp.bfloat16)
    position = spread_positions(slot_span_order.astype(jnp.int32), CH).astype(jnp.int32)
    group_size = QUERY_HEADS // KEY_VALUE_HEADS
    query_block = math.gcd(TOKENS, 512)
    block_count = TOKENS // query_block
    factor = 1.0 / math.sqrt(HEAD_SIZE)

    def one_tile(flat):
        flat = flat.astype(jnp.int32)
        zero_index = jnp.zeros((), jnp.int32)
        head_id = (flat // block_count).astype(jnp.int32)
        block_id = (flat % block_count).astype(jnp.int32)
        row_start = (block_id * query_block).astype(jnp.int32)
        head_column = (head_id * HEAD_SIZE).astype(jnp.int32)
        kv_column = (head_id // group_size * HEAD_SIZE).astype(jnp.int32)
        q_rows = lax.dynamic_slice(query_matrix, (row_start, head_column), (query_block, HEAD_SIZE)).astype(jnp.float32)
        k_rows = lax.dynamic_slice(frozen_key_rows, (zero_index, kv_column), (TOKENS, HEAD_SIZE)).astype(jnp.float32)
        v_rows = lax.dynamic_slice(value_matrix, (zero_index, kv_column), (TOKENS, HEAD_SIZE)).astype(jnp.float32)
        q_pos = lax.dynamic_slice(position, (row_start,), (query_block,))
        scores = lax.dot_general(q_rows, k_rows, (((1,), (1,)), ((), ())), precision=lax.Precision.HIGHEST) * factor
        visible = position[None, :] <= q_pos[:, None]
        row_max = lax.optimization_barrier(jnp.max(jnp.where(visible, scores, -jnp.inf), axis=1))
        weights = jnp.where(visible, jnp.exp(scores - row_max[:, None]), 0.0)
        denominator = lax.optimization_barrier(jnp.sum(weights, axis=1))
        rounded = lax.optimization_barrier(weights.astype(jnp.bfloat16)).astype(jnp.float32)
        numerator = jnp.dot(rounded, v_rows, precision=lax.Precision.HIGHEST)
        result = (numerator / denominator[:, None]).astype(jnp.bfloat16)
        return (result, row_max + jnp.log(denominator))
    tiles, normals = lax.map(one_tile, jnp.arange(QUERY_HEADS * block_count, dtype=jnp.int32))
    attended = tiles.reshape(QUERY_HEADS, TOKENS, HEAD_SIZE).transpose(1, 0, 2).reshape(TOKENS, QUERY_HEADS * HEAD_SIZE)
    return (attended, normals.reshape(QUERY_HEADS, TOKENS))
```

```python
import functools
import math

import jax
import jax.numpy as jnp
from jax import lax
from jax.experimental import pallas as pl
from jax.experimental.pallas import tpu as pltpu
from jax.sharding import PartitionSpec as P

HEAD_SIZE = 128
KEY_VALUE_HEADS = 2
ADAPTER_RANK = 32
ADAPTER_SCALE = 0.5
MASKED = -1e30
AXES = ("ctx", "head")


def exchange(value, ctx_bit, head_bits):
    ctx_count, head_count = lax.axis_size("ctx"), lax.axis_size("head")
    pairs = [
        (i * head_count + h, (i ^ ctx_bit) * head_count + (h ^ head_bits))
        for i in range(ctx_count)
        for h in range(head_count)
    ]
    return lax.ppermute(value, AXES, pairs)


def gather_patterns(bits):
    patterns = [0]
    for bit in bits:
        patterns += [p ^ bit for p in patterns]
    return patterns


def attention_kernel(
    patterns,
    place_ref,
    order_ref,
    frozen_query_ref,
    low_ref,
    query_up_ref,
    kv_ref,
    low_value_ref,
    value_up_ref,
    attended_ref,
    normalizer_ref,
    bias_ref,
    value_ref,
):
    tok_dev, width = frozen_query_ref.shape
    span = tok_dev // 2
    heads = width // HEAD_SIZE
    ctx, side = place_ref[0], place_ref[1]
    blocks = len(patterns)
    key_count = kv_ref.shape[0]

    queries = (
        frozen_query_ref[...].astype(jnp.float32)
        + ADAPTER_SCALE
        * jnp.dot(
            low_ref[:, :ADAPTER_RANK], query_up_ref[...], preferred_element_type=jnp.float32
        )
    ).astype(jnp.bfloat16)

    row = lax.broadcasted_iota(jnp.int32, (tok_dev, HEAD_SIZE), 0)
    lane = lax.broadcasted_iota(jnp.int32, (tok_dev, HEAD_SIZE), 1)
    query_pos = (
        jnp.where(row < span, order_ref[2 * ctx], order_ref[2 * ctx + 1]) * span + row % span
    )
    halves = []
    for entry in range(2 * blocks):
        pattern = patterns[entry % blocks]
        half = (side + pattern.bit_count() + entry // blocks) % 2
        halves.append((entry % blocks, half, order_ref[2 * (ctx ^ pattern) + half]))
    for tile in range(blocks):
        first, second = halves[2 * tile], halves[2 * tile + 1]
        key_pos = jnp.where(lane < span, first[2], second[2]) * span + lane % span
        bias_ref[:, tile * HEAD_SIZE : (tile + 1) * HEAD_SIZE] = jnp.where(
            key_pos <= query_pos, 0.0, MASKED
        )
    for entry in range(2 * blocks):
        index, half, _ = halves[entry]
        rows = pl.ds(pl.multiple_of(index * tok_dev + half * span, span), span)
        here = slice(entry * span, (entry + 1) * span)
        value_ref[here, :HEAD_SIZE] = (
            kv_ref[here, HEAD_SIZE:].astype(jnp.float32)
            + ADAPTER_SCALE
            * jnp.dot(
                low_value_ref[rows, :], value_up_ref[...], preferred_element_type=jnp.float32
            )
        ).astype(jnp.bfloat16)
    value_ref[:, HEAD_SIZE:] = jnp.ones((key_count, HEAD_SIZE), jnp.bfloat16)

    keys = kv_ref[:, :HEAD_SIZE]
    diagonal = row == lane
    factor = 1.0 / math.sqrt(HEAD_SIZE)
    for head in range(heads):
        columns = slice(head * HEAD_SIZE, (head + 1) * HEAD_SIZE)
        scores = (
            lax.dot_general(
                queries[:, columns], keys, (((1,), (1,)), ((), ())), preferred_element_type=jnp.float32
            )
            * factor
            + bias_ref[...]
        )
        row_max = jnp.max(scores, axis=1, keepdims=True)
        weights = jnp.exp(scores - row_max).astype(jnp.bfloat16)
        sums = jnp.dot(weights, value_ref[...], preferred_element_type=jnp.float32)
        total = sums[:, HEAD_SIZE:]
        attended_ref[:, columns] = (sums[:, :HEAD_SIZE] / total).astype(jnp.bfloat16)
        normal = row_max + jnp.log(total)
        normalizer_ref[head : head + 1, :] = jnp.sum(
            jnp.where(diagonal, normal, 0.0), axis=0, keepdims=True
        )


def attend(patterns, place, order, frozen_query, low, query_up, kv, low_value, value_up):
    tok_dev, width = frozen_query.shape
    heads = width // HEAD_SIZE
    key_count = kv.shape[0]
    smem = pl.BlockSpec(memory_space=pltpu.SMEM)
    vmem = pl.BlockSpec(memory_space=pltpu.VMEM)
    return pl.pallas_call(
        functools.partial(attention_kernel, patterns),
        out_shape=(
            jax.ShapeDtypeStruct((tok_dev, width), jnp.bfloat16),
            jax.ShapeDtypeStruct((heads, tok_dev), jnp.float32),
        ),
        in_specs=[smem, smem] + [vmem] * 6,
        out_specs=(vmem, vmem),
        scratch_shapes=[
            pltpu.VMEM((tok_dev, key_count), jnp.float32),
            pltpu.VMEM((key_count, 2 * HEAD_SIZE), jnp.bfloat16),
        ],
        compiler_params=pltpu.CompilerParams(vmem_limit_bytes=32 * 1024 * 1024),
        cost_estimate=pl.CostEstimate(
            flops=4 * tok_dev * width * key_count,
            bytes_accessed=2 * (tok_dev * width * 2 + key_count * 2 * HEAD_SIZE),
            transcendentals=heads * tok_dev * key_count,
        ),
    )(place, order, frozen_query, low, query_up, kv, low_value, value_up)


def attend_long(patterns, place, order, frozen_query, low, query_up, kv, low_value, value_up):
    tok_dev, width = frozen_query.shape
    span = tok_dev // 2
    heads = width // HEAD_SIZE
    blocks = len(patterns)
    ctx, side = place[0], place[1]
    queries = (
        frozen_query.astype(jnp.float32)
        + ADAPTER_SCALE
        * jnp.dot(low[:, :ADAPTER_RANK], query_up, preferred_element_type=jnp.float32)
    ).astype(jnp.bfloat16)
    queries = queries.reshape(tok_dev, heads, HEAD_SIZE).transpose(1, 0, 2).reshape(-1, HEAD_SIZE)
    pattern = jnp.tile(jnp.array(patterns, jnp.int32), 2)
    parity = jnp.array([p.bit_count() for p in patterns] + [p.bit_count() + 1 for p in patterns])
    half = (side + parity.astype(jnp.int32)) % 2
    key_spans = order[2 * (ctx ^ pattern) + half]
    inner = jnp.arange(span, dtype=jnp.int32)
    key_pos = (key_spans[:, None] * span + inner).reshape(-1)
    query_spans = lax.dynamic_slice_in_dim(order, 2 * ctx, 2)
    query_pos = jnp.tile((query_spans[:, None] * span + inner).reshape(-1), heads)
    index = jnp.tile(jnp.arange(blocks, dtype=jnp.int32), 2)
    low_rows = low_value.reshape(2 * blocks, span, ADAPTER_RANK)[2 * index + half]
    values = (
        kv[:, HEAD_SIZE:].astype(jnp.float32)
        + ADAPTER_SCALE
        * jnp.dot(
            low_rows.reshape(-1, ADAPTER_RANK), value_up, preferred_element_type=jnp.float32
        )
    ).astype(jnp.bfloat16)
    chunk = math.gcd(kv.shape[0], 1024)

    def step(number, state):
        top, total, summed = state
        at = number * chunk
        keys = lax.dynamic_slice_in_dim(kv, at, chunk, 0)[:, :HEAD_SIZE]
        scores = lax.dot_general(
            queries, keys, (((1,), (1,)), ((), ())), preferred_element_type=jnp.float32
        ) * (1.0 / math.sqrt(HEAD_SIZE))
        visible = lax.dynamic_slice_in_dim(key_pos, at, chunk)[None, :] <= query_pos[:, None]
        new_top = jnp.maximum(top, jnp.max(jnp.where(visible, scores, MASKED), axis=1))
        scale = jnp.exp(top - new_top)
        weights = jnp.where(visible, jnp.exp(scores - new_top[:, None]), 0.0)
        summed = summed * scale[:, None] + jnp.dot(
            weights.astype(jnp.bfloat16),
            lax.dynamic_slice_in_dim(values, at, chunk, 0),
            preferred_element_type=jnp.float32,
        )
        return (new_top, total * scale + jnp.sum(weights, axis=1), summed)

    rows = heads * tok_dev
    top, total, summed = lax.fori_loop(
        0,
        kv.shape[0] // chunk,
        step,
        (
            jnp.full((rows,), MASKED, jnp.float32),
            jnp.zeros((rows,), jnp.float32),
            jnp.zeros((rows, HEAD_SIZE), jnp.float32),
        ),
    )
    attended = (summed / total[:, None]).astype(jnp.bfloat16)
    attended = attended.reshape(heads, tok_dev, HEAD_SIZE).transpose(1, 0, 2)
    return attended.reshape(tok_dev, width), (top + jnp.log(total)).reshape(heads, tok_dev)


def local(
    hidden,
    frozen_query_rows,
    frozen_key_rows,
    frozen_value_rows,
    adapter_down_factors,
    query_up_factor,
    value_up_factor,
    slot_span_order,
):
    ctx_count, head_count = lax.axis_size("ctx"), lax.axis_size("head")
    ctx, head = lax.axis_index("ctx"), lax.axis_index("head")
    side = head % 2
    group = head // (head_count // KEY_VALUE_HEADS)
    bits = [ctx_count >> k for k in range(1, ctx_count.bit_length())]
    if len(bits) == 3:
        bits = [bits[0], bits[2], bits[1]]
    patterns = gather_patterns(bits)
    half = hidden.shape[0] // 2

    partial = jnp.dot(hidden, adapter_down_factors, preferred_element_type=jnp.float32)
    low = partial.astype(jnp.bfloat16)
    head_bit = 1
    while head_bit < head_count:
        other = exchange(low, 0, head_bit | 1)
        low = (low.astype(jnp.float32) + other.astype(jnp.float32)).astype(jnp.bfloat16)
        head_bit *= 2

    def own_half(rows):
        return lax.dynamic_slice(
            rows, (side * half, group * HEAD_SIZE), (half, HEAD_SIZE)
        )

    kv = jnp.concatenate([own_half(frozen_key_rows), own_half(frozen_value_rows)], axis=1)
    low_value = low[:, ADAPTER_RANK:]
    for bit in bits:
        low_value = jnp.concatenate([low_value, exchange(low_value, bit, 1)], axis=0)
        kv = jnp.concatenate([kv, exchange(kv, bit, 1)], axis=0)
    kv = jnp.concatenate([kv, exchange(kv, 0, 1)], axis=0)
    value_up = lax.dynamic_slice_in_dim(value_up_factor, group * HEAD_SIZE, HEAD_SIZE, 1)
    place = jnp.stack([ctx, side]).astype(jnp.int32)
    run = attend if kv.shape[0] <= 1024 else attend_long
    return run(
        patterns, place, slot_span_order, frozen_query_rows, low, query_up_factor, kv, low_value, value_up
    )


def solution(mesh):
    placed = (
        P("ctx", "head"),
        P("ctx", "head"),
        P("ctx", None),
        P("ctx", None),
        P("head", None),
        P(None, "head"),
        P(),
        P(),
    )
    return jax.shard_map(
        local,
        mesh=mesh,
        in_specs=placed,
        out_specs=(P("ctx", "head"), P("head", "ctx")),
        check_vma=False,
    )
```

```python
import functools
import math

import jax
import jax.numpy as jnp
from jax import lax
from jax.experimental import pallas as pl
from jax.experimental.pallas import tpu as pltpu
from jax.sharding import PartitionSpec as P

HEAD_SIZE = 128
KEY_VALUE_HEADS = 2
ADAPTER_RANK = 32
ADAPTER_SCALE = 0.5
MASKED = -1e30
AXES = ("ctx", "head")
SCORE_FACTOR = math.log2(math.e) / math.sqrt(HEAD_SIZE)
VMEM_LIMIT = 24 * 1024 * 1024


def exchange(value, ctx_bit, head_bits):
    ctx_count, head_count = lax.axis_size("ctx"), lax.axis_size("head")
    pairs = [
        (i * head_count + h, (i ^ ctx_bit) * head_count + (h ^ head_bits))
        for i in range(ctx_count)
        for h in range(head_count)
    ]
    return lax.ppermute(value, AXES, pairs)


def gather_patterns(bits):
    patterns = [0]
    for bit in bits:
        patterns += [p ^ bit for p in patterns]
    return patterns


def half_blocks(patterns, ctx, side):
    blocks = len(patterns)
    found = []
    for entry in range(2 * blocks):
        pattern = patterns[entry % blocks]
        half = (side + pattern.bit_count() + entry // blocks) % 2
        found.append((entry % blocks, half, 2 * (ctx ^ pattern) + half))
    return found


def diagonal_row(matrix):
    row = lax.broadcasted_iota(jnp.int32, matrix.shape, 0)
    lane = lax.broadcasted_iota(jnp.int32, matrix.shape, 1)
    return jnp.sum(jnp.where(row == lane, matrix, 0.0), axis=0, keepdims=True)


def prologue_kernel(
    hidden_ref, down_ref, key_ref, value_ref, low_ref, kv_ref, hidden_buf, down_buf, sems, kv_sems
):
    head = lax.axis_index("head")
    side = head % 2
    group = head // (lax.axis_size("head") // KEY_VALUE_HEADS)
    half = kv_ref.shape[0]
    rows = pl.ds(pl.multiple_of(side * half, half), half)
    columns = pl.ds(pl.multiple_of(group * HEAD_SIZE, HEAD_SIZE), HEAD_SIZE)
    chunks = sems.shape[0]
    depth = down_ref.shape[0] // chunks
    copies = []
    for chunk in range(chunks):
        part = pl.ds(chunk * depth, depth)
        pair = (
            pltpu.make_async_copy(hidden_ref.at[:, part], hidden_buf.at[:, part], sems.at[chunk, 0]),
            pltpu.make_async_copy(down_ref.at[part, :], down_buf.at[part, :], sems.at[chunk, 1]),
        )
        for copy in pair:
            copy.start()
        copies.append(pair)
    kv_copies = [
        pltpu.make_async_copy(
            ref.at[rows, columns], kv_ref.at[:, pl.ds(n * HEAD_SIZE, HEAD_SIZE)], kv_sems.at[n]
        )
        for n, ref in enumerate((key_ref, value_ref))
    ]
    for copy in kv_copies:
        copy.start()
    total = jnp.zeros((hidden_ref.shape[0], down_ref.shape[1]), jnp.float32)
    for chunk in range(chunks):
        for copy in copies[chunk]:
            copy.wait()
        part = slice(chunk * depth, (chunk + 1) * depth)
        total += jnp.dot(
            hidden_buf[:, part], down_buf[part, :], preferred_element_type=jnp.float32
        )
    low_ref[...] = total.T.astype(jnp.bfloat16)
    for copy in kv_copies:
        copy.wait()


def prologue(hidden, down, keys, values):
    tok_dev, depth = hidden.shape
    rank = down.shape[1]
    chunks = 4
    any_space = pl.BlockSpec(memory_space=pl.ANY)
    vmem = pl.BlockSpec(memory_space=pltpu.VMEM)
    return pl.pallas_call(
        prologue_kernel,
        out_shape=(
            jax.ShapeDtypeStruct((rank, tok_dev), jnp.bfloat16),
            jax.ShapeDtypeStruct((tok_dev // 2, 2 * HEAD_SIZE), jnp.bfloat16),
        ),
        in_specs=[any_space] * 4,
        out_specs=(vmem, vmem),
        scratch_shapes=[
            pltpu.VMEM(hidden.shape, jnp.bfloat16),
            pltpu.VMEM(down.shape, jnp.bfloat16),
            pltpu.SemaphoreType.DMA((chunks, 2)),
            pltpu.SemaphoreType.DMA((2,)),
        ],
        compiler_params=pltpu.CompilerParams(vmem_limit_bytes=VMEM_LIMIT),
        cost_estimate=pl.CostEstimate(
            flops=2 * tok_dev * depth * rank, bytes_accessed=tok_dev * depth * 4, transcendentals=0
        ),
    )(hidden, down, keys, values)


def weights_kernel(
    patterns, order_ref, frozen_query_ref, low_ref, query_up_ref, kv_ref, weights_ref, top_ref, bias_ref
):
    tok_dev, width = frozen_query_ref.shape
    span = tok_dev // 2
    heads = width // HEAD_SIZE
    ctx, side = lax.axis_index("ctx"), lax.axis_index("head") % 2

    queries = (
        frozen_query_ref[...].astype(jnp.float32)
        + ADAPTER_SCALE
        * lax.dot_general(
            low_ref[:ADAPTER_RANK, :],
            query_up_ref[...],
            (((0,), (0,)), ((), ())),
            preferred_element_type=jnp.float32,
        )
    ).astype(jnp.bfloat16)

    row = lax.broadcasted_iota(jnp.int32, (tok_dev, HEAD_SIZE), 0)
    lane = lax.broadcasted_iota(jnp.int32, (tok_dev, HEAD_SIZE), 1)
    query_pos = (
        jnp.where(row < span, order_ref[2 * ctx], order_ref[2 * ctx + 1]) * span + row % span
    )
    halves = half_blocks(patterns, ctx, side)
    for tile in range(len(patterns)):
        first, second = order_ref[halves[2 * tile][2]], order_ref[halves[2 * tile + 1][2]]
        key_pos = jnp.where(lane < span, first, second) * span + lane % span
        bias_ref[:, tile * HEAD_SIZE : (tile + 1) * HEAD_SIZE] = jnp.where(
            key_pos <= query_pos, 0.0, MASKED
        )
    keys = kv_ref[:, :HEAD_SIZE]
    for head in range(heads):
        scores = (
            lax.dot_general(
                queries[:, head * HEAD_SIZE : (head + 1) * HEAD_SIZE],
                keys,
                (((1,), (1,)), ((), ())),
                preferred_element_type=jnp.float32,
            )
            * SCORE_FACTOR
            + bias_ref[...]
        )
        top = jnp.max(scores, axis=1, keepdims=True)
        weights_ref[head * tok_dev : (head + 1) * tok_dev, :] = jnp.exp2(scores - top).astype(
            jnp.bfloat16
        )
        top_ref[head : head + 1, :] = diagonal_row(jnp.broadcast_to(top, (tok_dev, tok_dev)))


def make_weights(patterns, order, frozen_query, low, query_up, kv):
    tok_dev, width = frozen_query.shape
    heads = width // HEAD_SIZE
    key_count = kv.shape[0]
    vmem = pl.BlockSpec(memory_space=pltpu.VMEM)
    return pl.pallas_call(
        functools.partial(weights_kernel, patterns),
        out_shape=(
            jax.ShapeDtypeStruct((heads * tok_dev, key_count), jnp.bfloat16),
            jax.ShapeDtypeStruct((heads, tok_dev), jnp.float32),
        ),
        in_specs=[pl.BlockSpec(memory_space=pltpu.SMEM)] + [vmem] * 4,
        out_specs=(vmem, vmem),
        scratch_shapes=[pltpu.VMEM((tok_dev, key_count), jnp.float32)],
        compiler_params=pltpu.CompilerParams(vmem_limit_bytes=VMEM_LIMIT),
        cost_estimate=pl.CostEstimate(
            flops=2 * tok_dev * width * key_count,
            bytes_accessed=2 * tok_dev * heads * key_count,
            transcendentals=heads * tok_dev * key_count,
        ),
    )(order, frozen_query, low, query_up, kv)


def values_kernel(
    patterns, weights_ref, top_ref, kv_ref, low_value_ref, value_up_ref, attended_ref, normalizer_ref, value_ref
):
    heads, tok_dev = top_ref.shape
    span = tok_dev // 2
    head_index = lax.axis_index("head")
    ctx, side = lax.axis_index("ctx"), head_index % 2
    group = head_index // (lax.axis_size("head") // KEY_VALUE_HEADS)
    value_up = value_up_ref[:, pl.ds(pl.multiple_of(group * HEAD_SIZE, HEAD_SIZE), HEAD_SIZE)]
    updates = [
        ADAPTER_SCALE
        * lax.dot_general(
            low_value_ref[n * ADAPTER_RANK : (n + 1) * ADAPTER_RANK, :],
            value_up,
            (((0,), (0,)), ((), ())),
            preferred_element_type=jnp.float32,
        )
        for n in range(len(patterns))
    ]
    for entry, (block, half, _) in enumerate(half_blocks(patterns, ctx, side)):
        here = slice(entry * span, (entry + 1) * span)
        update = jnp.where(half == 0, updates[block][:span], updates[block][span:])
        value_ref[here, :HEAD_SIZE] = (
            kv_ref[here, HEAD_SIZE:].astype(jnp.float32) + update
        ).astype(jnp.bfloat16)
    value_ref[:, HEAD_SIZE:] = jnp.ones((value_ref.shape[0], HEAD_SIZE), jnp.bfloat16)
    for head in range(heads):
        sums = jnp.dot(
            weights_ref[head * tok_dev : (head + 1) * tok_dev, :],
            value_ref[...],
            preferred_element_type=jnp.float32,
        )
        total = sums[:, HEAD_SIZE:]
        attended_ref[:, head * HEAD_SIZE : (head + 1) * HEAD_SIZE] = (
            sums[:, :HEAD_SIZE] / total
        ).astype(jnp.bfloat16)
        normalizer_ref[head : head + 1, :] = top_ref[head : head + 1, :] * math.log(2.0) + jnp.log(
            diagonal_row(total)
        )


def weigh_values(patterns, weights, top, kv, low_value, value_up):
    heads, tok_dev = top.shape
    key_count = kv.shape[0]
    width = heads * HEAD_SIZE
    vmem = pl.BlockSpec(memory_space=pltpu.VMEM)
    return pl.pallas_call(
        functools.partial(values_kernel, patterns),
        out_shape=(
            jax.ShapeDtypeStruct((tok_dev, width), jnp.bfloat16),
            jax.ShapeDtypeStruct((heads, tok_dev), jnp.float32),
        ),
        in_specs=[vmem] * 5,
        out_specs=(vmem, vmem),
        scratch_shapes=[pltpu.VMEM((key_count, 2 * HEAD_SIZE), jnp.bfloat16)],
        compiler_params=pltpu.CompilerParams(vmem_limit_bytes=VMEM_LIMIT),
        cost_estimate=pl.CostEstimate(
            flops=2 * tok_dev * width * key_count,
            bytes_accessed=2 * tok_dev * heads * key_count,
            transcendentals=0,
        ),
    )(weights, top, kv, low_value, value_up)


def attend_long(patterns, ctx, head, order, frozen_query, low, query_up, kv, low_value, value_up):
    tok_dev, width = frozen_query.shape
    span = tok_dev // 2
    heads = width // HEAD_SIZE
    blocks = len(patterns)
    side = head % 2
    group = head // (lax.axis_size("head") // KEY_VALUE_HEADS)
    value_up = lax.dynamic_slice_in_dim(value_up, group * HEAD_SIZE, HEAD_SIZE, 1)
    low = low.T
    low_value = low_value.reshape(blocks, ADAPTER_RANK, tok_dev).transpose(0, 2, 1)
    queries = (
        frozen_query.astype(jnp.float32)
        + ADAPTER_SCALE
        * jnp.dot(low[:, :ADAPTER_RANK], query_up, preferred_element_type=jnp.float32)
    ).astype(jnp.bfloat16)
    queries = queries.reshape(tok_dev, heads, HEAD_SIZE).transpose(1, 0, 2).reshape(-1, HEAD_SIZE)
    pattern = jnp.tile(jnp.array(patterns, jnp.int32), 2)
    parity = jnp.array([p.bit_count() for p in patterns] + [p.bit_count() + 1 for p in patterns])
    half = (side + parity.astype(jnp.int32)) % 2
    key_spans = order[2 * (ctx ^ pattern) + half]
    inner = jnp.arange(span, dtype=jnp.int32)
    key_pos = (key_spans[:, None] * span + inner).reshape(-1)
    query_spans = lax.dynamic_slice_in_dim(order, 2 * ctx, 2)
    query_pos = jnp.tile((query_spans[:, None] * span + inner).reshape(-1), heads)
    index = jnp.tile(jnp.arange(blocks, dtype=jnp.int32), 2)
    low_rows = low_value.reshape(2 * blocks, span, ADAPTER_RANK)[2 * index + half]
    values = (
        kv[:, HEAD_SIZE:].astype(jnp.float32)
        + ADAPTER_SCALE
        * jnp.dot(
            low_rows.reshape(-1, ADAPTER_RANK), value_up, preferred_element_type=jnp.float32
        )
    ).astype(jnp.bfloat16)
    chunk = math.gcd(kv.shape[0], 1024)

    def step(number, state):
        top, total, summed = state
        at = number * chunk
        keys = lax.dynamic_slice_in_dim(kv, at, chunk, 0)[:, :HEAD_SIZE]
        scores = lax.dot_general(
            queries, keys, (((1,), (1,)), ((), ())), preferred_element_type=jnp.float32
        ) * (1.0 / math.sqrt(HEAD_SIZE))
        visible = lax.dynamic_slice_in_dim(key_pos, at, chunk)[None, :] <= query_pos[:, None]
        new_top = jnp.maximum(top, jnp.max(jnp.where(visible, scores, MASKED), axis=1))
        scale = jnp.exp(top - new_top)
        weights = jnp.where(visible, jnp.exp(scores - new_top[:, None]), 0.0)
        summed = summed * scale[:, None] + jnp.dot(
            weights.astype(jnp.bfloat16),
            lax.dynamic_slice_in_dim(values, at, chunk, 0),
            preferred_element_type=jnp.float32,
        )
        return (new_top, total * scale + jnp.sum(weights, axis=1), summed)

    rows = heads * tok_dev
    top, total, summed = lax.fori_loop(
        0,
        kv.shape[0] // chunk,
        step,
        (
            jnp.full((rows,), MASKED, jnp.float32),
            jnp.zeros((rows,), jnp.float32),
            jnp.zeros((rows, HEAD_SIZE), jnp.float32),
        ),
    )
    attended = (summed / total[:, None]).astype(jnp.bfloat16)
    attended = attended.reshape(heads, tok_dev, HEAD_SIZE).transpose(1, 0, 2)
    return attended.reshape(tok_dev, width), (top + jnp.log(total)).reshape(heads, tok_dev)


def local(
    hidden,
    frozen_query_rows,
    frozen_key_rows,
    frozen_value_rows,
    adapter_down_factors,
    query_up_factor,
    value_up_factor,
    slot_span_order,
):
    ctx_count, head_count = lax.axis_size("ctx"), lax.axis_size("head")
    ctx, head = lax.axis_index("ctx"), lax.axis_index("head")
    bits = [ctx_count >> k for k in range(1, ctx_count.bit_length())]
    if len(bits) == 3:
        bits = [bits[0], bits[2], bits[1]]
    patterns = gather_patterns(bits)

    low, kv = prologue(hidden, adapter_down_factors, frozen_key_rows, frozen_value_rows)
    head_bit = 1
    while head_bit < head_count:
        other = exchange(low, 0, head_bit | 1)
        low = (low.astype(jnp.float32) + other.astype(jnp.float32)).astype(jnp.bfloat16)
        if head_bit == 1:
            low, kv = lax.optimization_barrier((low, kv))
        head_bit *= 2
    low_value = low[ADAPTER_RANK:]
    for bit in bits:
        low_value = jnp.concatenate([low_value, exchange(low_value, bit, 1)], axis=0)
        kv = jnp.concatenate([kv, exchange(kv, bit, 1)], axis=0)
    kv = jnp.concatenate([kv, exchange(kv, 0, 1)], axis=0)
    if kv.shape[0] > 1024:
        return attend_long(
            patterns, ctx, head, slot_span_order, frozen_query_rows, low, query_up_factor, kv, low_value, value_up_factor
        )
    weights, top = make_weights(
        patterns, slot_span_order, frozen_query_rows, low, query_up_factor, kv
    )
    return weigh_values(patterns, weights, top, kv, low_value, value_up_factor)


def solution(mesh):
    placed = (
        P("ctx", "head"),
        P("ctx", "head"),
        P("ctx", None),
        P("ctx", None),
        P("head", None),
        P(None, "head"),
        P(),
        P(),
    )
    return jax.shard_map(
        local,
        mesh=mesh,
        in_specs=placed,
        out_specs=(P("ctx", "head"), P("head", "ctx")),
        check_vma=False,
    )
```

```python
import functools
import math

import jax
import jax.numpy as jnp
from jax import lax
from jax.experimental import pallas as pl
from jax.experimental.pallas import tpu as pltpu
from jax.sharding import PartitionSpec as P

HEAD_SIZE = 128
KEY_VALUE_HEADS = 2
ADAPTER_RANK = 32
ADAPTER_SCALE = 0.5
MASKED = -1e30
AXES = ("ctx", "head")
SCORE_FACTOR = math.log2(math.e) / math.sqrt(HEAD_SIZE)
VMEM_LIMIT = 24 * 1024 * 1024


def exchange(value, ctx_bit, head_bits):
    ctx_count, head_count = lax.axis_size("ctx"), lax.axis_size("head")
    pairs = [
        (i * head_count + h, (i ^ ctx_bit) * head_count + (h ^ head_bits))
        for i in range(ctx_count)
        for h in range(head_count)
    ]
    return lax.ppermute(value, AXES, pairs)


def gather_patterns(bits):
    patterns = [0]
    for bit in bits:
        patterns += [p ^ bit for p in patterns]
    return patterns


def half_blocks(patterns, ctx, side):
    blocks = len(patterns)
    found = []
    for entry in range(2 * blocks):
        pattern = patterns[entry % blocks]
        half = (side + pattern.bit_count() + entry // blocks) % 2
        found.append((entry % blocks, half, 2 * (ctx ^ pattern) + half))
    return found


def diagonal_row(matrix):
    row = lax.broadcasted_iota(jnp.int32, matrix.shape, 0)
    lane = lax.broadcasted_iota(jnp.int32, matrix.shape, 1)
    return jnp.sum(jnp.where(row == lane, matrix, 0.0), axis=0, keepdims=True)


def prologue_kernel(
    hidden_ref, down_ref, key_ref, value_ref, low_ref, kv_ref, hidden_buf, down_buf, sems, kv_sems
):
    head = lax.axis_index("head")
    side = head % 2
    group = head // (lax.axis_size("head") // KEY_VALUE_HEADS)
    half = kv_ref.shape[0]
    rows = pl.ds(pl.multiple_of(side * half, half), half)
    columns = pl.ds(pl.multiple_of(group * HEAD_SIZE, HEAD_SIZE), HEAD_SIZE)
    chunks = sems.shape[0]
    depth = down_ref.shape[1] // chunks
    copies = []
    for chunk in range(chunks):
        part = pl.ds(chunk * depth, depth)
        pair = (
            pltpu.make_async_copy(hidden_ref.at[:, part], hidden_buf.at[:, part], sems.at[chunk, 0]),
            pltpu.make_async_copy(down_ref.at[:, part], down_buf.at[:, part], sems.at[chunk, 1]),
        )
        for copy in pair:
            copy.start()
        copies.append(pair)
    kv_copies = [
        pltpu.make_async_copy(
            ref.at[rows, columns], kv_ref.at[:, pl.ds(n * HEAD_SIZE, HEAD_SIZE)], kv_sems.at[n]
        )
        for n, ref in enumerate((key_ref, value_ref))
    ]
    for copy in kv_copies:
        copy.start()
    total = jnp.zeros(low_ref.shape, jnp.float32)
    for chunk in range(chunks):
        for copy in copies[chunk]:
            copy.wait()
        part = slice(chunk * depth, (chunk + 1) * depth)
        total += lax.dot_general(
            down_buf[:, part],
            hidden_buf[:, part],
            (((1,), (1,)), ((), ())),
            preferred_element_type=jnp.float32,
        )
    low_ref[...] = total.astype(jnp.bfloat16)
    for copy in kv_copies:
        copy.wait()


def prologue(hidden, down, keys, values):
    tok_dev, depth = hidden.shape
    rank = down.shape[0]
    chunks = 4
    any_space = pl.BlockSpec(memory_space=pltpu.HBM)
    vmem = pl.BlockSpec(memory_space=pltpu.VMEM)
    return pl.pallas_call(
        prologue_kernel,
        out_shape=(
            jax.ShapeDtypeStruct((rank, tok_dev), jnp.bfloat16),
            jax.ShapeDtypeStruct((tok_dev // 2, 2 * HEAD_SIZE), jnp.bfloat16),
        ),
        in_specs=[any_space] * 4,
        out_specs=(vmem, vmem),
        scratch_shapes=[
            pltpu.VMEM(hidden.shape, jnp.bfloat16),
            pltpu.VMEM(down.shape, jnp.bfloat16),
            pltpu.SemaphoreType.DMA((chunks, 2)),
            pltpu.SemaphoreType.DMA((2,)),
        ],
        compiler_params=pltpu.CompilerParams(vmem_limit_bytes=VMEM_LIMIT),
        cost_estimate=pl.CostEstimate(
            flops=2 * tok_dev * depth * rank, bytes_accessed=tok_dev * depth * 4, transcendentals=0
        ),
    )(*(pltpu.with_memory_space_constraint(x, pltpu.HBM) for x in (hidden, down, keys, values)))


def weights_kernel(
    patterns, order_ref, frozen_query_ref, low_ref, query_up_ref, kv_ref, weights_ref, top_ref, bias_ref
):
    tok_dev, width = frozen_query_ref.shape
    span = tok_dev // 2
    heads = width // HEAD_SIZE
    ctx, side = lax.axis_index("ctx"), lax.axis_index("head") % 2

    queries = (
        frozen_query_ref[...].astype(jnp.float32)
        + ADAPTER_SCALE
        * lax.dot_general(
            low_ref[:ADAPTER_RANK, :],
            query_up_ref[...],
            (((0,), (0,)), ((), ())),
            preferred_element_type=jnp.float32,
        )
    ).astype(jnp.bfloat16)

    row = lax.broadcasted_iota(jnp.int32, (tok_dev, HEAD_SIZE), 0)
    lane = lax.broadcasted_iota(jnp.int32, (tok_dev, HEAD_SIZE), 1)
    query_pos = (
        jnp.where(row < span, order_ref[2 * ctx], order_ref[2 * ctx + 1]) * span + row % span
    )
    halves = half_blocks(patterns, ctx, side)
    for tile in range(len(patterns)):
        first, second = order_ref[halves[2 * tile][2]], order_ref[halves[2 * tile + 1][2]]
        key_pos = jnp.where(lane < span, first, second) * span + lane % span
        bias_ref[:, tile * HEAD_SIZE : (tile + 1) * HEAD_SIZE] = jnp.where(
            key_pos <= query_pos, 0.0, MASKED
        )
    keys = kv_ref[:, :HEAD_SIZE]
    for head in range(heads):
        scores = (
            lax.dot_general(
                queries[:, head * HEAD_SIZE : (head + 1) * HEAD_SIZE],
                keys,
                (((1,), (1,)), ((), ())),
                preferred_element_type=jnp.float32,
            )
            * SCORE_FACTOR
            + bias_ref[...]
        )
        top = jnp.max(scores, axis=1, keepdims=True)
        weights_ref[head * tok_dev : (head + 1) * tok_dev, :] = jnp.exp2(scores - top).astype(
            jnp.bfloat16
        )
        top_ref[head : head + 1, :] = diagonal_row(jnp.broadcast_to(top, (tok_dev, tok_dev)))


def make_weights(patterns, order, frozen_query, low, query_up, kv):
    tok_dev, width = frozen_query.shape
    heads = width // HEAD_SIZE
    key_count = kv.shape[0]
    vmem = pl.BlockSpec(memory_space=pltpu.VMEM)
    return pl.pallas_call(
        functools.partial(weights_kernel, patterns),
        out_shape=(
            jax.ShapeDtypeStruct((heads * tok_dev, key_count), jnp.bfloat16),
            jax.ShapeDtypeStruct((heads, tok_dev), jnp.float32),
        ),
        in_specs=[pl.BlockSpec(memory_space=pltpu.SMEM)] + [vmem] * 4,
        out_specs=(vmem, vmem),
        scratch_shapes=[pltpu.VMEM((tok_dev, key_count), jnp.float32)],
        compiler_params=pltpu.CompilerParams(vmem_limit_bytes=VMEM_LIMIT),
        cost_estimate=pl.CostEstimate(
            flops=2 * tok_dev * width * key_count,
            bytes_accessed=2 * tok_dev * heads * key_count,
            transcendentals=heads * tok_dev * key_count,
        ),
    )(order, frozen_query, low, query_up, kv)


def values_kernel(
    patterns, weights_ref, top_ref, kv_ref, low_value_ref, value_up_ref, attended_ref, normalizer_ref, value_ref
):
    heads, tok_dev = top_ref.shape
    span = tok_dev // 2
    head_index = lax.axis_index("head")
    ctx, side = lax.axis_index("ctx"), head_index % 2
    group = head_index // (lax.axis_size("head") // KEY_VALUE_HEADS)
    value_up = value_up_ref[:, pl.ds(pl.multiple_of(group * HEAD_SIZE, HEAD_SIZE), HEAD_SIZE)]
    updates = [
        ADAPTER_SCALE
        * lax.dot_general(
            low_value_ref[n * ADAPTER_RANK : (n + 1) * ADAPTER_RANK, :],
            value_up,
            (((0,), (0,)), ((), ())),
            preferred_element_type=jnp.float32,
        )
        for n in range(len(patterns))
    ]
    for entry, (block, half, _) in enumerate(half_blocks(patterns, ctx, side)):
        here = slice(entry * span, (entry + 1) * span)
        update = jnp.where(half == 0, updates[block][:span], updates[block][span:])
        value_ref[here, :HEAD_SIZE] = (
            kv_ref[here, HEAD_SIZE:].astype(jnp.float32) + update
        ).astype(jnp.bfloat16)
    value_ref[:, HEAD_SIZE:] = jnp.ones((value_ref.shape[0], HEAD_SIZE), jnp.bfloat16)
    for head in range(heads):
        sums = jnp.dot(
            weights_ref[head * tok_dev : (head + 1) * tok_dev, :],
            value_ref[...],
            preferred_element_type=jnp.float32,
        )
        total = sums[:, HEAD_SIZE:]
        attended_ref[:, head * HEAD_SIZE : (head + 1) * HEAD_SIZE] = (
            sums[:, :HEAD_SIZE] / total
        ).astype(jnp.bfloat16)
        normalizer_ref[head : head + 1, :] = top_ref[head : head + 1, :] * math.log(2.0) + jnp.log(
            diagonal_row(total)
        )


def weigh_values(patterns, weights, top, kv, low_value, value_up):
    heads, tok_dev = top.shape
    key_count = kv.shape[0]
    width = heads * HEAD_SIZE
    vmem = pl.BlockSpec(memory_space=pltpu.VMEM)
    return pl.pallas_call(
        functools.partial(values_kernel, patterns),
        out_shape=(
            jax.ShapeDtypeStruct((tok_dev, width), jnp.bfloat16),
            jax.ShapeDtypeStruct((heads, tok_dev), jnp.float32),
        ),
        in_specs=[vmem] * 5,
        out_specs=(vmem, vmem),
        scratch_shapes=[pltpu.VMEM((key_count, 2 * HEAD_SIZE), jnp.bfloat16)],
        compiler_params=pltpu.CompilerParams(vmem_limit_bytes=VMEM_LIMIT),
        cost_estimate=pl.CostEstimate(
            flops=2 * tok_dev * width * key_count,
            bytes_accessed=2 * tok_dev * heads * key_count,
            transcendentals=0,
        ),
    )(weights, top, kv, low_value, value_up)


def attend_long(patterns, ctx, head, order, frozen_query, low, query_up, kv, low_value, value_up):
    tok_dev, width = frozen_query.shape
    span = tok_dev // 2
    heads = width // HEAD_SIZE
    blocks = len(patterns)
    side = head % 2
    group = head // (lax.axis_size("head") // KEY_VALUE_HEADS)
    value_up = lax.dynamic_slice_in_dim(value_up, group * HEAD_SIZE, HEAD_SIZE, 1)
    low = low.T
    low_value = low_value.reshape(blocks, ADAPTER_RANK, tok_dev).transpose(0, 2, 1)
    queries = (
        frozen_query.astype(jnp.float32)
        + ADAPTER_SCALE
        * jnp.dot(low[:, :ADAPTER_RANK], query_up, preferred_element_type=jnp.float32)
    ).astype(jnp.bfloat16)
    queries = queries.reshape(tok_dev, heads, HEAD_SIZE).transpose(1, 0, 2).reshape(-1, HEAD_SIZE)
    pattern = jnp.tile(jnp.array(patterns, jnp.int32), 2)
    parity = jnp.array([p.bit_count() for p in patterns] + [p.bit_count() + 1 for p in patterns])
    half = (side + parity.astype(jnp.int32)) % 2
    key_spans = order[2 * (ctx ^ pattern) + half]
    inner = jnp.arange(span, dtype=jnp.int32)
    key_pos = (key_spans[:, None] * span + inner).reshape(-1)
    query_spans = lax.dynamic_slice_in_dim(order, 2 * ctx, 2)
    query_pos = jnp.tile((query_spans[:, None] * span + inner).reshape(-1), heads)
    index = jnp.tile(jnp.arange(blocks, dtype=jnp.int32), 2)
    low_rows = low_value.reshape(2 * blocks, span, ADAPTER_RANK)[2 * index + half]
    values = (
        kv[:, HEAD_SIZE:].astype(jnp.float32)
        + ADAPTER_SCALE
        * jnp.dot(
            low_rows.reshape(-1, ADAPTER_RANK), value_up, preferred_element_type=jnp.float32
        )
    ).astype(jnp.bfloat16)
    chunk = math.gcd(kv.shape[0], 1024)

    def step(number, state):
        top, total, summed = state
        at = number * chunk
        keys = lax.dynamic_slice_in_dim(kv, at, chunk, 0)[:, :HEAD_SIZE]
        scores = lax.dot_general(
            queries, keys, (((1,), (1,)), ((), ())), preferred_element_type=jnp.float32
        ) * (1.0 / math.sqrt(HEAD_SIZE))
        visible = lax.dynamic_slice_in_dim(key_pos, at, chunk)[None, :] <= query_pos[:, None]
        new_top = jnp.maximum(top, jnp.max(jnp.where(visible, scores, MASKED), axis=1))
        scale = jnp.exp(top - new_top)
        weights = jnp.where(visible, jnp.exp(scores - new_top[:, None]), 0.0)
        summed = summed * scale[:, None] + jnp.dot(
            weights.astype(jnp.bfloat16),
            lax.dynamic_slice_in_dim(values, at, chunk, 0),
            preferred_element_type=jnp.float32,
        )
        return (new_top, total * scale + jnp.sum(weights, axis=1), summed)

    rows = heads * tok_dev
    top, total, summed = lax.fori_loop(
        0,
        kv.shape[0] // chunk,
        step,
        (
            jnp.full((rows,), MASKED, jnp.float32),
            jnp.zeros((rows,), jnp.float32),
            jnp.zeros((rows, HEAD_SIZE), jnp.float32),
        ),
    )
    attended = (summed / total[:, None]).astype(jnp.bfloat16)
    attended = attended.reshape(heads, tok_dev, HEAD_SIZE).transpose(1, 0, 2)
    return attended.reshape(tok_dev, width), (top + jnp.log(total)).reshape(heads, tok_dev)


def local(
    hidden,
    frozen_query_rows,
    frozen_key_rows,
    frozen_value_rows,
    adapter_down_factors,
    query_up_factor,
    value_up_factor,
    slot_span_order,
):
    ctx_count, head_count = lax.axis_size("ctx"), lax.axis_size("head")
    ctx, head = lax.axis_index("ctx"), lax.axis_index("head")
    bits = [ctx_count >> k for k in range(1, ctx_count.bit_length())]
    if len(bits) == 3:
        bits = [bits[0], bits[2], bits[1]]
    patterns = gather_patterns(bits)

    low, kv = prologue(hidden, adapter_down_factors.T, frozen_key_rows, frozen_value_rows)
    head_bit = 1
    while head_bit < head_count:
        other = exchange(low, 0, head_bit | 1)
        low = (low.astype(jnp.float32) + other.astype(jnp.float32)).astype(jnp.bfloat16)
        head_bit *= 2
    low_value = low[ADAPTER_RANK:]
    for bit in bits:
        low_value = jnp.concatenate([low_value, exchange(low_value, bit, 1)], axis=0)
        kv = jnp.concatenate([kv, exchange(kv, bit, 1)], axis=0)
    kv = jnp.concatenate([kv, exchange(kv, 0, 1)], axis=0)
    if kv.shape[0] > 1024:
        return attend_long(
            patterns, ctx, head, slot_span_order, frozen_query_rows, low, query_up_factor, kv, low_value, value_up_factor
        )
    weights, top = make_weights(
        patterns, slot_span_order, frozen_query_rows, low, query_up_factor, kv
    )
    return weigh_values(patterns, weights, top, kv, low_value, value_up_factor)


def solution(mesh):
    placed = (
        P("ctx", "head"),
        P("ctx", "head"),
        P("ctx", None),
        P("ctx", None),
        P("head", None),
        P(None, "head"),
        P(),
        P(),
    )
    return jax.shard_map(
        local,
        mesh=mesh,
        in_specs=placed,
        out_specs=(P("ctx", "head"), P("head", "ctx")),
        check_vma=False,
    )
```

```python
import functools
import math

import jax
import jax.numpy as jnp
from jax import lax
from jax.experimental import pallas as pl
from jax.experimental.pallas import tpu as pltpu
from jax.sharding import PartitionSpec as P

HEAD_SIZE = 128
KEY_VALUE_HEADS = 2
ADAPTER_RANK = 32
ADAPTER_SCALE = 0.5
MASKED = -1e30
AXES = ("ctx", "head")
SCORE_FACTOR = math.log2(math.e) / math.sqrt(HEAD_SIZE)
VMEM_LIMIT = 24 * 1024 * 1024


def exchange(value, ctx_bit, head_bits):
    ctx_count, head_count = lax.axis_size("ctx"), lax.axis_size("head")
    pairs = [
        (i * head_count + h, (i ^ ctx_bit) * head_count + (h ^ head_bits))
        for i in range(ctx_count)
        for h in range(head_count)
    ]
    return lax.ppermute(value, AXES, pairs)


def gather_patterns(bits):
    patterns = [0]
    for bit in bits:
        patterns += [p ^ bit for p in patterns]
    return patterns


def half_blocks(patterns, ctx, side):
    blocks = len(patterns)
    found = []
    for entry in range(2 * blocks):
        pattern = patterns[entry % blocks]
        half = (side + pattern.bit_count() + entry // blocks) % 2
        found.append((entry % blocks, half, 2 * (ctx ^ pattern) + half))
    return found


def prologue_kernel(
    patterns,
    hidden_hbm,
    down_hbm,
    key_hbm,
    value_hbm,
    order_hbm,
    frozen_query_hbm,
    query_up_hbm,
    value_up_hbm,
    low_ref,
    kv_ref,
    bias_ref,
    frozen_query_ref,
    query_up_ref,
    value_up_ref,
    hidden_ref,
    down_ref,
    order_ref,
    sems,
    other_sems,
):
    ctx, head = lax.axis_index("ctx"), lax.axis_index("head")
    side = head % 2
    group = head // (lax.axis_size("head") // KEY_VALUE_HEADS)
    tok_dev = hidden_hbm.shape[0]
    span = tok_dev // 2
    rows = pl.ds(pl.multiple_of(side * span, span), span)
    columns = pl.ds(pl.multiple_of(group * HEAD_SIZE, HEAD_SIZE), HEAD_SIZE)
    chunks = sems.shape[0]
    depth = down_hbm.shape[1] // chunks
    copies = []
    for chunk in range(chunks):
        part = pl.ds(chunk * depth, depth)
        pair = (
            pltpu.make_async_copy(hidden_hbm.at[:, part], hidden_ref.at[:, part], sems.at[chunk, 0]),
            pltpu.make_async_copy(down_hbm.at[:, part], down_ref.at[:, part], sems.at[chunk, 1]),
        )
        for copy in pair:
            copy.start()
        copies.append(pair)
    others = [
        pltpu.make_async_copy(*refs, other_sems.at[n])
        for n, refs in enumerate(
            (
                (order_hbm, order_ref),
                (key_hbm.at[rows, columns], kv_ref.at[:, pl.ds(0, HEAD_SIZE)]),
                (value_hbm.at[rows, columns], kv_ref.at[:, pl.ds(HEAD_SIZE, HEAD_SIZE)]),
                (frozen_query_hbm, frozen_query_ref),
                (query_up_hbm, query_up_ref),
                (value_up_hbm.at[:, columns], value_up_ref),
            )
        )
    ]
    for copy in others:
        copy.start()
    others[0].wait()
    row = lax.broadcasted_iota(jnp.int32, (tok_dev, tok_dev), 0)
    lane = lax.broadcasted_iota(jnp.int32, (tok_dev, tok_dev), 1)
    first_row, first_lane = row < span, lane < span
    inner = row % span - lane % span
    query_spans = jnp.where(first_row, order_ref[2 * ctx], order_ref[2 * ctx + 1])
    entries = half_blocks(patterns, ctx, side)
    for tile in range(len(patterns)):
        first, second = order_ref[entries[2 * tile][2]], order_ref[entries[2 * tile + 1][2]]
        ahead = jnp.where(first_lane, first, second) - query_spans
        bias_ref[:, tile * tok_dev : (tile + 1) * tok_dev] = jnp.where(
            ahead * span <= inner, 0.0, MASKED
        )
    total = jnp.zeros(low_ref.shape, jnp.float32)
    for chunk in range(chunks):
        for copy in copies[chunk]:
            copy.wait()
        part = slice(chunk * depth, (chunk + 1) * depth)
        total += lax.dot_general(
            down_ref[:, part],
            hidden_ref[:, part],
            (((1,), (1,)), ((), ())),
            preferred_element_type=jnp.float32,
        )
    low_ref[...] = total.astype(jnp.bfloat16)
    for copy in others[1:]:
        copy.wait()


def prologue(patterns, hidden, down, keys, values, order, frozen_query, query_up, value_up):
    tok_dev, depth = hidden.shape
    rank = down.shape[0]
    chunks = 4
    hbm = pl.BlockSpec(memory_space=pltpu.HBM)
    vmem = pl.BlockSpec(memory_space=pltpu.VMEM)
    operands = (hidden, down, keys, values, order, frozen_query, query_up, value_up)
    return pl.pallas_call(
        functools.partial(prologue_kernel, patterns),
        out_shape=(
            jax.ShapeDtypeStruct((rank, tok_dev), jnp.bfloat16),
            jax.ShapeDtypeStruct((tok_dev // 2, 2 * HEAD_SIZE), jnp.bfloat16),
            jax.ShapeDtypeStruct((tok_dev, tok_dev * len(patterns)), jnp.float32),
            jax.ShapeDtypeStruct(frozen_query.shape, jnp.bfloat16),
            jax.ShapeDtypeStruct(query_up.shape, jnp.bfloat16),
            jax.ShapeDtypeStruct((value_up.shape[0], HEAD_SIZE), jnp.bfloat16),
        ),
        in_specs=[hbm] * len(operands),
        out_specs=(vmem,) * 6,
        scratch_shapes=[
            pltpu.VMEM(hidden.shape, jnp.bfloat16),
            pltpu.VMEM(down.shape, jnp.bfloat16),
            pltpu.SMEM(order.shape, jnp.int32),
            pltpu.SemaphoreType.DMA((chunks, 2)),
            pltpu.SemaphoreType.DMA((6,)),
        ],
        compiler_params=pltpu.CompilerParams(vmem_limit_bytes=VMEM_LIMIT),
        cost_estimate=pl.CostEstimate(
            flops=2 * tok_dev * depth * rank, bytes_accessed=tok_dev * depth * 4, transcendentals=0
        ),
    )(*(pltpu.with_memory_space_constraint(x, pltpu.HBM) for x in operands))


def queries_kernel(frozen_query_ref, low_ref, query_up_ref, queries_ref):
    queries_ref[...] = (
        frozen_query_ref[...].astype(jnp.float32)
        + ADAPTER_SCALE
        * lax.dot_general(
            low_ref[:ADAPTER_RANK, :],
            query_up_ref[...],
            (((0,), (0,)), ((), ())),
            preferred_element_type=jnp.float32,
        )
    ).astype(jnp.bfloat16)


def adapt_queries(frozen_query, low, query_up):
    tok_dev, width = frozen_query.shape
    vmem = pl.BlockSpec(memory_space=pltpu.VMEM)
    return pl.pallas_call(
        queries_kernel,
        out_shape=jax.ShapeDtypeStruct((tok_dev, width), jnp.bfloat16),
        in_specs=[vmem] * 3,
        out_specs=vmem,
        compiler_params=pltpu.CompilerParams(vmem_limit_bytes=VMEM_LIMIT),
        cost_estimate=pl.CostEstimate(
            flops=2 * tok_dev * width * ADAPTER_RANK,
            bytes_accessed=4 * tok_dev * width,
            transcendentals=0,
        ),
    )(frozen_query, low, query_up)


def weights_kernel(queries_ref, bias_ref, kv_ref, other_kv_ref, weights_ref, top_ref):
    tok_dev, width = queries_ref.shape
    half = kv_ref.shape[0]
    for head in range(width // HEAD_SIZE):
        columns = slice(head * HEAD_SIZE, (head + 1) * HEAD_SIZE)
        rows = slice(head * tok_dev, (head + 1) * tok_dev)
        scores = [
            lax.dot_general(
                queries_ref[:, columns],
                ref[:, :HEAD_SIZE],
                (((1,), (1,)), ((), ())),
                preferred_element_type=jnp.float32,
            )
            * SCORE_FACTOR
            + bias_ref[:, n * half : (n + 1) * half]
            for n, ref in enumerate((kv_ref, other_kv_ref))
        ]
        top = jnp.maximum(
            jnp.max(scores[0], axis=1, keepdims=True), jnp.max(scores[1], axis=1, keepdims=True)
        )
        for n in range(2):
            weights_ref[rows, n * half : (n + 1) * half] = jnp.exp2(scores[n] - top).astype(
                jnp.bfloat16
            )
        top_ref[:, columns] = jnp.broadcast_to(top, (tok_dev, HEAD_SIZE))


def make_weights(queries, bias, kv, other_kv):
    tok_dev, width = queries.shape
    heads = width // HEAD_SIZE
    key_count = 2 * kv.shape[0]
    vmem = pl.BlockSpec(memory_space=pltpu.VMEM)
    return pl.pallas_call(
        weights_kernel,
        out_shape=(
            jax.ShapeDtypeStruct((heads * tok_dev, key_count), jnp.bfloat16),
            jax.ShapeDtypeStruct((tok_dev, width), jnp.float32),
        ),
        in_specs=[vmem] * 4,
        out_specs=(vmem, vmem),
        compiler_params=pltpu.CompilerParams(vmem_limit_bytes=VMEM_LIMIT),
        cost_estimate=pl.CostEstimate(
            flops=2 * tok_dev * width * key_count,
            bytes_accessed=2 * tok_dev * heads * key_count,
            transcendentals=heads * tok_dev * key_count,
        ),
    )(queries, bias, kv, other_kv)


def values_kernel(
    patterns,
    weights_ref,
    top_ref,
    kv_ref,
    other_kv_ref,
    low_value_ref,
    value_up_ref,
    attended_ref,
    normalizer_ref,
    value_ref,
):
    tok_dev, width = top_ref.shape
    span = tok_dev // 2
    blocks = len(patterns)
    half_count = blocks * span
    heads = width // HEAD_SIZE
    ctx, side = lax.axis_index("ctx"), lax.axis_index("head") % 2
    entries = half_blocks(patterns, ctx, side)
    value_ref[:, HEAD_SIZE:] = jnp.ones((2 * half_count, HEAD_SIZE), jnp.bfloat16)
    for block in range(blocks):
        update = ADAPTER_SCALE * lax.dot_general(
            low_value_ref[block * ADAPTER_RANK : (block + 1) * ADAPTER_RANK, :],
            value_up_ref[...],
            (((0,), (0,)), ((), ())),
            preferred_element_type=jnp.float32,
        )
        low_half = entries[block][1] == 0
        parts = (
            jnp.where(low_half, update[:span], update[span:]),
            jnp.where(low_half, update[span:], update[:span]),
        )
        here = slice(block * span, (block + 1) * span)
        for n, ref in enumerate((kv_ref, other_kv_ref)):
            value_ref[n * half_count + block * span : n * half_count + (block + 1) * span, :HEAD_SIZE] = (
                ref[here, HEAD_SIZE:].astype(jnp.float32) + parts[n]
            ).astype(jnp.bfloat16)
    row = lax.broadcasted_iota(jnp.int32, (tok_dev, tok_dev), 0)
    lane = lax.broadcasted_iota(jnp.int32, (tok_dev, tok_dev), 1)
    for head in range(heads):
        columns = slice(head * HEAD_SIZE, (head + 1) * HEAD_SIZE)
        sums = jnp.dot(
            weights_ref[head * tok_dev : (head + 1) * tok_dev, :],
            value_ref[...],
            preferred_element_type=jnp.float32,
        )
        total = sums[:, HEAD_SIZE:]
        attended_ref[:, columns] = (sums[:, :HEAD_SIZE] / total).astype(jnp.bfloat16)
        normalizer_ref[head : head + 1, :] = jnp.sum(
            jnp.where(row == lane, top_ref[:, columns] * math.log(2.0) + jnp.log(total), 0.0),
            axis=0,
            keepdims=True,
        )


def weigh_values(patterns, weights, top, kv, other_kv, low_value, value_up):
    tok_dev, width = top.shape
    heads = width // HEAD_SIZE
    key_count = 2 * kv.shape[0]
    vmem = pl.BlockSpec(memory_space=pltpu.VMEM)
    return pl.pallas_call(
        functools.partial(values_kernel, patterns),
        out_shape=(
            jax.ShapeDtypeStruct((tok_dev, width), jnp.bfloat16),
            jax.ShapeDtypeStruct((heads, tok_dev), jnp.float32),
        ),
        in_specs=[vmem] * 6,
        out_specs=(vmem, vmem),
        scratch_shapes=[
            pltpu.VMEM((key_count, 2 * HEAD_SIZE), jnp.bfloat16),
        ],
        compiler_params=pltpu.CompilerParams(vmem_limit_bytes=VMEM_LIMIT),
        cost_estimate=pl.CostEstimate(
            flops=4 * tok_dev * width * key_count,
            bytes_accessed=4 * tok_dev * heads * key_count,
            transcendentals=0,
        ),
    )(weights, top, kv, other_kv, low_value, value_up)


def attend_long(patterns, ctx, head, order, frozen_query, low, query_up, kv, low_value, value_up):
    tok_dev, width = frozen_query.shape
    span = tok_dev // 2
    heads = width // HEAD_SIZE
    blocks = len(patterns)
    side = head % 2
    group = head // (lax.axis_size("head") // KEY_VALUE_HEADS)
    value_up = lax.dynamic_slice_in_dim(value_up, group * HEAD_SIZE, HEAD_SIZE, 1)
    low = low.T
    low_value = low_value.reshape(blocks, ADAPTER_RANK, tok_dev).transpose(0, 2, 1)
    queries = (
        frozen_query.astype(jnp.float32)
        + ADAPTER_SCALE
        * jnp.dot(low[:, :ADAPTER_RANK], query_up, preferred_element_type=jnp.float32)
    ).astype(jnp.bfloat16)
    queries = queries.reshape(tok_dev, heads, HEAD_SIZE).transpose(1, 0, 2).reshape(-1, HEAD_SIZE)
    pattern = jnp.tile(jnp.array(patterns, jnp.int32), 2)
    parity = jnp.array([p.bit_count() for p in patterns] + [p.bit_count() + 1 for p in patterns])
    half = (side + parity.astype(jnp.int32)) % 2
    key_spans = order[2 * (ctx ^ pattern) + half]
    inner = jnp.arange(span, dtype=jnp.int32)
    key_pos = (key_spans[:, None] * span + inner).reshape(-1)
    query_spans = lax.dynamic_slice_in_dim(order, 2 * ctx, 2)
    query_pos = jnp.tile((query_spans[:, None] * span + inner).reshape(-1), heads)
    index = jnp.tile(jnp.arange(blocks, dtype=jnp.int32), 2)
    low_rows = low_value.reshape(2 * blocks, span, ADAPTER_RANK)[2 * index + half]
    values = (
        kv[:, HEAD_SIZE:].astype(jnp.float32)
        + ADAPTER_SCALE
        * jnp.dot(
            low_rows.reshape(-1, ADAPTER_RANK), value_up, preferred_element_type=jnp.float32
        )
    ).astype(jnp.bfloat16)
    chunk = math.gcd(kv.shape[0], 1024)

    def step(number, state):
        top, total, summed = state
        at = number * chunk
        keys = lax.dynamic_slice_in_dim(kv, at, chunk, 0)[:, :HEAD_SIZE]
        scores = lax.dot_general(
            queries, keys, (((1,), (1,)), ((), ())), preferred_element_type=jnp.float32
        ) * (1.0 / math.sqrt(HEAD_SIZE))
        visible = lax.dynamic_slice_in_dim(key_pos, at, chunk)[None, :] <= query_pos[:, None]
        new_top = jnp.maximum(top, jnp.max(jnp.where(visible, scores, MASKED), axis=1))
        scale = jnp.exp(top - new_top)
        weights = jnp.where(visible, jnp.exp(scores - new_top[:, None]), 0.0)
        summed = summed * scale[:, None] + jnp.dot(
            weights.astype(jnp.bfloat16),
            lax.dynamic_slice_in_dim(values, at, chunk, 0),
            preferred_element_type=jnp.float32,
        )
        return (new_top, total * scale + jnp.sum(weights, axis=1), summed)

    rows = heads * tok_dev
    top, total, summed = lax.fori_loop(
        0,
        kv.shape[0] // chunk,
        step,
        (
            jnp.full((rows,), MASKED, jnp.float32),
            jnp.zeros((rows,), jnp.float32),
            jnp.zeros((rows, HEAD_SIZE), jnp.float32),
        ),
    )
    attended = (summed / total[:, None]).astype(jnp.bfloat16)
    attended = attended.reshape(heads, tok_dev, HEAD_SIZE).transpose(1, 0, 2)
    return attended.reshape(tok_dev, width), (top + jnp.log(total)).reshape(heads, tok_dev)


def local(
    hidden,
    frozen_query_rows,
    frozen_key_rows,
    frozen_value_rows,
    adapter_down_factors,
    query_up_factor,
    value_up_factor,
    slot_span_order,
):
    ctx_count, head_count = lax.axis_size("ctx"), lax.axis_size("head")
    ctx, head = lax.axis_index("ctx"), lax.axis_index("head")
    bits = [ctx_count >> k for k in range(1, ctx_count.bit_length())]
    if len(bits) == 3:
        bits = [bits[0], bits[2], bits[1]]
    patterns = gather_patterns(bits)

    low, kv, bias, frozen_query, query_up, value_up = prologue(
        patterns,
        hidden,
        adapter_down_factors.T,
        frozen_key_rows,
        frozen_value_rows,
        slot_span_order,
        frozen_query_rows,
        query_up_factor,
        value_up_factor,
    )
    head_bit = 1
    while head_bit < head_count:
        other = exchange(low, 0, head_bit | 1)
        low = (low.astype(jnp.float32) + other.astype(jnp.float32)).astype(jnp.bfloat16)
        head_bit *= 2
    low_value = low[ADAPTER_RANK:]
    short = hidden.shape[0] * ctx_count <= 1024
    if short:
        queries = adapt_queries(frozen_query, low, query_up)
    for bit in bits:
        if short and bit == bits[-1]:
            kv, _ = lax.optimization_barrier((kv, queries))
        low_value = jnp.concatenate([low_value, exchange(low_value, bit, 1)], axis=0)
        kv = jnp.concatenate([kv, exchange(kv, bit, 1)], axis=0)
    other_kv = exchange(kv, 0, 1)
    if not short:
        return attend_long(
            patterns,
            ctx,
            head,
            slot_span_order,
            frozen_query_rows,
            low,
            query_up_factor,
            jnp.concatenate([kv, other_kv], axis=0),
            low_value,
            value_up_factor,
        )
    weights, top = make_weights(queries, bias, kv, other_kv)
    return weigh_values(patterns, weights, top, kv, other_kv, low_value, value_up)


def solution(mesh):
    placed = (
        P("ctx", "head"),
        P("ctx", "head"),
        P("ctx", None),
        P("ctx", None),
        P("head", None),
        P(None, "head"),
        P(),
        P(),
    )
    return jax.shard_map(
        local,
        mesh=mesh,
        in_specs=placed,
        out_specs=(P("ctx", "head"), P("head", "ctx")),
        check_vma=False,
    )
```

```python
import functools
import math

import jax
import jax.numpy as jnp
from jax import lax
from jax.experimental import pallas as pl
from jax.experimental.pallas import tpu as pltpu
from jax.sharding import PartitionSpec as P

HEAD_SIZE = 128
KEY_VALUE_HEADS = 2
ADAPTER_RANK = 32
ADAPTER_SCALE = 0.5
MASKED = -1e30
AXES = ("ctx", "head")
SCORE_FACTOR = math.log2(math.e) / math.sqrt(HEAD_SIZE)
VMEM_LIMIT = 24 * 1024 * 1024


def exchange(value, ctx_bit, head_bits):
    ctx_count, head_count = lax.axis_size("ctx"), lax.axis_size("head")
    pairs = [
        (i * head_count + h, (i ^ ctx_bit) * head_count + (h ^ head_bits))
        for i in range(ctx_count)
        for h in range(head_count)
    ]
    return lax.ppermute(value, AXES, pairs)


def gather_patterns(bits):
    patterns = [0]
    for bit in bits:
        patterns += [p ^ bit for p in patterns]
    return patterns


def half_blocks(patterns, ctx):
    blocks = len(patterns)
    found = []
    for entry in range(2 * blocks):
        pattern = patterns[entry % blocks]
        half = (pattern.bit_count() + entry // blocks) % 2
        found.append((entry % blocks, half, 2 * (ctx ^ pattern) + half))
    return found


def prologue_kernel(
    patterns,
    hidden_hbm,
    down_hbm,
    key_hbm,
    value_hbm,
    order_hbm,
    frozen_query_hbm,
    query_up_hbm,
    value_up_hbm,
    low_ref,
    kv_ref,
    bias_ref,
    frozen_query_ref,
    query_up_ref,
    value_up_ref,
    hidden_ref,
    down_ref,
    order_ref,
    sems,
    other_sems,
):
    ctx, head = lax.axis_index("ctx"), lax.axis_index("head")
    side = head % 2
    group = head // (lax.axis_size("head") // KEY_VALUE_HEADS)
    tok_dev = hidden_hbm.shape[0]
    span = tok_dev // 2
    rows = pl.ds(pl.multiple_of(side * span, span), span)
    columns = pl.ds(pl.multiple_of(group * HEAD_SIZE, HEAD_SIZE), HEAD_SIZE)
    chunks = sems.shape[0]
    depth = down_hbm.shape[1] // chunks
    copies = []
    for chunk in range(chunks):
        part = pl.ds(chunk * depth, depth)
        pair = (
            pltpu.make_async_copy(hidden_hbm.at[:, part], hidden_ref.at[:, part], sems.at[chunk, 0]),
            pltpu.make_async_copy(down_hbm.at[:, part], down_ref.at[:, part], sems.at[chunk, 1]),
        )
        for copy in pair:
            copy.start()
        copies.append(pair)
    others = [
        pltpu.make_async_copy(*refs, other_sems.at[n])
        for n, refs in enumerate(
            (
                (order_hbm, order_ref),
                (key_hbm.at[rows, columns], kv_ref.at[:, pl.ds(0, HEAD_SIZE)]),
                (value_hbm.at[rows, columns], kv_ref.at[:, pl.ds(HEAD_SIZE, HEAD_SIZE)]),
                (frozen_query_hbm, frozen_query_ref),
                (query_up_hbm, query_up_ref),
                (value_up_hbm.at[:, columns], value_up_ref),
            )
        )
    ]
    for copy in others:
        copy.start()
    others[0].wait()
    row = lax.broadcasted_iota(jnp.int32, (tok_dev, tok_dev), 0)
    lane = lax.broadcasted_iota(jnp.int32, (tok_dev, tok_dev), 1)
    first_row, first_lane = row < span, lane < span
    inner = row % span - lane % span
    query_spans = jnp.where(first_row, order_ref[2 * ctx], order_ref[2 * ctx + 1])
    entries = half_blocks(patterns, ctx)
    for tile in range(len(patterns)):
        first, second = order_ref[entries[2 * tile][2]], order_ref[entries[2 * tile + 1][2]]
        ahead = jnp.where(first_lane, first, second) - query_spans
        bias_ref[:, tile * tok_dev : (tile + 1) * tok_dev] = jnp.where(
            ahead * span <= inner, 0.0, MASKED
        )
    total = jnp.zeros(low_ref.shape, jnp.float32)
    for chunk in range(chunks):
        for copy in copies[chunk]:
            copy.wait()
        part = slice(chunk * depth, (chunk + 1) * depth)
        total += lax.dot_general(
            down_ref[:, part],
            hidden_ref[:, part],
            (((1,), (1,)), ((), ())),
            preferred_element_type=jnp.float32,
        )
    low_ref[...] = total.astype(jnp.bfloat16)
    for copy in others[1:]:
        copy.wait()


def prologue(patterns, hidden, down, keys, values, order, frozen_query, query_up, value_up):
    tok_dev, depth = hidden.shape
    rank = down.shape[0]
    chunks = 4
    hbm = pl.BlockSpec(memory_space=pltpu.HBM)
    vmem = pl.BlockSpec(memory_space=pltpu.VMEM)
    operands = (hidden, down, keys, values, order, frozen_query, query_up, value_up)
    return pl.pallas_call(
        functools.partial(prologue_kernel, patterns),
        out_shape=(
            jax.ShapeDtypeStruct((rank, tok_dev), jnp.bfloat16),
            jax.ShapeDtypeStruct((tok_dev // 2, 2 * HEAD_SIZE), jnp.bfloat16),
            jax.ShapeDtypeStruct((tok_dev, tok_dev * len(patterns)), jnp.float32),
            jax.ShapeDtypeStruct(frozen_query.shape, jnp.bfloat16),
            jax.ShapeDtypeStruct(query_up.shape, jnp.bfloat16),
            jax.ShapeDtypeStruct((value_up.shape[0], HEAD_SIZE), jnp.bfloat16),
        ),
        in_specs=[hbm] * len(operands),
        out_specs=(vmem,) * 6,
        scratch_shapes=[
            pltpu.VMEM(hidden.shape, jnp.bfloat16),
            pltpu.VMEM(down.shape, jnp.bfloat16),
            pltpu.SMEM(order.shape, jnp.int32),
            pltpu.SemaphoreType.DMA((chunks, 2)),
            pltpu.SemaphoreType.DMA((6,)),
        ],
        compiler_params=pltpu.CompilerParams(vmem_limit_bytes=VMEM_LIMIT),
        cost_estimate=pl.CostEstimate(
            flops=2 * tok_dev * depth * rank, bytes_accessed=tok_dev * depth * 4, transcendentals=0
        ),
    )(*(pltpu.with_memory_space_constraint(x, pltpu.HBM) for x in operands))


def queries_kernel(frozen_query_ref, low_ref, query_up_ref, queries_ref):
    queries_ref[...] = (
        frozen_query_ref[...].astype(jnp.float32)
        + ADAPTER_SCALE
        * lax.dot_general(
            low_ref[:ADAPTER_RANK, :],
            query_up_ref[...],
            (((0,), (0,)), ((), ())),
            preferred_element_type=jnp.float32,
        )
    ).astype(jnp.bfloat16)


def adapt_queries(frozen_query, low, query_up):
    tok_dev, width = frozen_query.shape
    vmem = pl.BlockSpec(memory_space=pltpu.VMEM)
    return pl.pallas_call(
        queries_kernel,
        out_shape=jax.ShapeDtypeStruct((tok_dev, width), jnp.bfloat16),
        in_specs=[vmem] * 3,
        out_specs=vmem,
        compiler_params=pltpu.CompilerParams(vmem_limit_bytes=VMEM_LIMIT),
        cost_estimate=pl.CostEstimate(
            flops=2 * tok_dev * width * ADAPTER_RANK,
            bytes_accessed=4 * tok_dev * width,
            transcendentals=0,
        ),
    )(frozen_query, low, query_up)


def weights_kernel(queries_ref, bias_ref, kv_ref, weights_ref, top_ref):
    tok_dev, width = queries_ref.shape
    for head in range(width // HEAD_SIZE):
        columns = slice(head * HEAD_SIZE, (head + 1) * HEAD_SIZE)
        scores = (
            lax.dot_general(
                queries_ref[:, columns],
                kv_ref[:, :HEAD_SIZE],
                (((1,), (1,)), ((), ())),
                preferred_element_type=jnp.float32,
            )
            * SCORE_FACTOR
            + bias_ref[...]
        )
        top = jnp.max(scores, axis=1, keepdims=True)
        weights_ref[head * tok_dev : (head + 1) * tok_dev, :] = jnp.exp2(scores - top).astype(
            jnp.bfloat16
        )
        top_ref[:, columns] = jnp.broadcast_to(top, (tok_dev, HEAD_SIZE))


def make_weights(queries, bias, kv):
    tok_dev, width = queries.shape
    heads = width // HEAD_SIZE
    key_count = kv.shape[0]
    vmem = pl.BlockSpec(memory_space=pltpu.VMEM)
    return pl.pallas_call(
        weights_kernel,
        out_shape=(
            jax.ShapeDtypeStruct((heads * tok_dev, key_count), jnp.bfloat16),
            jax.ShapeDtypeStruct((tok_dev, width), jnp.float32),
        ),
        in_specs=[vmem] * 3,
        out_specs=(vmem, vmem),
        compiler_params=pltpu.CompilerParams(vmem_limit_bytes=VMEM_LIMIT),
        cost_estimate=pl.CostEstimate(
            flops=2 * tok_dev * width * key_count,
            bytes_accessed=2 * tok_dev * heads * key_count,
            transcendentals=heads * tok_dev * key_count,
        ),
    )(queries, bias, kv)


def values_kernel(
    patterns,
    weights_ref,
    top_ref,
    kv_ref,
    low_value_ref,
    value_up_ref,
    attended_ref,
    normalizer_ref,
    value_ref,
):
    tok_dev, width = top_ref.shape
    span = tok_dev // 2
    heads = width // HEAD_SIZE
    value_ref[:, HEAD_SIZE:] = jnp.ones((value_ref.shape[0], HEAD_SIZE), jnp.bfloat16)
    updates = [
        ADAPTER_SCALE
        * lax.dot_general(
            low_value_ref[block * ADAPTER_RANK : (block + 1) * ADAPTER_RANK, :],
            value_up_ref[...],
            (((0,), (0,)), ((), ())),
            preferred_element_type=jnp.float32,
        )
        for block in range(len(patterns))
    ]
    for entry, (block, half, _) in enumerate(half_blocks(patterns, 0)):
        here = slice(entry * span, (entry + 1) * span)
        value_ref[here, :HEAD_SIZE] = (
            kv_ref[here, HEAD_SIZE:].astype(jnp.float32)
            + updates[block][half * span : (half + 1) * span]
        ).astype(jnp.bfloat16)
    row = lax.broadcasted_iota(jnp.int32, (tok_dev, tok_dev), 0)
    lane = lax.broadcasted_iota(jnp.int32, (tok_dev, tok_dev), 1)
    for head in range(heads):
        columns = slice(head * HEAD_SIZE, (head + 1) * HEAD_SIZE)
        sums = jnp.dot(
            weights_ref[head * tok_dev : (head + 1) * tok_dev, :],
            value_ref[...],
            preferred_element_type=jnp.float32,
        )
        total = sums[:, HEAD_SIZE:]
        attended_ref[:, columns] = (sums[:, :HEAD_SIZE] / total).astype(jnp.bfloat16)
        normalizer_ref[head : head + 1, :] = jnp.sum(
            jnp.where(row == lane, top_ref[:, columns] * math.log(2.0) + jnp.log(total), 0.0),
            axis=0,
            keepdims=True,
        )


def weigh_values(patterns, weights, top, kv, low_value, value_up):
    tok_dev, width = top.shape
    heads = width // HEAD_SIZE
    key_count = kv.shape[0]
    vmem = pl.BlockSpec(memory_space=pltpu.VMEM)
    return pl.pallas_call(
        functools.partial(values_kernel, patterns),
        out_shape=(
            jax.ShapeDtypeStruct((tok_dev, width), jnp.bfloat16),
            jax.ShapeDtypeStruct((heads, tok_dev), jnp.float32),
        ),
        in_specs=[vmem] * 5,
        out_specs=(vmem, vmem),
        scratch_shapes=[
            pltpu.VMEM((key_count, 2 * HEAD_SIZE), jnp.bfloat16),
        ],
        compiler_params=pltpu.CompilerParams(vmem_limit_bytes=VMEM_LIMIT),
        cost_estimate=pl.CostEstimate(
            flops=4 * tok_dev * width * key_count,
            bytes_accessed=4 * tok_dev * heads * key_count,
            transcendentals=0,
        ),
    )(weights, top, kv, low_value, value_up)


def attend_long(patterns, ctx, head, order, frozen_query, low, query_up, kv, low_value, value_up):
    tok_dev, width = frozen_query.shape
    span = tok_dev // 2
    heads = width // HEAD_SIZE
    blocks = len(patterns)
    group = head // (lax.axis_size("head") // KEY_VALUE_HEADS)
    value_up = lax.dynamic_slice_in_dim(value_up, group * HEAD_SIZE, HEAD_SIZE, 1)
    low = low.T
    low_value = low_value.reshape(blocks, ADAPTER_RANK, tok_dev).transpose(0, 2, 1)
    queries = (
        frozen_query.astype(jnp.float32)
        + ADAPTER_SCALE
        * jnp.dot(low[:, :ADAPTER_RANK], query_up, preferred_element_type=jnp.float32)
    ).astype(jnp.bfloat16)
    queries = queries.reshape(tok_dev, heads, HEAD_SIZE).transpose(1, 0, 2).reshape(-1, HEAD_SIZE)
    entries = half_blocks(patterns, 0)
    pattern = jnp.array([slot // 2 for _, _, slot in entries], jnp.int32)
    index = jnp.array([block for block, _, _ in entries], jnp.int32)
    half = jnp.array([half for _, half, _ in entries], jnp.int32)
    key_spans = order[2 * (ctx ^ pattern) + half]
    inner = jnp.arange(span, dtype=jnp.int32)
    key_pos = (key_spans[:, None] * span + inner).reshape(-1)
    query_spans = lax.dynamic_slice_in_dim(order, 2 * ctx, 2)
    query_pos = jnp.tile((query_spans[:, None] * span + inner).reshape(-1), heads)
    low_rows = low_value.reshape(2 * blocks, span, ADAPTER_RANK)[2 * index + half]
    values = (
        kv[:, HEAD_SIZE:].astype(jnp.float32)
        + ADAPTER_SCALE
        * jnp.dot(
            low_rows.reshape(-1, ADAPTER_RANK), value_up, preferred_element_type=jnp.float32
        )
    ).astype(jnp.bfloat16)
    chunk = math.gcd(kv.shape[0], 1024)

    def step(number, state):
        top, total, summed = state
        at = number * chunk
        keys = lax.dynamic_slice_in_dim(kv, at, chunk, 0)[:, :HEAD_SIZE]
        scores = lax.dot_general(
            queries, keys, (((1,), (1,)), ((), ())), preferred_element_type=jnp.float32
        ) * (1.0 / math.sqrt(HEAD_SIZE))
        visible = lax.dynamic_slice_in_dim(key_pos, at, chunk)[None, :] <= query_pos[:, None]
        new_top = jnp.maximum(top, jnp.max(jnp.where(visible, scores, MASKED), axis=1))
        scale = jnp.exp(top - new_top)
        weights = jnp.where(visible, jnp.exp(scores - new_top[:, None]), 0.0)
        summed = summed * scale[:, None] + jnp.dot(
            weights.astype(jnp.bfloat16),
            lax.dynamic_slice_in_dim(values, at, chunk, 0),
            preferred_element_type=jnp.float32,
        )
        return (new_top, total * scale + jnp.sum(weights, axis=1), summed)

    rows = heads * tok_dev
    top, total, summed = lax.fori_loop(
        0,
        kv.shape[0] // chunk,
        step,
        (
            jnp.full((rows,), MASKED, jnp.float32),
            jnp.zeros((rows,), jnp.float32),
            jnp.zeros((rows, HEAD_SIZE), jnp.float32),
        ),
    )
    attended = (summed / total[:, None]).astype(jnp.bfloat16)
    attended = attended.reshape(heads, tok_dev, HEAD_SIZE).transpose(1, 0, 2)
    return attended.reshape(tok_dev, width), (top + jnp.log(total)).reshape(heads, tok_dev)


def local(
    hidden,
    frozen_query_rows,
    frozen_key_rows,
    frozen_value_rows,
    adapter_down_factors,
    query_up_factor,
    value_up_factor,
    slot_span_order,
):
    ctx_count, head_count = lax.axis_size("ctx"), lax.axis_size("head")
    ctx, head = lax.axis_index("ctx"), lax.axis_index("head")
    bits = [ctx_count >> k for k in range(1, ctx_count.bit_length())]
    if len(bits) == 3:
        bits = [bits[0], bits[2], bits[1]]
    patterns = gather_patterns(bits)

    low, kv, bias, frozen_query, query_up, value_up = prologue(
        patterns,
        hidden,
        adapter_down_factors.T,
        frozen_key_rows,
        frozen_value_rows,
        slot_span_order,
        frozen_query_rows,
        query_up_factor,
        value_up_factor,
    )
    head_bit = 1
    while head_bit < head_count:
        other = exchange(low, 0, head_bit | 1)
        low = (low.astype(jnp.float32) + other.astype(jnp.float32)).astype(jnp.bfloat16)
        head_bit *= 2
    low_value = low[ADAPTER_RANK:]
    short = hidden.shape[0] * ctx_count <= 1024
    if short:
        queries = adapt_queries(frozen_query, low, query_up)
    for bit in bits:
        if short and bit == bits[-1]:
            kv, _ = lax.optimization_barrier((kv, queries))
        last_low = exchange(low_value, bit, 1)
        if not short or bit != bits[-1]:
            low_value = jnp.concatenate([low_value, last_low], axis=0)
        kv = jnp.concatenate([kv, exchange(kv, bit, 1)], axis=0)
    pairs = [[h, h + 1] for h in range(0, head_count, 2)]
    kv = lax.all_gather(kv, "head", axis=0, tiled=True, axis_index_groups=pairs)
    if not short:
        return attend_long(
            patterns,
            ctx,
            head,
            slot_span_order,
            frozen_query_rows,
            low,
            query_up_factor,
            kv,
            low_value,
            value_up_factor,
        )
    weights, top = make_weights(queries, bias, kv)
    last_low, weights = lax.optimization_barrier((last_low, weights))
    low_value = jnp.concatenate([low_value, last_low], axis=0)
    return weigh_values(patterns, weights, top, kv, low_value, value_up)


def solution(mesh):
    placed = (
        P("ctx", "head"),
        P("ctx", "head"),
        P("ctx", None),
        P("ctx", None),
        P("head", None),
        P(None, "head"),
        P(),
        P(),
    )
    return jax.shard_map(
        local,
        mesh=mesh,
        in_specs=placed,
        out_specs=(P("ctx", "head"), P("head", "ctx")),
        check_vma=False,
    )
```

```python
import functools
import math

import jax
import jax.numpy as jnp
from jax import lax
from jax.experimental import pallas as pl
from jax.experimental.pallas import tpu as pltpu
from jax.sharding import PartitionSpec as P

HEAD_SIZE = 128
KEY_VALUE_HEADS = 2
ADAPTER_RANK = 32
ADAPTER_SCALE = 0.5
MASKED = -1e30
AXES = ("ctx", "head")
SCORE_FACTOR = math.log2(math.e) / math.sqrt(HEAD_SIZE)
VMEM_LIMIT = 24 * 1024 * 1024


def exchange(value, ctx_bit, head_bits):
    ctx_count, head_count = lax.axis_size("ctx"), lax.axis_size("head")
    pairs = [
        (i * head_count + h, (i ^ ctx_bit) * head_count + (h ^ head_bits))
        for i in range(ctx_count)
        for h in range(head_count)
    ]
    return lax.ppermute(value, AXES, pairs)


def gather_patterns(bits):
    patterns = [0]
    for bit in bits:
        patterns += [p ^ bit for p in patterns]
    return patterns


def half_blocks(patterns, ctx, side):
    half_count = len(patterns) // 2
    found = []
    for first in (0, half_count):
        for other in (0, 1):
            for block in range(first, first + half_count):
                half = (side + patterns[block].bit_count() + other) % 2
                found.append((block, half, 2 * (ctx ^ patterns[block]) + half))
    return found


def prologue_kernel(
    patterns,
    hidden_hbm,
    down_hbm,
    key_hbm,
    value_hbm,
    order_hbm,
    frozen_query_hbm,
    query_up_hbm,
    value_up_hbm,
    low_ref,
    kv_ref,
    bias_ref,
    frozen_query_ref,
    query_up_ref,
    value_up_ref,
    hidden_ref,
    down_ref,
    order_ref,
    sems,
    other_sems,
):
    ctx, head = lax.axis_index("ctx"), lax.axis_index("head")
    side = head % 2
    group = head // (lax.axis_size("head") // KEY_VALUE_HEADS)
    tok_dev = hidden_hbm.shape[0]
    span = tok_dev // 2
    rows = pl.ds(pl.multiple_of(side * span, span), span)
    columns = pl.ds(pl.multiple_of(group * HEAD_SIZE, HEAD_SIZE), HEAD_SIZE)
    chunks = sems.shape[0]
    depth = down_hbm.shape[1] // chunks
    copies = []
    for chunk in range(chunks):
        part = pl.ds(chunk * depth, depth)
        pair = (
            pltpu.make_async_copy(hidden_hbm.at[:, part], hidden_ref.at[:, part], sems.at[chunk, 0]),
            pltpu.make_async_copy(down_hbm.at[:, part], down_ref.at[:, part], sems.at[chunk, 1]),
        )
        for copy in pair:
            copy.start()
        copies.append(pair)
    others = [
        pltpu.make_async_copy(*refs, other_sems.at[n])
        for n, refs in enumerate(
            (
                (order_hbm, order_ref),
                (key_hbm.at[rows, columns], kv_ref.at[:, pl.ds(0, HEAD_SIZE)]),
                (value_hbm.at[rows, columns], kv_ref.at[:, pl.ds(HEAD_SIZE, HEAD_SIZE)]),
                (frozen_query_hbm, frozen_query_ref),
                (query_up_hbm, query_up_ref),
                (value_up_hbm.at[:, columns], value_up_ref),
            )
        )
    ]
    for copy in others:
        copy.start()
    others[0].wait()
    row = lax.broadcasted_iota(jnp.int32, (tok_dev, tok_dev), 0)
    lane = lax.broadcasted_iota(jnp.int32, (tok_dev, tok_dev), 1)
    first_row, first_lane = row < span, lane < span
    inner = row % span - lane % span
    query_spans = jnp.where(first_row, order_ref[2 * ctx], order_ref[2 * ctx + 1])
    entries = half_blocks(patterns, ctx, side)
    for tile in range(len(patterns)):
        first, second = order_ref[entries[2 * tile][2]], order_ref[entries[2 * tile + 1][2]]
        ahead = jnp.where(first_lane, first, second) - query_spans
        bias_ref[:, tile * tok_dev : (tile + 1) * tok_dev] = jnp.where(
            ahead * span <= inner, 0.0, MASKED
        )
    total = jnp.zeros(low_ref.shape, jnp.float32)
    for chunk in range(chunks):
        for copy in copies[chunk]:
            copy.wait()
        part = slice(chunk * depth, (chunk + 1) * depth)
        total += lax.dot_general(
            down_ref[:, part],
            hidden_ref[:, part],
            (((1,), (1,)), ((), ())),
            preferred_element_type=jnp.float32,
        )
    low_ref[...] = total.astype(jnp.bfloat16)
    for copy in others[1:]:
        copy.wait()


def prologue(patterns, hidden, down, keys, values, order, frozen_query, query_up, value_up):
    tok_dev, depth = hidden.shape
    rank = down.shape[0]
    chunks = 4
    hbm = pl.BlockSpec(memory_space=pltpu.HBM)
    vmem = pl.BlockSpec(memory_space=pltpu.VMEM)
    operands = (hidden, down, keys, values, order, frozen_query, query_up, value_up)
    return pl.pallas_call(
        functools.partial(prologue_kernel, patterns),
        out_shape=(
            jax.ShapeDtypeStruct((rank, tok_dev), jnp.bfloat16),
            jax.ShapeDtypeStruct((tok_dev // 2, 2 * HEAD_SIZE), jnp.bfloat16),
            jax.ShapeDtypeStruct((tok_dev, tok_dev * len(patterns)), jnp.float32),
            jax.ShapeDtypeStruct(frozen_query.shape, jnp.bfloat16),
            jax.ShapeDtypeStruct(query_up.shape, jnp.bfloat16),
            jax.ShapeDtypeStruct((value_up.shape[0], HEAD_SIZE), jnp.bfloat16),
        ),
        in_specs=[hbm] * len(operands),
        out_specs=(vmem,) * 6,
        scratch_shapes=[
            pltpu.VMEM(hidden.shape, jnp.bfloat16),
            pltpu.VMEM(down.shape, jnp.bfloat16),
            pltpu.SMEM(order.shape, jnp.int32),
            pltpu.SemaphoreType.DMA((chunks, 2)),
            pltpu.SemaphoreType.DMA((6,)),
        ],
        compiler_params=pltpu.CompilerParams(vmem_limit_bytes=VMEM_LIMIT),
        cost_estimate=pl.CostEstimate(
            flops=2 * tok_dev * depth * rank, bytes_accessed=tok_dev * depth * 4, transcendentals=0
        ),
    )(*(pltpu.with_memory_space_constraint(x, pltpu.HBM) for x in operands))


def queries_kernel(frozen_query_ref, low_ref, query_up_ref, queries_ref):
    queries_ref[...] = (
        frozen_query_ref[...].astype(jnp.float32)
        + ADAPTER_SCALE
        * lax.dot_general(
            low_ref[:ADAPTER_RANK, :],
            query_up_ref[...],
            (((0,), (0,)), ((), ())),
            preferred_element_type=jnp.float32,
        )
    ).astype(jnp.bfloat16)


def adapt_queries(frozen_query, low, query_up):
    tok_dev, width = frozen_query.shape
    vmem = pl.BlockSpec(memory_space=pltpu.VMEM)
    return pl.pallas_call(
        queries_kernel,
        out_shape=jax.ShapeDtypeStruct((tok_dev, width), jnp.bfloat16),
        in_specs=[vmem] * 3,
        out_specs=vmem,
        compiler_params=pltpu.CompilerParams(vmem_limit_bytes=VMEM_LIMIT),
        cost_estimate=pl.CostEstimate(
            flops=2 * tok_dev * width * ADAPTER_RANK,
            bytes_accessed=4 * tok_dev * width,
            transcendentals=0,
        ),
    )(frozen_query, low, query_up)


def fill_values(value_ref, patterns, kv_refs, low_value_ref, value_up_ref):
    span = value_ref.shape[0] // (2 * len(patterns))
    side = lax.axis_index("head") % 2
    value_ref[:, HEAD_SIZE:] = jnp.ones((value_ref.shape[0], HEAD_SIZE), jnp.bfloat16)
    for n, pattern in enumerate(patterns):
        update = ADAPTER_SCALE * lax.dot_general(
            low_value_ref[n * ADAPTER_RANK : (n + 1) * ADAPTER_RANK, :],
            value_up_ref[...],
            (((0,), (0,)), ((), ())),
            preferred_element_type=jnp.float32,
        )
        own_half = (side + pattern.bit_count()) % 2 == 0
        parts = (
            jnp.where(own_half, update[:span], update[span:]),
            jnp.where(own_half, update[span:], update[:span]),
        )
        for other, kv_ref in enumerate(kv_refs):
            at = (other * len(patterns) + n) * span
            value_ref[at : at + span, :HEAD_SIZE] = (
                kv_ref[n * span : (n + 1) * span, HEAD_SIZE:].astype(jnp.float32) + parts[other]
            ).astype(jnp.bfloat16)


def scores_of(queries, kv_ref, bias):
    return (
        lax.dot_general(
            queries,
            kv_ref[:, :HEAD_SIZE],
            (((1,), (1,)), ((), ())),
            preferred_element_type=jnp.float32,
        )
        * SCORE_FACTOR
        + bias
    )


def first_kernel(
    patterns,
    queries_ref,
    bias_ref,
    kv_ref,
    other_kv_ref,
    low_value_ref,
    value_up_ref,
    top_ref,
    sums_ref,
    weights_ref,
    value_ref,
):
    tok_dev, width = queries_ref.shape
    heads = width // HEAD_SIZE
    count = kv_ref.shape[0]
    fill_values(
        value_ref, patterns[: len(patterns) // 2], (kv_ref, other_kv_ref), low_value_ref, value_up_ref
    )
    for head in range(heads):
        columns = slice(head * HEAD_SIZE, (head + 1) * HEAD_SIZE)
        rows = slice(head * tok_dev, (head + 1) * tok_dev)
        scores = [
            scores_of(queries_ref[:, columns], ref, bias_ref[:, n * count : (n + 1) * count])
            for n, ref in enumerate((kv_ref, other_kv_ref))
        ]
        top = jnp.maximum(
            jnp.max(scores[0], axis=1, keepdims=True), jnp.max(scores[1], axis=1, keepdims=True)
        )
        for n in range(2):
            weights_ref[rows, n * count : (n + 1) * count] = jnp.exp2(scores[n] - top).astype(
                jnp.bfloat16
            )
        top_ref[:, columns] = jnp.broadcast_to(top, (tok_dev, HEAD_SIZE))
    for head in range(heads):
        rows = slice(head * tok_dev, (head + 1) * tok_dev)
        sums_ref[rows, :] = jnp.dot(
            weights_ref[rows, :], value_ref[...], preferred_element_type=jnp.float32
        )


def second_kernel(
    patterns, queries_ref, bias_ref, kv_ref, other_kv_ref, first_top_ref, weights_ref, top_ref, scale_ref
):
    tok_dev, width = queries_ref.shape
    count = kv_ref.shape[0]
    before = bias_ref.shape[1] // 2
    for head in range(width // HEAD_SIZE):
        columns = slice(head * HEAD_SIZE, (head + 1) * HEAD_SIZE)
        rows = slice(head * tok_dev, (head + 1) * tok_dev)
        scores = [
            scores_of(
                queries_ref[:, columns],
                ref,
                bias_ref[:, before + n * count : before + (n + 1) * count],
            )
            for n, ref in enumerate((kv_ref, other_kv_ref))
        ]
        new_top = jnp.maximum(
            jnp.max(scores[0], axis=1, keepdims=True), jnp.max(scores[1], axis=1, keepdims=True)
        )
        first_top = first_top_ref[:, columns]
        top = jnp.maximum(first_top, new_top)
        for n in range(2):
            for at in range(0, count, HEAD_SIZE):
                weights_ref[rows, n * count + at : n * count + at + HEAD_SIZE] = jnp.exp2(
                    scores[n][:, at : at + HEAD_SIZE] - top
                ).astype(jnp.bfloat16)
        top_ref[:, columns] = top
        scale_ref[:, columns] = jnp.exp2(first_top - top)


def third_kernel(
    patterns,
    weights_ref,
    top_ref,
    scale_ref,
    first_sums_ref,
    kv_ref,
    other_kv_ref,
    low_value_ref,
    value_up_ref,
    attended_ref,
    normalizer_ref,
    value_ref,
):
    tok_dev, width = top_ref.shape
    fill_values(
        value_ref, patterns[len(patterns) // 2 :], (kv_ref, other_kv_ref), low_value_ref, value_up_ref
    )
    row = lax.broadcasted_iota(jnp.int32, (tok_dev, tok_dev), 0)
    lane = lax.broadcasted_iota(jnp.int32, (tok_dev, tok_dev), 1)
    for head in range(width // HEAD_SIZE):
        columns = slice(head * HEAD_SIZE, (head + 1) * HEAD_SIZE)
        rows = slice(head * tok_dev, (head + 1) * tok_dev)
        sums = jnp.dot(weights_ref[rows, :], value_ref[...], preferred_element_type=jnp.float32)
        scale = scale_ref[:, columns]
        total = first_sums_ref[rows, HEAD_SIZE:] * scale + sums[:, HEAD_SIZE:]
        attended_ref[:, columns] = (
            (first_sums_ref[rows, :HEAD_SIZE] * scale + sums[:, :HEAD_SIZE]) / total
        ).astype(jnp.bfloat16)
        normalizer_ref[head : head + 1, :] = jnp.sum(
            jnp.where(row == lane, top_ref[:, columns] * math.log(2.0) + jnp.log(total), 0.0),
            axis=0,
            keepdims=True,
        )


def call(kernel, patterns, out_shape, scratch_shapes, work, *operands):
    vmem = pl.BlockSpec(memory_space=pltpu.VMEM)
    return pl.pallas_call(
        functools.partial(kernel, patterns),
        out_shape=out_shape,
        in_specs=[vmem] * len(operands),
        out_specs=(vmem,) * len(out_shape),
        scratch_shapes=scratch_shapes,
        compiler_params=pltpu.CompilerParams(vmem_limit_bytes=VMEM_LIMIT),
        cost_estimate=pl.CostEstimate(
            flops=work, bytes_accessed=work // 384, transcendentals=work // 768
        ),
    )(*operands)


def attend_long(patterns, ctx, head, order, frozen_query, low, query_up, kv, low_value, value_up):
    tok_dev, width = frozen_query.shape
    span = tok_dev // 2
    heads = width // HEAD_SIZE
    blocks = len(patterns)
    group = head // (lax.axis_size("head") // KEY_VALUE_HEADS)
    value_up = lax.dynamic_slice_in_dim(value_up, group * HEAD_SIZE, HEAD_SIZE, 1)
    low = low.T
    low_value = low_value.reshape(blocks, ADAPTER_RANK, tok_dev).transpose(0, 2, 1)
    queries = (
        frozen_query.astype(jnp.float32)
        + ADAPTER_SCALE
        * jnp.dot(low[:, :ADAPTER_RANK], query_up, preferred_element_type=jnp.float32)
    ).astype(jnp.bfloat16)
    queries = queries.reshape(tok_dev, heads, HEAD_SIZE).transpose(1, 0, 2).reshape(-1, HEAD_SIZE)
    side = head % 2
    entries = half_blocks(patterns, 0, 0)
    pattern = jnp.array([slot // 2 for _, _, slot in entries], jnp.int32)
    index = jnp.array([block for block, _, _ in entries], jnp.int32)
    half = (jnp.array([half for _, half, _ in entries], jnp.int32) + side) % 2
    key_spans = order[2 * (ctx ^ pattern) + half]
    inner = jnp.arange(span, dtype=jnp.int32)
    key_pos = (key_spans[:, None] * span + inner).reshape(-1)
    query_spans = lax.dynamic_slice_in_dim(order, 2 * ctx, 2)
    query_pos = jnp.tile((query_spans[:, None] * span + inner).reshape(-1), heads)
    low_rows = low_value.reshape(2 * blocks, span, ADAPTER_RANK)[2 * index + half]
    values = (
        kv[:, HEAD_SIZE:].astype(jnp.float32)
        + ADAPTER_SCALE
        * jnp.dot(
            low_rows.reshape(-1, ADAPTER_RANK), value_up, preferred_element_type=jnp.float32
        )
    ).astype(jnp.bfloat16)
    chunk = math.gcd(kv.shape[0], 1024)

    def step(number, state):
        top, total, summed = state
        at = number * chunk
        keys = lax.dynamic_slice_in_dim(kv, at, chunk, 0)[:, :HEAD_SIZE]
        scores = lax.dot_general(
            queries, keys, (((1,), (1,)), ((), ())), preferred_element_type=jnp.float32
        ) * (1.0 / math.sqrt(HEAD_SIZE))
        visible = lax.dynamic_slice_in_dim(key_pos, at, chunk)[None, :] <= query_pos[:, None]
        new_top = jnp.maximum(top, jnp.max(jnp.where(visible, scores, MASKED), axis=1))
        scale = jnp.exp(top - new_top)
        weights = jnp.where(visible, jnp.exp(scores - new_top[:, None]), 0.0)
        summed = summed * scale[:, None] + jnp.dot(
            weights.astype(jnp.bfloat16),
            lax.dynamic_slice_in_dim(values, at, chunk, 0),
            preferred_element_type=jnp.float32,
        )
        return (new_top, total * scale + jnp.sum(weights, axis=1), summed)

    rows = heads * tok_dev
    top, total, summed = lax.fori_loop(
        0,
        kv.shape[0] // chunk,
        step,
        (
            jnp.full((rows,), MASKED, jnp.float32),
            jnp.zeros((rows,), jnp.float32),
            jnp.zeros((rows, HEAD_SIZE), jnp.float32),
        ),
    )
    attended = (summed / total[:, None]).astype(jnp.bfloat16)
    attended = attended.reshape(heads, tok_dev, HEAD_SIZE).transpose(1, 0, 2)
    return attended.reshape(tok_dev, width), (top + jnp.log(total)).reshape(heads, tok_dev)


def local(
    hidden,
    frozen_query_rows,
    frozen_key_rows,
    frozen_value_rows,
    adapter_down_factors,
    query_up_factor,
    value_up_factor,
    slot_span_order,
):
    ctx_count, head_count = lax.axis_size("ctx"), lax.axis_size("head")
    ctx, head = lax.axis_index("ctx"), lax.axis_index("head")
    bits = [ctx_count >> k for k in range(1, ctx_count.bit_length())]
    if len(bits) == 3:
        bits = [bits[0], bits[2], bits[1]]
    patterns = gather_patterns(bits)

    low, kv, bias, frozen_query, query_up, value_up = prologue(
        patterns,
        hidden,
        adapter_down_factors.T,
        frozen_key_rows,
        frozen_value_rows,
        slot_span_order,
        frozen_query_rows,
        query_up_factor,
        value_up_factor,
    )
    head_bit = 1
    while head_bit < head_count:
        other = exchange(low, 0, head_bit | 1)
        low = (low.astype(jnp.float32) + other.astype(jnp.float32)).astype(jnp.bfloat16)
        head_bit *= 2
    low_value = low[ADAPTER_RANK:]
    short = hidden.shape[0] * ctx_count <= 1024
    if short:
        queries = adapt_queries(frozen_query, low, query_up)
    for bit in bits[:-1]:
        low_value = jnp.concatenate([low_value, exchange(low_value, bit, 1)], axis=0)
        kv = jnp.concatenate([kv, exchange(kv, bit, 1)], axis=0)
    if short:
        kv, _ = lax.optimization_barrier((kv, queries))
    last_low = exchange(low_value, bits[-1], 1)
    last_kv = exchange(kv, bits[-1], 1)
    other_kv = exchange(kv, 0, 1)
    last_other_kv = exchange(last_kv, 0, 1)
    if not short:
        return attend_long(
            patterns,
            ctx,
            head,
            slot_span_order,
            frozen_query_rows,
            low,
            query_up_factor,
            jnp.concatenate([kv, other_kv, last_kv, last_other_kv], axis=0),
            jnp.concatenate([low_value, last_low], axis=0),
            value_up_factor,
        )
    tok_dev, width = queries.shape
    rows = width // HEAD_SIZE * tok_dev
    key_count = 2 * kv.shape[0]
    work = 6 * tok_dev * width * key_count
    wide = jax.ShapeDtypeStruct((tok_dev, width), jnp.float32)
    value_scratch = pltpu.VMEM((key_count, 2 * HEAD_SIZE), jnp.bfloat16)
    first_top, sums = call(
        first_kernel,
        patterns,
        (wide, jax.ShapeDtypeStruct((rows, 2 * HEAD_SIZE), jnp.float32)),
        [pltpu.VMEM((rows, key_count), jnp.bfloat16), value_scratch],
        30 * work,
        queries,
        bias,
        kv,
        other_kv,
        low_value,
        value_up,
    )
    weights, top, scale = call(
        second_kernel,
        patterns,
        (jax.ShapeDtypeStruct((rows, key_count), jnp.bfloat16), wide, wide),
        [],
        30 * work,
        queries,
        bias,
        last_kv,
        last_other_kv,
        first_top,
    )
    return call(
        third_kernel,
        patterns,
        (
            jax.ShapeDtypeStruct((tok_dev, width), jnp.bfloat16),
            jax.ShapeDtypeStruct((width // HEAD_SIZE, tok_dev), jnp.float32),
        ),
        [value_scratch],
        work,
        weights,
        top,
        scale,
        sums,
        last_kv,
        last_other_kv,
        last_low,
        value_up,
    )


def solution(mesh):
    placed = (
        P("ctx", "head"),
        P("ctx", "head"),
        P("ctx", None),
        P("ctx", None),
        P("head", None),
        P(None, "head"),
        P(),
        P(),
    )
    return jax.shard_map(
        local,
        mesh=mesh,
        in_specs=placed,
        out_specs=(P("ctx", "head"), P("head", "ctx")),
        check_vma=False,
    )
```

```python
import functools
import math

import jax
import jax.numpy as jnp
from jax import lax
from jax.experimental import pallas as pl
from jax.experimental.pallas import tpu as pltpu
from jax.sharding import PartitionSpec as P

HEAD_SIZE = 128
KEY_VALUE_HEADS = 2
ADAPTER_RANK = 32
ADAPTER_SCALE = 0.5
MASKED = -1e30
AXES = ("ctx", "head")
SCORE_FACTOR = math.log2(math.e) / math.sqrt(HEAD_SIZE)
VMEM_LIMIT = 24 * 1024 * 1024


def exchange(value, ctx_bit, head_bits):
    ctx_count, head_count = lax.axis_size("ctx"), lax.axis_size("head")
    pairs = [
        (i * head_count + h, (i ^ ctx_bit) * head_count + (h ^ head_bits))
        for i in range(ctx_count)
        for h in range(head_count)
    ]
    return lax.ppermute(value, AXES, pairs)


def gather_patterns(bits):
    patterns = [0]
    for bit in bits:
        patterns += [p ^ bit for p in patterns]
    return patterns


def half_blocks(patterns, ctx, side):
    half_count = len(patterns) // 2
    found = []
    for first in (0, half_count):
        for other in (0, 1):
            for block in range(first, first + half_count):
                half = (side + patterns[block].bit_count() + other) % 2
                found.append((block, half, 2 * (ctx ^ patterns[block]) + half))
    return found


def prologue_kernel(
    patterns,
    hidden_hbm,
    down_hbm,
    key_hbm,
    value_hbm,
    order_hbm,
    frozen_query_hbm,
    query_up_hbm,
    value_up_hbm,
    low_ref,
    kv_ref,
    bias_ref,
    frozen_query_ref,
    query_up_ref,
    value_up_ref,
    hidden_ref,
    down_ref,
    order_ref,
    sems,
    other_sems,
):
    ctx, head = lax.axis_index("ctx"), lax.axis_index("head")
    side = head % 2
    group = head // (lax.axis_size("head") // KEY_VALUE_HEADS)
    tok_dev = hidden_hbm.shape[0]
    span = tok_dev // 2
    rows = pl.ds(pl.multiple_of(side * span, span), span)
    columns = pl.ds(pl.multiple_of(group * HEAD_SIZE, HEAD_SIZE), HEAD_SIZE)
    chunks = sems.shape[0]
    depth = down_hbm.shape[1] // chunks
    copies = []
    for chunk in range(chunks):
        part = pl.ds(chunk * depth, depth)
        pair = (
            pltpu.make_async_copy(hidden_hbm.at[:, part], hidden_ref.at[:, part], sems.at[chunk, 0]),
            pltpu.make_async_copy(down_hbm.at[:, part], down_ref.at[:, part], sems.at[chunk, 1]),
        )
        for copy in pair:
            copy.start()
        copies.append(pair)
    others = [
        pltpu.make_async_copy(*refs, other_sems.at[n])
        for n, refs in enumerate(
            (
                (order_hbm, order_ref),
                (key_hbm.at[rows, columns], kv_ref.at[:, pl.ds(0, HEAD_SIZE)]),
                (value_hbm.at[rows, columns], kv_ref.at[:, pl.ds(HEAD_SIZE, HEAD_SIZE)]),
                (frozen_query_hbm, frozen_query_ref),
                (query_up_hbm, query_up_ref),
                (value_up_hbm.at[:, columns], value_up_ref),
            )
        )
    ]
    for copy in others:
        copy.start()
    others[0].wait()
    row = lax.broadcasted_iota(jnp.int32, (tok_dev, tok_dev), 0)
    lane = lax.broadcasted_iota(jnp.int32, (tok_dev, tok_dev), 1)
    first_row, first_lane = row < span, lane < span
    inner = row % span - lane % span
    query_spans = jnp.where(first_row, order_ref[2 * ctx], order_ref[2 * ctx + 1])
    entries = half_blocks(patterns, ctx, side)
    for tile in range(len(patterns)):
        first, second = order_ref[entries[2 * tile][2]], order_ref[entries[2 * tile + 1][2]]
        ahead = jnp.where(first_lane, first, second) - query_spans
        bias_ref[:, tile * tok_dev : (tile + 1) * tok_dev] = jnp.where(
            ahead * span <= inner, 0.0, MASKED
        )
    total = jnp.zeros(low_ref.shape, jnp.float32)
    for chunk in range(chunks):
        for copy in copies[chunk]:
            copy.wait()
        part = slice(chunk * depth, (chunk + 1) * depth)
        total += lax.dot_general(
            down_ref[:, part],
            hidden_ref[:, part],
            (((1,), (1,)), ((), ())),
            preferred_element_type=jnp.float32,
        )
    low_ref[...] = total.astype(jnp.bfloat16)
    for copy in others[1:]:
        copy.wait()


def prologue(patterns, hidden, down, keys, values, order, frozen_query, query_up, value_up):
    tok_dev, depth = hidden.shape
    rank = down.shape[0]
    chunks = 4
    hbm = pl.BlockSpec(memory_space=pltpu.HBM)
    vmem = pl.BlockSpec(memory_space=pltpu.VMEM)
    operands = (hidden, down, keys, values, order, frozen_query, query_up, value_up)
    return pl.pallas_call(
        functools.partial(prologue_kernel, patterns),
        out_shape=(
            jax.ShapeDtypeStruct((rank, tok_dev), jnp.bfloat16),
            jax.ShapeDtypeStruct((tok_dev // 2, 2 * HEAD_SIZE), jnp.bfloat16),
            jax.ShapeDtypeStruct((tok_dev, tok_dev * len(patterns)), jnp.float32),
            jax.ShapeDtypeStruct(frozen_query.shape, jnp.bfloat16),
            jax.ShapeDtypeStruct(query_up.shape, jnp.bfloat16),
            jax.ShapeDtypeStruct((value_up.shape[0], HEAD_SIZE), jnp.bfloat16),
        ),
        in_specs=[hbm] * len(operands),
        out_specs=(vmem,) * 6,
        scratch_shapes=[
            pltpu.VMEM(hidden.shape, jnp.bfloat16),
            pltpu.VMEM(down.shape, jnp.bfloat16),
            pltpu.SMEM(order.shape, jnp.int32),
            pltpu.SemaphoreType.DMA((chunks, 2)),
            pltpu.SemaphoreType.DMA((6,)),
        ],
        compiler_params=pltpu.CompilerParams(vmem_limit_bytes=VMEM_LIMIT),
        cost_estimate=pl.CostEstimate(
            flops=2 * tok_dev * depth * rank, bytes_accessed=tok_dev * depth * 4, transcendentals=0
        ),
    )(*(pltpu.with_memory_space_constraint(x, pltpu.HBM) for x in operands))


def fill_values(value_ref, patterns, kv_refs, low_value_ref, value_up_ref):
    span = value_ref.shape[0] // (2 * len(patterns))
    side = lax.axis_index("head") % 2
    value_ref[:, HEAD_SIZE:] = jnp.ones((value_ref.shape[0], HEAD_SIZE), jnp.bfloat16)
    for n, pattern in enumerate(patterns):
        update = ADAPTER_SCALE * lax.dot_general(
            low_value_ref[n * ADAPTER_RANK : (n + 1) * ADAPTER_RANK, :],
            value_up_ref[...],
            (((0,), (0,)), ((), ())),
            preferred_element_type=jnp.float32,
        )
        own_half = (side + pattern.bit_count()) % 2 == 0
        parts = (
            jnp.where(own_half, update[:span], update[span:]),
            jnp.where(own_half, update[span:], update[:span]),
        )
        for other, kv_ref in enumerate(kv_refs):
            at = (other * len(patterns) + n) * span
            value_ref[at : at + span, :HEAD_SIZE] = (
                kv_ref[n * span : (n + 1) * span, HEAD_SIZE:].astype(jnp.float32) + parts[other]
            ).astype(jnp.bfloat16)


def scores_of(queries, kv_ref, bias):
    return (
        lax.dot_general(
            queries,
            kv_ref[:, :HEAD_SIZE],
            (((1,), (1,)), ((), ())),
            preferred_element_type=jnp.float32,
        )
        * SCORE_FACTOR
        + bias
    )


def first_kernel(
    patterns,
    frozen_query_ref,
    low_ref,
    query_up_ref,
    bias_ref,
    kv_ref,
    other_kv_ref,
    low_value_ref,
    value_up_ref,
    queries_ref,
    top_ref,
    sums_ref,
    weights_ref,
    value_ref,
):
    queries_ref[...] = (
        frozen_query_ref[...].astype(jnp.float32)
        + ADAPTER_SCALE
        * lax.dot_general(
            low_ref[:ADAPTER_RANK, :],
            query_up_ref[...],
            (((0,), (0,)), ((), ())),
            preferred_element_type=jnp.float32,
        )
    ).astype(jnp.bfloat16)
    tok_dev, width = queries_ref.shape
    heads = width // HEAD_SIZE
    count = kv_ref.shape[0]
    fill_values(
        value_ref, patterns[: len(patterns) // 2], (kv_ref, other_kv_ref), low_value_ref, value_up_ref
    )
    for head in range(heads):
        columns = slice(head * HEAD_SIZE, (head + 1) * HEAD_SIZE)
        rows = slice(head * tok_dev, (head + 1) * tok_dev)
        scores = [
            scores_of(queries_ref[:, columns], ref, bias_ref[:, n * count : (n + 1) * count])
            for n, ref in enumerate((kv_ref, other_kv_ref))
        ]
        top = jnp.maximum(
            jnp.max(scores[0], axis=1, keepdims=True), jnp.max(scores[1], axis=1, keepdims=True)
        )
        for n in range(2):
            weights_ref[rows, n * count : (n + 1) * count] = jnp.exp2(scores[n] - top).astype(
                jnp.bfloat16
            )
        top_ref[:, columns] = jnp.broadcast_to(top, (tok_dev, HEAD_SIZE))
    for head in range(heads):
        rows = slice(head * tok_dev, (head + 1) * tok_dev)
        sums_ref[rows, :] = jnp.dot(
            weights_ref[rows, :], value_ref[...], preferred_element_type=jnp.float32
        )


def second_kernel(
    patterns, queries_ref, bias_ref, kv_ref, other_kv_ref, first_top_ref, weights_ref, top_ref, scale_ref
):
    tok_dev, width = queries_ref.shape
    count = kv_ref.shape[0]
    before = bias_ref.shape[1] // 2
    for head in range(width // HEAD_SIZE):
        columns = slice(head * HEAD_SIZE, (head + 1) * HEAD_SIZE)
        rows = slice(head * tok_dev, (head + 1) * tok_dev)
        scores = [
            scores_of(
                queries_ref[:, columns],
                ref,
                bias_ref[:, before + n * count : before + (n + 1) * count],
            )
            for n, ref in enumerate((kv_ref, other_kv_ref))
        ]
        new_top = jnp.maximum(
            jnp.max(scores[0], axis=1, keepdims=True), jnp.max(scores[1], axis=1, keepdims=True)
        )
        first_top = first_top_ref[:, columns]
        top = jnp.maximum(first_top, new_top)
        for n in range(2):
            for at in range(0, count, HEAD_SIZE):
                weights_ref[rows, n * count + at : n * count + at + HEAD_SIZE] = jnp.exp2(
                    scores[n][:, at : at + HEAD_SIZE] - top
                ).astype(jnp.bfloat16)
        top_ref[:, columns] = top
        scale_ref[:, columns] = jnp.exp2(first_top - top)


def third_kernel(
    patterns,
    weights_ref,
    top_ref,
    scale_ref,
    first_sums_ref,
    kv_ref,
    other_kv_ref,
    low_value_ref,
    value_up_ref,
    attended_ref,
    normalizer_ref,
    value_ref,
):
    tok_dev, width = top_ref.shape
    fill_values(
        value_ref, patterns[len(patterns) // 2 :], (kv_ref, other_kv_ref), low_value_ref, value_up_ref
    )
    row = lax.broadcasted_iota(jnp.int32, (tok_dev, tok_dev), 0)
    lane = lax.broadcasted_iota(jnp.int32, (tok_dev, tok_dev), 1)
    for head in range(width // HEAD_SIZE):
        columns = slice(head * HEAD_SIZE, (head + 1) * HEAD_SIZE)
        rows = slice(head * tok_dev, (head + 1) * tok_dev)
        sums = jnp.dot(weights_ref[rows, :], value_ref[...], preferred_element_type=jnp.float32)
        scale = scale_ref[:, columns]
        total = first_sums_ref[rows, HEAD_SIZE:] * scale + sums[:, HEAD_SIZE:]
        attended_ref[:, columns] = (
            (first_sums_ref[rows, :HEAD_SIZE] * scale + sums[:, :HEAD_SIZE]) / total
        ).astype(jnp.bfloat16)
        normalizer_ref[head : head + 1, :] = jnp.sum(
            jnp.where(row == lane, top_ref[:, columns] * math.log(2.0) + jnp.log(total), 0.0),
            axis=0,
            keepdims=True,
        )


def call(kernel, patterns, out_shape, scratch_shapes, work, *operands):
    vmem = pl.BlockSpec(memory_space=pltpu.VMEM)
    return pl.pallas_call(
        functools.partial(kernel, patterns),
        out_shape=out_shape,
        in_specs=[vmem] * len(operands),
        out_specs=(vmem,) * len(out_shape),
        scratch_shapes=scratch_shapes,
        compiler_params=pltpu.CompilerParams(vmem_limit_bytes=VMEM_LIMIT),
        cost_estimate=pl.CostEstimate(
            flops=work, bytes_accessed=work // 384, transcendentals=work // 768
        ),
    )(*operands)


def attend_long(patterns, ctx, head, order, frozen_query, low, query_up, kv, low_value, value_up):
    tok_dev, width = frozen_query.shape
    span = tok_dev // 2
    heads = width // HEAD_SIZE
    blocks = len(patterns)
    group = head // (lax.axis_size("head") // KEY_VALUE_HEADS)
    value_up = lax.dynamic_slice_in_dim(value_up, group * HEAD_SIZE, HEAD_SIZE, 1)
    low = low.T
    low_value = low_value.reshape(blocks, ADAPTER_RANK, tok_dev).transpose(0, 2, 1)
    queries = (
        frozen_query.astype(jnp.float32)
        + ADAPTER_SCALE
        * jnp.dot(low[:, :ADAPTER_RANK], query_up, preferred_element_type=jnp.float32)
    ).astype(jnp.bfloat16)
    queries = queries.reshape(tok_dev, heads, HEAD_SIZE).transpose(1, 0, 2).reshape(-1, HEAD_SIZE)
    side = head % 2
    entries = half_blocks(patterns, 0, 0)
    pattern = jnp.array([slot // 2 for _, _, slot in entries], jnp.int32)
    index = jnp.array([block for block, _, _ in entries], jnp.int32)
    half = (jnp.array([half for _, half, _ in entries], jnp.int32) + side) % 2
    key_spans = order[2 * (ctx ^ pattern) + half]
    inner = jnp.arange(span, dtype=jnp.int32)
    key_pos = (key_spans[:, None] * span + inner).reshape(-1)
    query_spans = lax.dynamic_slice_in_dim(order, 2 * ctx, 2)
    query_pos = jnp.tile((query_spans[:, None] * span + inner).reshape(-1), heads)
    low_rows = low_value.reshape(2 * blocks, span, ADAPTER_RANK)[2 * index + half]
    values = (
        kv[:, HEAD_SIZE:].astype(jnp.float32)
        + ADAPTER_SCALE
        * jnp.dot(
            low_rows.reshape(-1, ADAPTER_RANK), value_up, preferred_element_type=jnp.float32
        )
    ).astype(jnp.bfloat16)
    chunk = math.gcd(kv.shape[0], 1024)

    def step(number, state):
        top, total, summed = state
        at = number * chunk
        keys = lax.dynamic_slice_in_dim(kv, at, chunk, 0)[:, :HEAD_SIZE]
        scores = lax.dot_general(
            queries, keys, (((1,), (1,)), ((), ())), preferred_element_type=jnp.float32
        ) * (1.0 / math.sqrt(HEAD_SIZE))
        visible = lax.dynamic_slice_in_dim(key_pos, at, chunk)[None, :] <= query_pos[:, None]
        new_top = jnp.maximum(top, jnp.max(jnp.where(visible, scores, MASKED), axis=1))
        scale = jnp.exp(top - new_top)
        weights = jnp.where(visible, jnp.exp(scores - new_top[:, None]), 0.0)
        summed = summed * scale[:, None] + jnp.dot(
            weights.astype(jnp.bfloat16),
            lax.dynamic_slice_in_dim(values, at, chunk, 0),
            preferred_element_type=jnp.float32,
        )
        return (new_top, total * scale + jnp.sum(weights, axis=1), summed)

    rows = heads * tok_dev
    top, total, summed = lax.fori_loop(
        0,
        kv.shape[0] // chunk,
        step,
        (
            jnp.full((rows,), MASKED, jnp.float32),
            jnp.zeros((rows,), jnp.float32),
            jnp.zeros((rows, HEAD_SIZE), jnp.float32),
        ),
    )
    attended = (summed / total[:, None]).astype(jnp.bfloat16)
    attended = attended.reshape(heads, tok_dev, HEAD_SIZE).transpose(1, 0, 2)
    return attended.reshape(tok_dev, width), (top + jnp.log(total)).reshape(heads, tok_dev)


def local(
    hidden,
    frozen_query_rows,
    frozen_key_rows,
    frozen_value_rows,
    adapter_down_factors,
    query_up_factor,
    value_up_factor,
    slot_span_order,
):
    ctx_count, head_count = lax.axis_size("ctx"), lax.axis_size("head")
    ctx, head = lax.axis_index("ctx"), lax.axis_index("head")
    bits = [ctx_count >> k for k in range(1, ctx_count.bit_length())]
    if len(bits) == 3:
        bits = [bits[0], bits[2], bits[1]]
    patterns = gather_patterns(bits)

    low, kv, bias, frozen_query, query_up, value_up = prologue(
        patterns,
        hidden,
        adapter_down_factors.T,
        frozen_key_rows,
        frozen_value_rows,
        slot_span_order,
        frozen_query_rows,
        query_up_factor,
        value_up_factor,
    )
    head_bit = 1
    while head_bit < head_count:
        other = exchange(low, 0, head_bit | 1)
        low = (low.astype(jnp.float32) + other.astype(jnp.float32)).astype(jnp.bfloat16)
        head_bit *= 2
    low_value = low[ADAPTER_RANK:]
    short = hidden.shape[0] * ctx_count <= 1024
    for bit in bits[:-1]:
        low_value = jnp.concatenate([low_value, exchange(low_value, bit, 1)], axis=0)
        kv = jnp.concatenate([kv, exchange(kv, bit, 1)], axis=0)
    if short:
        kv, _ = lax.optimization_barrier((kv, low))
    last_low = exchange(low_value, bits[-1], 1)
    last_kv = exchange(kv, bits[-1], 1)
    other_kv = exchange(kv, 0, 1)
    last_other_kv = exchange(last_kv, 0, 1)
    if not short:
        return attend_long(
            patterns,
            ctx,
            head,
            slot_span_order,
            frozen_query_rows,
            low,
            query_up_factor,
            jnp.concatenate([kv, other_kv, last_kv, last_other_kv], axis=0),
            jnp.concatenate([low_value, last_low], axis=0),
            value_up_factor,
        )
    tok_dev, width = frozen_query.shape
    rows = width // HEAD_SIZE * tok_dev
    key_count = 2 * kv.shape[0]
    work = 6 * tok_dev * width * key_count
    wide = jax.ShapeDtypeStruct((tok_dev, width), jnp.float32)
    value_scratch = pltpu.VMEM((key_count, 2 * HEAD_SIZE), jnp.bfloat16)
    queries, first_top, sums = call(
        first_kernel,
        patterns,
        (jax.ShapeDtypeStruct((tok_dev, width), jnp.bfloat16), wide, jax.ShapeDtypeStruct((rows, 2 * HEAD_SIZE), jnp.float32)),
        [pltpu.VMEM((rows, key_count), jnp.bfloat16), value_scratch],
        30 * work,
        frozen_query,
        low,
        query_up,
        bias,
        kv,
        other_kv,
        low_value,
        value_up,
    )
    weights, top, scale = call(
        second_kernel,
        patterns,
        (jax.ShapeDtypeStruct((rows, key_count), jnp.bfloat16), wide, wide),
        [],
        30 * work,
        queries,
        bias,
        last_kv,
        last_other_kv,
        first_top,
    )
    return call(
        third_kernel,
        patterns,
        (
            jax.ShapeDtypeStruct((tok_dev, width), jnp.bfloat16),
            jax.ShapeDtypeStruct((width // HEAD_SIZE, tok_dev), jnp.float32),
        ),
        [value_scratch],
        work,
        weights,
        top,
        scale,
        sums,
        last_kv,
        last_other_kv,
        last_low,
        value_up,
    )


def solution(mesh):
    placed = (
        P("ctx", "head"),
        P("ctx", "head"),
        P("ctx", None),
        P("ctx", None),
        P("head", None),
        P(None, "head"),
        P(),
        P(),
    )
    return jax.shard_map(
        local,
        mesh=mesh,
        in_specs=placed,
        out_specs=(P("ctx", "head"), P("head", "ctx")),
        check_vma=False,
    )
```

```python
import functools
import math

import jax
import jax.numpy as jnp
from jax import lax
from jax.experimental import pallas as pl
from jax.experimental.pallas import tpu as pltpu
from jax.sharding import PartitionSpec as P

HEAD_SIZE = 128
KEY_VALUE_HEADS = 2
ADAPTER_RANK = 32
ADAPTER_SCALE = 0.5
MASKED = -1e30
AXES = ("ctx", "head")
SCORE_FACTOR = math.log2(math.e) / math.sqrt(HEAD_SIZE)
VMEM_LIMIT = 24 * 1024 * 1024


def exchange(value, ctx_bit, head_bits):
    ctx_count, head_count = lax.axis_size("ctx"), lax.axis_size("head")
    pairs = [
        (i * head_count + h, (i ^ ctx_bit) * head_count + (h ^ head_bits))
        for i in range(ctx_count)
        for h in range(head_count)
    ]
    return lax.ppermute(value, AXES, pairs)


def gather_patterns(bits):
    patterns = [0]
    for bit in bits:
        patterns += [p ^ bit for p in patterns]
    return patterns


def half_blocks(patterns, ctx, side):
    half_count = len(patterns) // 2
    found = []
    for first in (0, half_count):
        for other in (0, 1):
            for block in range(first, first + half_count):
                half = (side + patterns[block].bit_count() + other) % 2
                found.append((block, half, 2 * (ctx ^ patterns[block]) + half))
    return found


def prologue_kernel(
    patterns,
    hidden_hbm,
    down_hbm,
    key_hbm,
    value_hbm,
    order_hbm,
    frozen_query_hbm,
    query_up_hbm,
    value_up_hbm,
    low_ref,
    kv_ref,
    bias_ref,
    frozen_query_ref,
    query_up_ref,
    value_up_ref,
    hidden_ref,
    down_ref,
    order_ref,
    sems,
    other_sems,
):
    ctx, head = lax.axis_index("ctx"), lax.axis_index("head")
    side = head % 2
    group = head // (lax.axis_size("head") // KEY_VALUE_HEADS)
    tok_dev = hidden_hbm.shape[0]
    span = tok_dev // 2
    rows = pl.ds(pl.multiple_of(side * span, span), span)
    columns = pl.ds(pl.multiple_of(group * HEAD_SIZE, HEAD_SIZE), HEAD_SIZE)
    chunks = sems.shape[0]
    depth = down_hbm.shape[1] // chunks
    copies = []
    for chunk in range(chunks):
        part = pl.ds(chunk * depth, depth)
        pair = (
            pltpu.make_async_copy(hidden_hbm.at[:, part], hidden_ref.at[:, part], sems.at[chunk, 0]),
            pltpu.make_async_copy(down_hbm.at[:, part], down_ref.at[:, part], sems.at[chunk, 1]),
        )
        for copy in pair:
            copy.start()
        copies.append(pair)
    others = [
        pltpu.make_async_copy(*refs, other_sems.at[n])
        for n, refs in enumerate(
            (
                (order_hbm, order_ref),
                (key_hbm.at[rows, columns], kv_ref.at[:, pl.ds(0, HEAD_SIZE)]),
                (value_hbm.at[rows, columns], kv_ref.at[:, pl.ds(HEAD_SIZE, HEAD_SIZE)]),
                (frozen_query_hbm, frozen_query_ref),
                (query_up_hbm, query_up_ref),
                (value_up_hbm.at[:, columns], value_up_ref),
            )
        )
    ]
    for copy in others:
        copy.start()
    others[0].wait()
    row = lax.broadcasted_iota(jnp.int32, (tok_dev, tok_dev), 0)
    lane = lax.broadcasted_iota(jnp.int32, (tok_dev, tok_dev), 1)
    first_row, first_lane = row < span, lane < span
    inner = row % span - lane % span
    query_spans = jnp.where(first_row, order_ref[2 * ctx], order_ref[2 * ctx + 1])
    entries = half_blocks(patterns, ctx, side)
    for tile in range(len(patterns)):
        first, second = order_ref[entries[2 * tile][2]], order_ref[entries[2 * tile + 1][2]]
        ahead = jnp.where(first_lane, first, second) - query_spans
        bias_ref[:, tile * tok_dev : (tile + 1) * tok_dev] = jnp.where(
            ahead * span <= inner, 0.0, MASKED
        )
    total = jnp.zeros(low_ref.shape, jnp.float32)
    for chunk in range(chunks):
        for copy in copies[chunk]:
            copy.wait()
        part = slice(chunk * depth, (chunk + 1) * depth)
        total += lax.dot_general(
            down_ref[:, part],
            hidden_ref[:, part],
            (((1,), (1,)), ((), ())),
            preferred_element_type=jnp.float32,
        )
    low_ref[...] = total.astype(jnp.bfloat16)
    for copy in others[1:]:
        copy.wait()


def prologue(patterns, hidden, down, keys, values, order, frozen_query, query_up, value_up):
    tok_dev, depth = hidden.shape
    rank = down.shape[0]
    chunks = 4
    hbm = pl.BlockSpec(memory_space=pltpu.HBM)
    vmem = pl.BlockSpec(memory_space=pltpu.VMEM)
    operands = (hidden, down, keys, values, order, frozen_query, query_up, value_up)
    return pl.pallas_call(
        functools.partial(prologue_kernel, patterns),
        out_shape=(
            jax.ShapeDtypeStruct((rank, tok_dev), jnp.bfloat16),
            jax.ShapeDtypeStruct((tok_dev // 2, 2 * HEAD_SIZE), jnp.bfloat16),
            jax.ShapeDtypeStruct((tok_dev, tok_dev * len(patterns)), jnp.float32),
            jax.ShapeDtypeStruct(frozen_query.shape, jnp.bfloat16),
            jax.ShapeDtypeStruct(query_up.shape, jnp.bfloat16),
            jax.ShapeDtypeStruct((value_up.shape[0], HEAD_SIZE), jnp.bfloat16),
        ),
        in_specs=[hbm] * len(operands),
        out_specs=(vmem,) * 6,
        scratch_shapes=[
            pltpu.VMEM(hidden.shape, jnp.bfloat16),
            pltpu.VMEM(down.shape, jnp.bfloat16),
            pltpu.SMEM(order.shape, jnp.int32),
            pltpu.SemaphoreType.DMA((chunks, 2)),
            pltpu.SemaphoreType.DMA((6,)),
        ],
        compiler_params=pltpu.CompilerParams(vmem_limit_bytes=VMEM_LIMIT),
        cost_estimate=pl.CostEstimate(
            flops=2 * tok_dev * depth * rank, bytes_accessed=tok_dev * depth * 4, transcendentals=0
        ),
    )(*(pltpu.with_memory_space_constraint(x, pltpu.HBM) for x in operands))


def fill_values(value_ref, patterns, kv_refs, low_value_ref, value_up_ref):
    span = value_ref.shape[0] // (2 * len(patterns))
    side = lax.axis_index("head") % 2
    value_ref[:, HEAD_SIZE:] = jnp.ones((value_ref.shape[0], HEAD_SIZE), jnp.bfloat16)
    for n, pattern in enumerate(patterns):
        update = ADAPTER_SCALE * lax.dot_general(
            low_value_ref[n * ADAPTER_RANK : (n + 1) * ADAPTER_RANK, :],
            value_up_ref[...],
            (((0,), (0,)), ((), ())),
            preferred_element_type=jnp.float32,
        )
        own_half = (side + pattern.bit_count()) % 2 == 0
        parts = (
            jnp.where(own_half, update[:span], update[span:]),
            jnp.where(own_half, update[span:], update[:span]),
        )
        for other, kv_ref in enumerate(kv_refs):
            at = (other * len(patterns) + n) * span
            value_ref[at : at + span, :HEAD_SIZE] = (
                kv_ref[n * span : (n + 1) * span, HEAD_SIZE:].astype(jnp.float32) + parts[other]
            ).astype(jnp.bfloat16)


def scores_of(queries, kv_ref, bias):
    return (
        lax.dot_general(
            queries,
            kv_ref[:, :HEAD_SIZE],
            (((1,), (1,)), ((), ())),
            preferred_element_type=jnp.float32,
        )
        * SCORE_FACTOR
        + bias
    )


def first_kernel(
    patterns,
    frozen_query_ref,
    low_ref,
    query_up_ref,
    bias_ref,
    kv_ref,
    other_kv_ref,
    low_value_ref,
    value_up_ref,
    queries_ref,
    top_ref,
    sums_ref,
    weights_ref,
    value_ref,
):
    queries_ref[...] = (
        frozen_query_ref[...].astype(jnp.float32)
        + ADAPTER_SCALE
        * lax.dot_general(
            low_ref[:ADAPTER_RANK, :],
            query_up_ref[...],
            (((0,), (0,)), ((), ())),
            preferred_element_type=jnp.float32,
        )
    ).astype(jnp.bfloat16)
    tok_dev, width = queries_ref.shape
    heads = width // HEAD_SIZE
    count = kv_ref.shape[0]
    fill_values(
        value_ref, patterns[: len(patterns) // 2], (kv_ref, other_kv_ref), low_value_ref, value_up_ref
    )
    for head in range(heads):
        columns = slice(head * HEAD_SIZE, (head + 1) * HEAD_SIZE)
        rows = slice(head * tok_dev, (head + 1) * tok_dev)
        scores = [
            scores_of(queries_ref[:, columns], ref, bias_ref[:, n * count : (n + 1) * count])
            for n, ref in enumerate((kv_ref, other_kv_ref))
        ]
        top = jnp.maximum(
            jnp.max(scores[0], axis=1, keepdims=True), jnp.max(scores[1], axis=1, keepdims=True)
        )
        for n in range(2):
            weights_ref[rows, n * count : (n + 1) * count] = jnp.exp2(scores[n] - top).astype(
                jnp.bfloat16
            )
        top_ref[:, columns] = jnp.broadcast_to(top, (tok_dev, HEAD_SIZE))
    for head in range(heads):
        rows = slice(head * tok_dev, (head + 1) * tok_dev)
        sums_ref[rows, :] = jnp.dot(
            weights_ref[rows, :], value_ref[...], preferred_element_type=jnp.float32
        )


def second_kernel(
    patterns, queries_ref, bias_ref, kv_ref, other_kv_ref, first_top_ref, weights_ref, top_ref, scale_ref
):
    tok_dev, width = queries_ref.shape
    count = kv_ref.shape[0]
    before = bias_ref.shape[1] // 2
    for head in range(width // HEAD_SIZE):
        columns = slice(head * HEAD_SIZE, (head + 1) * HEAD_SIZE)
        rows = slice(head * tok_dev, (head + 1) * tok_dev)
        scores = [
            scores_of(
                queries_ref[:, columns],
                ref,
                bias_ref[:, before + n * count : before + (n + 1) * count],
            )
            for n, ref in enumerate((kv_ref, other_kv_ref))
        ]
        new_top = jnp.maximum(
            jnp.max(scores[0], axis=1, keepdims=True), jnp.max(scores[1], axis=1, keepdims=True)
        )
        first_top = first_top_ref[:, columns]
        top = jnp.maximum(first_top, new_top)
        for n in range(2):
            for at in range(0, count, HEAD_SIZE):
                weights_ref[rows, n * count + at : n * count + at + HEAD_SIZE] = jnp.exp2(
                    scores[n][:, at : at + HEAD_SIZE] - top
                ).astype(jnp.bfloat16)
        top_ref[:, columns] = top
        scale_ref[:, columns] = jnp.exp2(first_top - top)


def third_kernel(
    patterns,
    weights_ref,
    top_ref,
    scale_ref,
    first_sums_ref,
    kv_ref,
    other_kv_ref,
    low_value_ref,
    value_up_ref,
    attended_ref,
    normalizer_ref,
    value_ref,
):
    tok_dev, width = top_ref.shape
    fill_values(
        value_ref, patterns[len(patterns) // 2 :], (kv_ref, other_kv_ref), low_value_ref, value_up_ref
    )
    row = lax.broadcasted_iota(jnp.int32, (tok_dev, tok_dev), 0)
    lane = lax.broadcasted_iota(jnp.int32, (tok_dev, tok_dev), 1)
    for head in range(width // HEAD_SIZE):
        columns = slice(head * HEAD_SIZE, (head + 1) * HEAD_SIZE)
        rows = slice(head * tok_dev, (head + 1) * tok_dev)
        sums = jnp.dot(weights_ref[rows, :], value_ref[...], preferred_element_type=jnp.float32)
        scale = scale_ref[:, columns]
        total = first_sums_ref[rows, HEAD_SIZE:] * scale + sums[:, HEAD_SIZE:]
        attended_ref[:, columns] = (
            (first_sums_ref[rows, :HEAD_SIZE] * scale + sums[:, :HEAD_SIZE]) / total
        ).astype(jnp.bfloat16)
        normalizer_ref[head : head + 1, :] = jnp.sum(
            jnp.where(row == lane, top_ref[:, columns] * math.log(2.0) + jnp.log(total), 0.0),
            axis=0,
            keepdims=True,
        )


def call(kernel, patterns, out_shape, scratch_shapes, work, *operands):
    vmem = pl.BlockSpec(memory_space=pltpu.VMEM)
    return pl.pallas_call(
        functools.partial(kernel, patterns),
        out_shape=out_shape,
        in_specs=[vmem] * len(operands),
        out_specs=(vmem,) * len(out_shape),
        scratch_shapes=scratch_shapes,
        compiler_params=pltpu.CompilerParams(vmem_limit_bytes=VMEM_LIMIT),
        cost_estimate=pl.CostEstimate(
            flops=work, bytes_accessed=work // 384, transcendentals=work // 768
        ),
    )(*operands)


def attend_long(patterns, ctx, head, order, frozen_query, low, query_up, kv, low_value, value_up):
    tok_dev, width = frozen_query.shape
    span = tok_dev // 2
    heads = width // HEAD_SIZE
    blocks = len(patterns)
    group = head // (lax.axis_size("head") // KEY_VALUE_HEADS)
    value_up = lax.dynamic_slice_in_dim(value_up, group * HEAD_SIZE, HEAD_SIZE, 1)
    low = low.T
    low_value = low_value.reshape(blocks, ADAPTER_RANK, tok_dev).transpose(0, 2, 1)
    queries = (
        frozen_query.astype(jnp.float32)
        + ADAPTER_SCALE
        * jnp.dot(low[:, :ADAPTER_RANK], query_up, preferred_element_type=jnp.float32)
    ).astype(jnp.bfloat16)
    queries = queries.reshape(tok_dev, heads, HEAD_SIZE).transpose(1, 0, 2).reshape(-1, HEAD_SIZE)
    side = head % 2
    entries = half_blocks(patterns, 0, 0)
    pattern = jnp.array([slot // 2 for _, _, slot in entries], jnp.int32)
    index = jnp.array([block for block, _, _ in entries], jnp.int32)
    half = (jnp.array([half for _, half, _ in entries], jnp.int32) + side) % 2
    key_spans = order[2 * (ctx ^ pattern) + half]
    inner = jnp.arange(span, dtype=jnp.int32)
    key_pos = (key_spans[:, None] * span + inner).reshape(-1)
    query_spans = lax.dynamic_slice_in_dim(order, 2 * ctx, 2)
    query_pos = jnp.tile((query_spans[:, None] * span + inner).reshape(-1), heads)
    low_rows = low_value.reshape(2 * blocks, span, ADAPTER_RANK)[2 * index + half]
    values = (
        kv[:, HEAD_SIZE:].astype(jnp.float32)
        + ADAPTER_SCALE
        * jnp.dot(
            low_rows.reshape(-1, ADAPTER_RANK), value_up, preferred_element_type=jnp.float32
        )
    ).astype(jnp.bfloat16)
    chunk = math.gcd(kv.shape[0], 1024)

    def step(number, state):
        top, total, summed = state
        at = number * chunk
        keys = lax.dynamic_slice_in_dim(kv, at, chunk, 0)[:, :HEAD_SIZE]
        scores = lax.dot_general(
            queries, keys, (((1,), (1,)), ((), ())), preferred_element_type=jnp.float32
        ) * (1.0 / math.sqrt(HEAD_SIZE))
        visible = lax.dynamic_slice_in_dim(key_pos, at, chunk)[None, :] <= query_pos[:, None]
        new_top = jnp.maximum(top, jnp.max(jnp.where(visible, scores, MASKED), axis=1))
        scale = jnp.exp(top - new_top)
        weights = jnp.where(visible, jnp.exp(scores - new_top[:, None]), 0.0)
        summed = summed * scale[:, None] + jnp.dot(
            weights.astype(jnp.bfloat16),
            lax.dynamic_slice_in_dim(values, at, chunk, 0),
            preferred_element_type=jnp.float32,
        )
        return (new_top, total * scale + jnp.sum(weights, axis=1), summed)

    rows = heads * tok_dev
    top, total, summed = lax.fori_loop(
        0,
        kv.shape[0] // chunk,
        step,
        (
            jnp.full((rows,), MASKED, jnp.float32),
            jnp.zeros((rows,), jnp.float32),
            jnp.zeros((rows, HEAD_SIZE), jnp.float32),
        ),
    )
    attended = (summed / total[:, None]).astype(jnp.bfloat16)
    attended = attended.reshape(heads, tok_dev, HEAD_SIZE).transpose(1, 0, 2)
    return attended.reshape(tok_dev, width), (top + jnp.log(total)).reshape(heads, tok_dev)


def local(
    hidden,
    frozen_query_rows,
    frozen_key_rows,
    frozen_value_rows,
    adapter_down_factors,
    query_up_factor,
    value_up_factor,
    slot_span_order,
):
    ctx_count, head_count = lax.axis_size("ctx"), lax.axis_size("head")
    ctx, head = lax.axis_index("ctx"), lax.axis_index("head")
    bits = [ctx_count >> k for k in range(1, ctx_count.bit_length())]
    patterns = gather_patterns(bits)

    low, kv, bias, frozen_query, query_up, value_up = prologue(
        patterns,
        hidden,
        adapter_down_factors.T,
        frozen_key_rows,
        frozen_value_rows,
        slot_span_order,
        frozen_query_rows,
        query_up_factor,
        value_up_factor,
    )
    head_bit = 1
    while head_bit < head_count:
        other = exchange(low, 0, head_bit | 1)
        low = (low.astype(jnp.float32) + other.astype(jnp.float32)).astype(jnp.bfloat16)
        head_bit *= 2
    low_value = low[ADAPTER_RANK:]
    short = hidden.shape[0] * ctx_count <= 1024
    for bit in bits[:-1]:
        low_value = jnp.concatenate([low_value, exchange(low_value, bit, 1)], axis=0)
        kv = jnp.concatenate([kv, exchange(kv, bit, 1)], axis=0)
    if short:
        kv, _ = lax.optimization_barrier((kv, low))
    last_low = exchange(low_value, bits[-1], 1)
    last_kv = exchange(kv, bits[-1], 1)
    other_kv = exchange(kv, 0, 1)
    last_other_kv = exchange(last_kv, 0, 1)
    if not short:
        return attend_long(
            patterns,
            ctx,
            head,
            slot_span_order,
            frozen_query_rows,
            low,
            query_up_factor,
            jnp.concatenate([kv, other_kv, last_kv, last_other_kv], axis=0),
            jnp.concatenate([low_value, last_low], axis=0),
            value_up_factor,
        )
    tok_dev, width = frozen_query.shape
    rows = width // HEAD_SIZE * tok_dev
    key_count = 2 * kv.shape[0]
    work = 6 * tok_dev * width * key_count
    wide = jax.ShapeDtypeStruct((tok_dev, width), jnp.float32)
    value_scratch = pltpu.VMEM((key_count, 2 * HEAD_SIZE), jnp.bfloat16)
    queries, first_top, sums = call(
        first_kernel,
        patterns,
        (jax.ShapeDtypeStruct((tok_dev, width), jnp.bfloat16), wide, jax.ShapeDtypeStruct((rows, 2 * HEAD_SIZE), jnp.float32)),
        [pltpu.VMEM((rows, key_count), jnp.bfloat16), value_scratch],
        30 * work,
        frozen_query,
        low,
        query_up,
        bias,
        kv,
        other_kv,
        low_value,
        value_up,
    )
    weights, top, scale = call(
        second_kernel,
        patterns,
        (jax.ShapeDtypeStruct((rows, key_count), jnp.bfloat16), wide, wide),
        [],
        30 * work,
        queries,
        bias,
        last_kv,
        last_other_kv,
        first_top,
    )
    return call(
        third_kernel,
        patterns,
        (
            jax.ShapeDtypeStruct((tok_dev, width), jnp.bfloat16),
            jax.ShapeDtypeStruct((width // HEAD_SIZE, tok_dev), jnp.float32),
        ),
        [value_scratch],
        work,
        weights,
        top,
        scale,
        sums,
        last_kv,
        last_other_kv,
        last_low,
        value_up,
    )


def solution(mesh):
    placed = (
        P("ctx", "head"),
        P("ctx", "head"),
        P("ctx", None),
        P("ctx", None),
        P("head", None),
        P(None, "head"),
        P(),
        P(),
    )
    return jax.shard_map(
        local,
        mesh=mesh,
        in_specs=placed,
        out_specs=(P("ctx", "head"), P("head", "ctx")),
        check_vma=False,
    )
```

```python
import functools
import math

import jax
import jax.numpy as jnp
from jax import lax
from jax.experimental import pallas as pl
from jax.experimental.pallas import tpu as pltpu
from jax.sharding import PartitionSpec as P

HEAD_SIZE = 128
KEY_VALUE_HEADS = 2
ADAPTER_RANK = 32
ADAPTER_SCALE = 0.5
MASKED = -1e30
AXES = ("ctx", "head")
SCORE_FACTOR = math.log2(math.e) / math.sqrt(HEAD_SIZE)
VMEM_LIMIT = 24 * 1024 * 1024


def exchange(value, ctx_bit, head_bits):
    ctx_count, head_count = lax.axis_size("ctx"), lax.axis_size("head")
    pairs = [
        (i * head_count + h, (i ^ ctx_bit) * head_count + (h ^ head_bits))
        for i in range(ctx_count)
        for h in range(head_count)
    ]
    return lax.ppermute(value, AXES, pairs)


def gather_patterns(bits):
    patterns = [0]
    for bit in bits:
        patterns += [p ^ bit for p in patterns]
    return patterns


def half_blocks(patterns, ctx, side):
    half_count = len(patterns) // 2
    found = []
    for first in (0, half_count):
        for other in (0, 1):
            for block in range(first, first + half_count):
                half = (side + patterns[block].bit_count() + other) % 2
                found.append((block, half, 2 * (ctx ^ patterns[block]) + half))
    return found


def prologue_kernel(
    patterns,
    hidden_hbm,
    down_hbm,
    key_hbm,
    value_hbm,
    order_hbm,
    frozen_query_hbm,
    query_up_hbm,
    value_up_hbm,
    low_ref,
    kv_ref,
    bias_ref,
    frozen_query_ref,
    query_up_ref,
    value_up_ref,
    hidden_ref,
    down_ref,
    order_ref,
    sems,
    other_sems,
):
    ctx, head = lax.axis_index("ctx"), lax.axis_index("head")
    side = head % 2
    group = head // (lax.axis_size("head") // KEY_VALUE_HEADS)
    tok_dev = hidden_hbm.shape[0]
    span = tok_dev // 2
    rows = pl.ds(pl.multiple_of(side * span, span), span)
    columns = pl.ds(pl.multiple_of(group * HEAD_SIZE, HEAD_SIZE), HEAD_SIZE)
    copies = (
        pltpu.make_async_copy(hidden_hbm, hidden_ref, sems.at[0]),
        pltpu.make_async_copy(down_hbm, down_ref, sems.at[1]),
    )
    for copy in copies:
        copy.start()
    others = [
        pltpu.make_async_copy(*refs, other_sems.at[n])
        for n, refs in enumerate(
            (
                (order_hbm, order_ref),
                (key_hbm.at[rows, columns], kv_ref.at[:, pl.ds(0, HEAD_SIZE)]),
                (value_hbm.at[rows, columns], kv_ref.at[:, pl.ds(HEAD_SIZE, HEAD_SIZE)]),
                (frozen_query_hbm, frozen_query_ref),
                (query_up_hbm, query_up_ref),
                (value_up_hbm.at[:, columns], value_up_ref),
            )
        )
    ]
    for copy in others:
        copy.start()
    others[0].wait()
    row = lax.broadcasted_iota(jnp.int32, (tok_dev, tok_dev), 0)
    lane = lax.broadcasted_iota(jnp.int32, (tok_dev, tok_dev), 1)
    first_row, first_lane = row < span, lane < span
    inner = row % span - lane % span
    query_spans = jnp.where(first_row, order_ref[2 * ctx], order_ref[2 * ctx + 1])
    entries = half_blocks(patterns, ctx, side)
    for tile in range(len(patterns)):
        first, second = order_ref[entries[2 * tile][2]], order_ref[entries[2 * tile + 1][2]]
        ahead = jnp.where(first_lane, first, second) - query_spans
        bias_ref[:, tile * tok_dev : (tile + 1) * tok_dev] = jnp.where(
            ahead * span <= inner, 0.0, MASKED
        )
    for copy in copies:
        copy.wait()
    low_ref[...] = lax.dot_general(
        down_ref[...],
        hidden_ref[...],
        (((1,), (1,)), ((), ())),
        preferred_element_type=jnp.float32,
    ).astype(jnp.bfloat16)
    for copy in others[1:]:
        copy.wait()


def prologue(patterns, hidden, down, keys, values, order, frozen_query, query_up, value_up):
    tok_dev, depth = hidden.shape
    rank = down.shape[0]
    hbm = pl.BlockSpec(memory_space=pltpu.HBM)
    vmem = pl.BlockSpec(memory_space=pltpu.VMEM)
    operands = (hidden, down, keys, values, order, frozen_query, query_up, value_up)
    return pl.pallas_call(
        functools.partial(prologue_kernel, patterns),
        out_shape=(
            jax.ShapeDtypeStruct((rank, tok_dev), jnp.bfloat16),
            jax.ShapeDtypeStruct((tok_dev // 2, 2 * HEAD_SIZE), jnp.bfloat16),
            jax.ShapeDtypeStruct((tok_dev, tok_dev * len(patterns)), jnp.float32),
            jax.ShapeDtypeStruct(frozen_query.shape, jnp.bfloat16),
            jax.ShapeDtypeStruct(query_up.shape, jnp.bfloat16),
            jax.ShapeDtypeStruct((value_up.shape[0], HEAD_SIZE), jnp.bfloat16),
        ),
        in_specs=[hbm] * len(operands),
        out_specs=(vmem,) * 6,
        scratch_shapes=[
            pltpu.VMEM(hidden.shape, jnp.bfloat16),
            pltpu.VMEM(down.shape, jnp.bfloat16),
            pltpu.SMEM(order.shape, jnp.int32),
            pltpu.SemaphoreType.DMA((2,)),
            pltpu.SemaphoreType.DMA((6,)),
        ],
        compiler_params=pltpu.CompilerParams(vmem_limit_bytes=VMEM_LIMIT),
        cost_estimate=pl.CostEstimate(
            flops=2 * tok_dev * depth * rank, bytes_accessed=tok_dev * depth * 4, transcendentals=0
        ),
    )(*(pltpu.with_memory_space_constraint(x, pltpu.HBM) for x in operands))


def fill_values(value_ref, patterns, kv_refs, low_value_ref, value_up_ref):
    span = value_ref.shape[0] // (2 * len(patterns))
    side = lax.axis_index("head") % 2
    value_ref[:, HEAD_SIZE:] = jnp.ones((value_ref.shape[0], HEAD_SIZE), jnp.bfloat16)
    for n, pattern in enumerate(patterns):
        update = ADAPTER_SCALE * lax.dot_general(
            low_value_ref[n * ADAPTER_RANK : (n + 1) * ADAPTER_RANK, :],
            value_up_ref[...],
            (((0,), (0,)), ((), ())),
            preferred_element_type=jnp.float32,
        )
        own_half = (side + pattern.bit_count()) % 2 == 0
        parts = (
            jnp.where(own_half, update[:span], update[span:]),
            jnp.where(own_half, update[span:], update[:span]),
        )
        for other, kv_ref in enumerate(kv_refs):
            at = (other * len(patterns) + n) * span
            value_ref[at : at + span, :HEAD_SIZE] = (
                kv_ref[n * span : (n + 1) * span, HEAD_SIZE:].astype(jnp.float32) + parts[other]
            ).astype(jnp.bfloat16)


def scores_of(queries, kv_ref, bias):
    return (
        lax.dot_general(
            queries,
            kv_ref[:, :HEAD_SIZE],
            (((1,), (1,)), ((), ())),
            preferred_element_type=jnp.float32,
        )
        * SCORE_FACTOR
        + bias
    )


def first_kernel(
    patterns,
    frozen_query_ref,
    low_ref,
    query_up_ref,
    bias_ref,
    kv_ref,
    other_kv_ref,
    low_value_ref,
    value_up_ref,
    queries_ref,
    top_ref,
    sums_ref,
    weights_ref,
    value_ref,
):
    queries_ref[...] = (
        frozen_query_ref[...].astype(jnp.float32)
        + ADAPTER_SCALE
        * lax.dot_general(
            low_ref[:ADAPTER_RANK, :],
            query_up_ref[...],
            (((0,), (0,)), ((), ())),
            preferred_element_type=jnp.float32,
        )
    ).astype(jnp.bfloat16)
    tok_dev, width = queries_ref.shape
    heads = width // HEAD_SIZE
    count = kv_ref.shape[0]
    fill_values(
        value_ref, patterns[: len(patterns) // 2], (kv_ref, other_kv_ref), low_value_ref, value_up_ref
    )
    for head in range(heads):
        columns = slice(head * HEAD_SIZE, (head + 1) * HEAD_SIZE)
        rows = slice(head * tok_dev, (head + 1) * tok_dev)
        scores = [
            scores_of(queries_ref[:, columns], ref, bias_ref[:, n * count : (n + 1) * count])
            for n, ref in enumerate((kv_ref, other_kv_ref))
        ]
        top = jnp.maximum(
            jnp.max(scores[0], axis=1, keepdims=True), jnp.max(scores[1], axis=1, keepdims=True)
        )
        for n in range(2):
            weights_ref[rows, n * count : (n + 1) * count] = jnp.exp2(scores[n] - top).astype(
                jnp.bfloat16
            )
        top_ref[:, columns] = jnp.broadcast_to(top, (tok_dev, HEAD_SIZE))
    for head in range(heads):
        rows = slice(head * tok_dev, (head + 1) * tok_dev)
        sums_ref[rows, :] = jnp.dot(
            weights_ref[rows, :], value_ref[...], preferred_element_type=jnp.float32
        )


def second_kernel(
    patterns, queries_ref, bias_ref, kv_ref, other_kv_ref, first_top_ref, weights_ref, top_ref, scale_ref
):
    tok_dev, width = queries_ref.shape
    count = kv_ref.shape[0]
    before = bias_ref.shape[1] // 2
    for head in range(width // HEAD_SIZE):
        columns = slice(head * HEAD_SIZE, (head + 1) * HEAD_SIZE)
        rows = slice(head * tok_dev, (head + 1) * tok_dev)
        scores = [
            scores_of(
                queries_ref[:, columns],
                ref,
                bias_ref[:, before + n * count : before + (n + 1) * count],
            )
            for n, ref in enumerate((kv_ref, other_kv_ref))
        ]
        new_top = jnp.maximum(
            jnp.max(scores[0], axis=1, keepdims=True), jnp.max(scores[1], axis=1, keepdims=True)
        )
        first_top = first_top_ref[:, columns]
        top = jnp.maximum(first_top, new_top)
        for n in range(2):
            for at in range(0, count, HEAD_SIZE):
                weights_ref[rows, n * count + at : n * count + at + HEAD_SIZE] = jnp.exp2(
                    scores[n][:, at : at + HEAD_SIZE] - top
                ).astype(jnp.bfloat16)
        top_ref[:, columns] = top
        scale_ref[:, columns] = jnp.exp2(first_top - top)


def third_kernel(
    patterns,
    weights_ref,
    top_ref,
    scale_ref,
    first_sums_ref,
    kv_ref,
    other_kv_ref,
    low_value_ref,
    value_up_ref,
    attended_ref,
    normalizer_ref,
    value_ref,
):
    tok_dev, width = top_ref.shape
    fill_values(
        value_ref, patterns[len(patterns) // 2 :], (kv_ref, other_kv_ref), low_value_ref, value_up_ref
    )
    row = lax.broadcasted_iota(jnp.int32, (tok_dev, tok_dev), 0)
    lane = lax.broadcasted_iota(jnp.int32, (tok_dev, tok_dev), 1)
    for head in range(width // HEAD_SIZE):
        columns = slice(head * HEAD_SIZE, (head + 1) * HEAD_SIZE)
        rows = slice(head * tok_dev, (head + 1) * tok_dev)
        sums = jnp.dot(weights_ref[rows, :], value_ref[...], preferred_element_type=jnp.float32)
        scale = scale_ref[:, columns]
        total = first_sums_ref[rows, HEAD_SIZE:] * scale + sums[:, HEAD_SIZE:]
        attended_ref[:, columns] = (
            (first_sums_ref[rows, :HEAD_SIZE] * scale + sums[:, :HEAD_SIZE]) / total
        ).astype(jnp.bfloat16)
        normalizer_ref[head : head + 1, :] = jnp.sum(
            jnp.where(row == lane, top_ref[:, columns] * math.log(2.0) + jnp.log(total), 0.0),
            axis=0,
            keepdims=True,
        )


def call(kernel, patterns, out_shape, scratch_shapes, work, *operands):
    vmem = pl.BlockSpec(memory_space=pltpu.VMEM)
    return pl.pallas_call(
        functools.partial(kernel, patterns),
        out_shape=out_shape,
        in_specs=[vmem] * len(operands),
        out_specs=(vmem,) * len(out_shape),
        scratch_shapes=scratch_shapes,
        compiler_params=pltpu.CompilerParams(vmem_limit_bytes=VMEM_LIMIT),
        cost_estimate=pl.CostEstimate(
            flops=work, bytes_accessed=work // 384, transcendentals=work // 768
        ),
    )(*operands)


def attend_long(patterns, ctx, head, order, frozen_query, low, query_up, kv, low_value, value_up):
    tok_dev, width = frozen_query.shape
    span = tok_dev // 2
    heads = width // HEAD_SIZE
    blocks = len(patterns)
    group = head // (lax.axis_size("head") // KEY_VALUE_HEADS)
    value_up = lax.dynamic_slice_in_dim(value_up, group * HEAD_SIZE, HEAD_SIZE, 1)
    low = low.T
    low_value = low_value.reshape(blocks, ADAPTER_RANK, tok_dev).transpose(0, 2, 1)
    queries = (
        frozen_query.astype(jnp.float32)
        + ADAPTER_SCALE
        * jnp.dot(low[:, :ADAPTER_RANK], query_up, preferred_element_type=jnp.float32)
    ).astype(jnp.bfloat16)
    queries = queries.reshape(tok_dev, heads, HEAD_SIZE).transpose(1, 0, 2).reshape(-1, HEAD_SIZE)
    side = head % 2
    entries = half_blocks(patterns, 0, 0)
    pattern = jnp.array([slot // 2 for _, _, slot in entries], jnp.int32)
    index = jnp.array([block for block, _, _ in entries], jnp.int32)
    half = (jnp.array([half for _, half, _ in entries], jnp.int32) + side) % 2
    key_spans = order[2 * (ctx ^ pattern) + half]
    inner = jnp.arange(span, dtype=jnp.int32)
    key_pos = (key_spans[:, None] * span + inner).reshape(-1)
    query_spans = lax.dynamic_slice_in_dim(order, 2 * ctx, 2)
    query_pos = jnp.tile((query_spans[:, None] * span + inner).reshape(-1), heads)
    low_rows = low_value.reshape(2 * blocks, span, ADAPTER_RANK)[2 * index + half]
    values = (
        kv[:, HEAD_SIZE:].astype(jnp.float32)
        + ADAPTER_SCALE
        * jnp.dot(
            low_rows.reshape(-1, ADAPTER_RANK), value_up, preferred_element_type=jnp.float32
        )
    ).astype(jnp.bfloat16)
    chunk = math.gcd(kv.shape[0], 1024)

    def step(number, state):
        top, total, summed = state
        at = number * chunk
        keys = lax.dynamic_slice_in_dim(kv, at, chunk, 0)[:, :HEAD_SIZE]
        scores = lax.dot_general(
            queries, keys, (((1,), (1,)), ((), ())), preferred_element_type=jnp.float32
        ) * (1.0 / math.sqrt(HEAD_SIZE))
        visible = lax.dynamic_slice_in_dim(key_pos, at, chunk)[None, :] <= query_pos[:, None]
        new_top = jnp.maximum(top, jnp.max(jnp.where(visible, scores, MASKED), axis=1))
        scale = jnp.exp(top - new_top)
        weights = jnp.where(visible, jnp.exp(scores - new_top[:, None]), 0.0)
        summed = summed * scale[:, None] + jnp.dot(
            weights.astype(jnp.bfloat16),
            lax.dynamic_slice_in_dim(values, at, chunk, 0),
            preferred_element_type=jnp.float32,
        )
        return (new_top, total * scale + jnp.sum(weights, axis=1), summed)

    rows = heads * tok_dev
    top, total, summed = lax.fori_loop(
        0,
        kv.shape[0] // chunk,
        step,
        (
            jnp.full((rows,), MASKED, jnp.float32),
            jnp.zeros((rows,), jnp.float32),
            jnp.zeros((rows, HEAD_SIZE), jnp.float32),
        ),
    )
    attended = (summed / total[:, None]).astype(jnp.bfloat16)
    attended = attended.reshape(heads, tok_dev, HEAD_SIZE).transpose(1, 0, 2)
    return attended.reshape(tok_dev, width), (top + jnp.log(total)).reshape(heads, tok_dev)


def local(
    hidden,
    frozen_query_rows,
    frozen_key_rows,
    frozen_value_rows,
    adapter_down_factors,
    query_up_factor,
    value_up_factor,
    slot_span_order,
):
    ctx_count, head_count = lax.axis_size("ctx"), lax.axis_size("head")
    ctx, head = lax.axis_index("ctx"), lax.axis_index("head")
    bits = [ctx_count >> k for k in range(1, ctx_count.bit_length())]
    patterns = gather_patterns(bits)

    low, kv, bias, frozen_query, query_up, value_up = prologue(
        patterns,
        hidden,
        adapter_down_factors.T,
        frozen_key_rows,
        frozen_value_rows,
        slot_span_order,
        frozen_query_rows,
        query_up_factor,
        value_up_factor,
    )
    head_bit = 1
    while head_bit < head_count:
        other = exchange(low, 0, head_bit | 1)
        low = (low.astype(jnp.float32) + other.astype(jnp.float32)).astype(jnp.bfloat16)
        head_bit *= 2
    low_value = low[ADAPTER_RANK:]
    short = hidden.shape[0] * ctx_count <= 1024
    for bit in bits[:-1]:
        low_value = jnp.concatenate([low_value, exchange(low_value, bit, 1)], axis=0)
        kv = jnp.concatenate([kv, exchange(kv, bit, 1)], axis=0)
    if short:
        kv, _ = lax.optimization_barrier((kv, low))
    last_low = exchange(low_value, bits[-1], 1)
    last_kv = exchange(kv, bits[-1], 1)
    other_kv = exchange(kv, 0, 1)
    last_other_kv = exchange(last_kv, 0, 1)
    if not short:
        return attend_long(
            patterns,
            ctx,
            head,
            slot_span_order,
            frozen_query_rows,
            low,
            query_up_factor,
            jnp.concatenate([kv, other_kv, last_kv, last_other_kv], axis=0),
            jnp.concatenate([low_value, last_low], axis=0),
            value_up_factor,
        )
    tok_dev, width = frozen_query.shape
    rows = width // HEAD_SIZE * tok_dev
    key_count = 2 * kv.shape[0]
    work = 6 * tok_dev * width * key_count
    wide = jax.ShapeDtypeStruct((tok_dev, width), jnp.float32)
    value_scratch = pltpu.VMEM((key_count, 2 * HEAD_SIZE), jnp.bfloat16)
    queries, first_top, sums = call(
        first_kernel,
        patterns,
        (jax.ShapeDtypeStruct((tok_dev, width), jnp.bfloat16), wide, jax.ShapeDtypeStruct((rows, 2 * HEAD_SIZE), jnp.float32)),
        [pltpu.VMEM((rows, key_count), jnp.bfloat16), value_scratch],
        30 * work,
        frozen_query,
        low,
        query_up,
        bias,
        kv,
        other_kv,
        low_value,
        value_up,
    )
    weights, top, scale = call(
        second_kernel,
        patterns,
        (jax.ShapeDtypeStruct((rows, key_count), jnp.bfloat16), wide, wide),
        [],
        30 * work,
        queries,
        bias,
        last_kv,
        last_other_kv,
        first_top,
    )
    return call(
        third_kernel,
        patterns,
        (
            jax.ShapeDtypeStruct((tok_dev, width), jnp.bfloat16),
            jax.ShapeDtypeStruct((width // HEAD_SIZE, tok_dev), jnp.float32),
        ),
        [value_scratch],
        work,
        weights,
        top,
        scale,
        sums,
        last_kv,
        last_other_kv,
        last_low,
        value_up,
    )


def solution(mesh):
    placed = (
        P("ctx", "head"),
        P("ctx", "head"),
        P("ctx", None),
        P("ctx", None),
        P("head", None),
        P(None, "head"),
        P(),
        P(),
    )
    return jax.shard_map(
        local,
        mesh=mesh,
        in_specs=placed,
        out_specs=(P("ctx", "head"), P("head", "ctx")),
        check_vma=False,
    )
```

```python
import functools
import math

import jax
import jax.numpy as jnp
from jax import lax
from jax.experimental import pallas as pl
from jax.experimental.pallas import tpu as pltpu
from jax.sharding import PartitionSpec as P

HEAD_SIZE = 128
KEY_VALUE_HEADS = 2
ADAPTER_RANK = 32
ADAPTER_SCALE = 0.5
MASKED = -1e30
AXES = ("ctx", "head")
SCORE_FACTOR = math.log2(math.e) / math.sqrt(HEAD_SIZE)
VMEM_LIMIT = 24 * 1024 * 1024


def exchange(value, ctx_bit, head_bits):
    ctx_count, head_count = lax.axis_size("ctx"), lax.axis_size("head")
    pairs = [
        (i * head_count + h, (i ^ ctx_bit) * head_count + (h ^ head_bits))
        for i in range(ctx_count)
        for h in range(head_count)
    ]
    return lax.ppermute(value, AXES, pairs)


def gather_patterns(bits):
    patterns = [0]
    for bit in bits:
        patterns += [p ^ bit for p in patterns]
    return patterns


def half_blocks(patterns, ctx, side):
    half_count = len(patterns) // 2
    found = []
    for first in (0, half_count):
        for other in (0, 1):
            for block in range(first, first + half_count):
                half = (side + patterns[block].bit_count() + other) % 2
                found.append((block, half, 2 * (ctx ^ patterns[block]) + half))
    return found


def prologue_kernel(
    patterns,
    hidden_hbm,
    down_hbm,
    key_hbm,
    value_hbm,
    order_hbm,
    frozen_query_hbm,
    query_up_hbm,
    value_up_hbm,
    low_ref,
    kv_ref,
    bias_ref,
    frozen_query_ref,
    query_up_ref,
    value_up_ref,
    hidden_ref,
    down_ref,
    order_ref,
    sems,
    other_sems,
):
    ctx, head = lax.axis_index("ctx"), lax.axis_index("head")
    side = head % 2
    group = head // (lax.axis_size("head") // KEY_VALUE_HEADS)
    tok_dev = hidden_hbm.shape[0]
    span = tok_dev // 2
    rows = pl.ds(pl.multiple_of(side * span, span), span)
    columns = pl.ds(pl.multiple_of(group * HEAD_SIZE, HEAD_SIZE), HEAD_SIZE)
    copies = (
        pltpu.make_async_copy(hidden_hbm, hidden_ref, sems.at[0]),
        pltpu.make_async_copy(down_hbm, down_ref, sems.at[1]),
    )
    for copy in copies:
        copy.start()
    others = [
        pltpu.make_async_copy(*refs, other_sems.at[n])
        for n, refs in enumerate(
            (
                (order_hbm, order_ref),
                (key_hbm.at[rows, columns], kv_ref.at[:, pl.ds(0, HEAD_SIZE)]),
                (value_hbm.at[rows, columns], kv_ref.at[:, pl.ds(HEAD_SIZE, HEAD_SIZE)]),
                (frozen_query_hbm, frozen_query_ref),
                (query_up_hbm, query_up_ref),
                (value_up_hbm.at[:, columns], value_up_ref),
            )
        )
    ]
    for copy in others:
        copy.start()
    others[0].wait()
    row = lax.broadcasted_iota(jnp.int32, (tok_dev, tok_dev), 0)
    lane = lax.broadcasted_iota(jnp.int32, (tok_dev, tok_dev), 1)
    first_row, first_lane = row < span, lane < span
    inner = row % span - lane % span
    query_spans = jnp.where(first_row, order_ref[2 * ctx], order_ref[2 * ctx + 1])
    entries = half_blocks(patterns, ctx, side)
    for tile in range(len(patterns)):
        first, second = order_ref[entries[2 * tile][2]], order_ref[entries[2 * tile + 1][2]]
        ahead = jnp.where(first_lane, first, second) - query_spans
        bias_ref[:, tile * tok_dev : (tile + 1) * tok_dev] = jnp.where(
            ahead * span <= inner, 0.0, MASKED
        )
    for copy in copies:
        copy.wait()
    low_ref[...] = lax.dot_general(
        down_ref[...],
        hidden_ref[...],
        (((1,), (1,)), ((), ())),
        preferred_element_type=jnp.float32,
    ).astype(jnp.bfloat16)
    for copy in others[1:]:
        copy.wait()


def prologue(patterns, hidden, down, keys, values, order, frozen_query, query_up, value_up):
    tok_dev, depth = hidden.shape
    rank = down.shape[0]
    hbm = pl.BlockSpec(memory_space=pltpu.HBM)
    vmem = pl.BlockSpec(memory_space=pltpu.VMEM)
    operands = (hidden, down, keys, values, order, frozen_query, query_up, value_up)
    return pl.pallas_call(
        functools.partial(prologue_kernel, patterns),
        out_shape=(
            jax.ShapeDtypeStruct((rank, tok_dev), jnp.bfloat16),
            jax.ShapeDtypeStruct((tok_dev // 2, 2 * HEAD_SIZE), jnp.bfloat16),
            jax.ShapeDtypeStruct((tok_dev, tok_dev * len(patterns)), jnp.float32),
            jax.ShapeDtypeStruct(frozen_query.shape, jnp.bfloat16),
            jax.ShapeDtypeStruct(query_up.shape, jnp.bfloat16),
            jax.ShapeDtypeStruct((value_up.shape[0], HEAD_SIZE), jnp.bfloat16),
        ),
        in_specs=[hbm] * len(operands),
        out_specs=(vmem,) * 6,
        scratch_shapes=[
            pltpu.VMEM(hidden.shape, jnp.bfloat16),
            pltpu.VMEM(down.shape, jnp.bfloat16),
            pltpu.SMEM(order.shape, jnp.int32),
            pltpu.SemaphoreType.DMA((2,)),
            pltpu.SemaphoreType.DMA((6,)),
        ],
        compiler_params=pltpu.CompilerParams(vmem_limit_bytes=VMEM_LIMIT),
        cost_estimate=pl.CostEstimate(
            flops=2 * tok_dev * depth * rank, bytes_accessed=tok_dev * depth * 4, transcendentals=0
        ),
    )(*(pltpu.with_memory_space_constraint(x, pltpu.HBM) for x in operands))


def fill_values(value_ref, patterns, kv_refs, low_value_ref, value_up_ref):
    span = value_ref.shape[0] // (2 * len(patterns))
    side = lax.axis_index("head") % 2
    value_ref[:, HEAD_SIZE:] = jnp.ones((value_ref.shape[0], HEAD_SIZE), jnp.bfloat16)
    for n, pattern in enumerate(patterns):
        update = ADAPTER_SCALE * lax.dot_general(
            low_value_ref[n * ADAPTER_RANK : (n + 1) * ADAPTER_RANK, :],
            value_up_ref[...],
            (((0,), (0,)), ((), ())),
            preferred_element_type=jnp.float32,
        )
        own_half = (side + pattern.bit_count()) % 2 == 0
        parts = (
            jnp.where(own_half, update[:span], update[span:]),
            jnp.where(own_half, update[span:], update[:span]),
        )
        for other, kv_ref in enumerate(kv_refs):
            at = (other * len(patterns) + n) * span
            value_ref[at : at + span, :HEAD_SIZE] = (
                kv_ref[n * span : (n + 1) * span, HEAD_SIZE:].astype(jnp.float32) + parts[other]
            ).astype(jnp.bfloat16)


def scores_of(queries, kv_ref, bias):
    return (
        lax.dot_general(
            queries,
            kv_ref[:, :HEAD_SIZE],
            (((1,), (1,)), ((), ())),
            preferred_element_type=jnp.float32,
        )
        * SCORE_FACTOR
        + bias
    )


def first_kernel(
    patterns,
    frozen_query_ref,
    low_ref,
    query_up_ref,
    bias_ref,
    kv_ref,
    other_kv_ref,
    low_value_ref,
    value_up_ref,
    queries_ref,
    top_ref,
    sums_ref,
    weights_ref,
    value_ref,
):
    queries_ref[...] = (
        frozen_query_ref[...].astype(jnp.float32)
        + ADAPTER_SCALE
        * lax.dot_general(
            low_ref[:ADAPTER_RANK, :],
            query_up_ref[...],
            (((0,), (0,)), ((), ())),
            preferred_element_type=jnp.float32,
        )
    ).astype(jnp.bfloat16)
    tok_dev, width = queries_ref.shape
    heads = width // HEAD_SIZE
    count = kv_ref.shape[0]
    fill_values(
        value_ref, patterns[: len(patterns) // 2], (kv_ref, other_kv_ref), low_value_ref, value_up_ref
    )
    for head in range(heads):
        columns = slice(head * HEAD_SIZE, (head + 1) * HEAD_SIZE)
        rows = slice(head * tok_dev, (head + 1) * tok_dev)
        scores = [
            scores_of(queries_ref[:, columns], ref, bias_ref[:, n * count : (n + 1) * count])
            for n, ref in enumerate((kv_ref, other_kv_ref))
        ]
        top = jnp.maximum(
            jnp.max(scores[0], axis=1, keepdims=True), jnp.max(scores[1], axis=1, keepdims=True)
        )
        for n in range(2):
            weights_ref[rows, n * count : (n + 1) * count] = jnp.exp2(scores[n] - top).astype(
                jnp.bfloat16
            )
        top_ref[:, columns] = jnp.broadcast_to(top, (tok_dev, HEAD_SIZE))
    for head in range(heads):
        rows = slice(head * tok_dev, (head + 1) * tok_dev)
        sums_ref[rows, :] = jnp.dot(
            weights_ref[rows, :], value_ref[...], preferred_element_type=jnp.float32
        )


def second_kernel(
    part, queries_ref, bias_ref, kv_ref, old_top_ref, weights_ref, top_ref, scale_ref
):
    tok_dev, width = queries_ref.shape
    count = kv_ref.shape[0]
    before = bias_ref.shape[1] // 2 + part * count
    for head in range(width // HEAD_SIZE):
        columns = slice(head * HEAD_SIZE, (head + 1) * HEAD_SIZE)
        rows = slice(head * tok_dev, (head + 1) * tok_dev)
        scores = scores_of(queries_ref[:, columns], kv_ref, bias_ref[:, before : before + count])
        old_top = old_top_ref[:, columns]
        top = jnp.maximum(old_top, jnp.max(scores, axis=1, keepdims=True))
        for at in range(0, count, HEAD_SIZE):
            weights_ref[rows, at : at + HEAD_SIZE] = jnp.exp2(
                scores[:, at : at + HEAD_SIZE] - top
            ).astype(jnp.bfloat16)
        top_ref[:, columns] = top
        scale_ref[:, columns] = jnp.exp2(old_top - top)


def third_kernel(
    patterns,
    weights_ref,
    other_weights_ref,
    top_ref,
    scale_ref,
    other_scale_ref,
    first_sums_ref,
    kv_ref,
    other_kv_ref,
    low_value_ref,
    value_up_ref,
    attended_ref,
    normalizer_ref,
    value_ref,
):
    tok_dev, width = top_ref.shape
    fill_values(
        value_ref, patterns[len(patterns) // 2 :], (kv_ref, other_kv_ref), low_value_ref, value_up_ref
    )
    row = lax.broadcasted_iota(jnp.int32, (tok_dev, tok_dev), 0)
    lane = lax.broadcasted_iota(jnp.int32, (tok_dev, tok_dev), 1)
    for head in range(width // HEAD_SIZE):
        columns = slice(head * HEAD_SIZE, (head + 1) * HEAD_SIZE)
        rows = slice(head * tok_dev, (head + 1) * tok_dev)
        half = value_ref.shape[0] // 2
        sums = jnp.dot(weights_ref[rows, :], value_ref[:half, :], preferred_element_type=jnp.float32)
        other_sums = jnp.dot(
            other_weights_ref[rows, :], value_ref[half:, :], preferred_element_type=jnp.float32
        )
        scale, other_scale = scale_ref[:, columns], other_scale_ref[:, columns]
        weighted, total = (
            (first_sums_ref[rows, part] * scale + sums[:, part]) * other_scale + other_sums[:, part]
            for part in (slice(0, HEAD_SIZE), slice(HEAD_SIZE, 2 * HEAD_SIZE))
        )
        attended_ref[:, columns] = (weighted / total).astype(jnp.bfloat16)
        normalizer_ref[head : head + 1, :] = jnp.sum(
            jnp.where(row == lane, top_ref[:, columns] * math.log(2.0) + jnp.log(total), 0.0),
            axis=0,
            keepdims=True,
        )


def call(kernel, patterns, out_shape, scratch_shapes, work, *operands):
    vmem = pl.BlockSpec(memory_space=pltpu.VMEM)
    return pl.pallas_call(
        functools.partial(kernel, patterns),
        out_shape=out_shape,
        in_specs=[vmem] * len(operands),
        out_specs=(vmem,) * len(out_shape),
        scratch_shapes=scratch_shapes,
        compiler_params=pltpu.CompilerParams(vmem_limit_bytes=VMEM_LIMIT),
        cost_estimate=pl.CostEstimate(
            flops=work, bytes_accessed=work // 384, transcendentals=work // 768
        ),
    )(*operands)


def attend_long(patterns, ctx, head, order, frozen_query, low, query_up, kv, low_value, value_up):
    tok_dev, width = frozen_query.shape
    span = tok_dev // 2
    heads = width // HEAD_SIZE
    blocks = len(patterns)
    group = head // (lax.axis_size("head") // KEY_VALUE_HEADS)
    value_up = lax.dynamic_slice_in_dim(value_up, group * HEAD_SIZE, HEAD_SIZE, 1)
    low = low.T
    low_value = low_value.reshape(blocks, ADAPTER_RANK, tok_dev).transpose(0, 2, 1)
    queries = (
        frozen_query.astype(jnp.float32)
        + ADAPTER_SCALE
        * jnp.dot(low[:, :ADAPTER_RANK], query_up, preferred_element_type=jnp.float32)
    ).astype(jnp.bfloat16)
    queries = queries.reshape(tok_dev, heads, HEAD_SIZE).transpose(1, 0, 2).reshape(-1, HEAD_SIZE)
    side = head % 2
    entries = half_blocks(patterns, 0, 0)
    pattern = jnp.array([slot // 2 for _, _, slot in entries], jnp.int32)
    index = jnp.array([block for block, _, _ in entries], jnp.int32)
    half = (jnp.array([half for _, half, _ in entries], jnp.int32) + side) % 2
    key_spans = order[2 * (ctx ^ pattern) + half]
    inner = jnp.arange(span, dtype=jnp.int32)
    key_pos = (key_spans[:, None] * span + inner).reshape(-1)
    query_spans = lax.dynamic_slice_in_dim(order, 2 * ctx, 2)
    query_pos = jnp.tile((query_spans[:, None] * span + inner).reshape(-1), heads)
    low_rows = low_value.reshape(2 * blocks, span, ADAPTER_RANK)[2 * index + half]
    values = (
        kv[:, HEAD_SIZE:].astype(jnp.float32)
        + ADAPTER_SCALE
        * jnp.dot(
            low_rows.reshape(-1, ADAPTER_RANK), value_up, preferred_element_type=jnp.float32
        )
    ).astype(jnp.bfloat16)
    chunk = math.gcd(kv.shape[0], 1024)

    def step(number, state):
        top, total, summed = state
        at = number * chunk
        keys = lax.dynamic_slice_in_dim(kv, at, chunk, 0)[:, :HEAD_SIZE]
        scores = lax.dot_general(
            queries, keys, (((1,), (1,)), ((), ())), preferred_element_type=jnp.float32
        ) * (1.0 / math.sqrt(HEAD_SIZE))
        visible = lax.dynamic_slice_in_dim(key_pos, at, chunk)[None, :] <= query_pos[:, None]
        new_top = jnp.maximum(top, jnp.max(jnp.where(visible, scores, MASKED), axis=1))
        scale = jnp.exp(top - new_top)
        weights = jnp.where(visible, jnp.exp(scores - new_top[:, None]), 0.0)
        summed = summed * scale[:, None] + jnp.dot(
            weights.astype(jnp.bfloat16),
            lax.dynamic_slice_in_dim(values, at, chunk, 0),
            preferred_element_type=jnp.float32,
        )
        return (new_top, total * scale + jnp.sum(weights, axis=1), summed)

    rows = heads * tok_dev
    top, total, summed = lax.fori_loop(
        0,
        kv.shape[0] // chunk,
        step,
        (
            jnp.full((rows,), MASKED, jnp.float32),
            jnp.zeros((rows,), jnp.float32),
            jnp.zeros((rows, HEAD_SIZE), jnp.float32),
        ),
    )
    attended = (summed / total[:, None]).astype(jnp.bfloat16)
    attended = attended.reshape(heads, tok_dev, HEAD_SIZE).transpose(1, 0, 2)
    return attended.reshape(tok_dev, width), (top + jnp.log(total)).reshape(heads, tok_dev)


def local(
    hidden,
    frozen_query_rows,
    frozen_key_rows,
    frozen_value_rows,
    adapter_down_factors,
    query_up_factor,
    value_up_factor,
    slot_span_order,
):
    ctx_count, head_count = lax.axis_size("ctx"), lax.axis_size("head")
    ctx, head = lax.axis_index("ctx"), lax.axis_index("head")
    bits = [ctx_count >> k for k in range(1, ctx_count.bit_length())]
    patterns = gather_patterns(bits)

    low, kv, bias, frozen_query, query_up, value_up = prologue(
        patterns,
        hidden,
        adapter_down_factors.T,
        frozen_key_rows,
        frozen_value_rows,
        slot_span_order,
        frozen_query_rows,
        query_up_factor,
        value_up_factor,
    )
    head_bit = 1
    while head_bit < head_count:
        other = exchange(low, 0, head_bit | 1)
        low = (low.astype(jnp.float32) + other.astype(jnp.float32)).astype(jnp.bfloat16)
        head_bit *= 2
    low_value = low[ADAPTER_RANK:]
    short = hidden.shape[0] * ctx_count <= 1024
    for bit in bits[:-1]:
        low_value = jnp.concatenate([low_value, exchange(low_value, bit, 1)], axis=0)
        kv = jnp.concatenate([kv, exchange(kv, bit, 1)], axis=0)
    if short:
        kv, _ = lax.optimization_barrier((kv, low))
    last_low = exchange(low_value, bits[-1], 1)
    last_kv = exchange(kv, bits[-1], 1)
    other_kv = exchange(kv, 0, 1)
    last_other_kv = exchange(last_kv, 0, 1)
    if not short:
        return attend_long(
            patterns,
            ctx,
            head,
            slot_span_order,
            frozen_query_rows,
            low,
            query_up_factor,
            jnp.concatenate([kv, other_kv, last_kv, last_other_kv], axis=0),
            jnp.concatenate([low_value, last_low], axis=0),
            value_up_factor,
        )
    tok_dev, width = frozen_query.shape
    rows = width // HEAD_SIZE * tok_dev
    key_count = 2 * kv.shape[0]
    work = 6 * tok_dev * width * key_count
    wide = jax.ShapeDtypeStruct((tok_dev, width), jnp.float32)
    value_scratch = pltpu.VMEM((key_count, 2 * HEAD_SIZE), jnp.bfloat16)
    queries, first_top, sums = call(
        first_kernel,
        patterns,
        (jax.ShapeDtypeStruct((tok_dev, width), jnp.bfloat16), wide, jax.ShapeDtypeStruct((rows, 2 * HEAD_SIZE), jnp.float32)),
        [pltpu.VMEM((rows, key_count), jnp.bfloat16), value_scratch],
        30 * work,
        frozen_query,
        low,
        query_up,
        bias,
        kv,
        other_kv,
        low_value,
        value_up,
    )
    parts = []
    top = first_top
    for part, rows_of_part in enumerate((last_kv, last_other_kv)):
        weights, top, scale = call(
            second_kernel,
            part,
            (jax.ShapeDtypeStruct((rows, key_count // 2), jnp.bfloat16), wide, wide),
            [],
            15 * work,
            queries,
            bias,
            rows_of_part,
            top,
        )
        parts.append((weights, scale))
    (weights, scale), (other_weights, other_scale) = parts
    return call(
        third_kernel,
        patterns,
        (
            jax.ShapeDtypeStruct((tok_dev, width), jnp.bfloat16),
            jax.ShapeDtypeStruct((width // HEAD_SIZE, tok_dev), jnp.float32),
        ),
        [value_scratch],
        work,
        weights,
        other_weights,
        top,
        scale,
        other_scale,
        sums,
        last_kv,
        last_other_kv,
        last_low,
        value_up,
    )


def solution(mesh):
    placed = (
        P("ctx", "head"),
        P("ctx", "head"),
        P("ctx", None),
        P("ctx", None),
        P("head", None),
        P(None, "head"),
        P(),
        P(),
    )
    return jax.shard_map(
        local,
        mesh=mesh,
        in_specs=placed,
        out_specs=(P("ctx", "head"), P("head", "ctx")),
        check_vma=False,
    )
```

```python
import functools
import math

import jax
import jax.numpy as jnp
from jax import lax
from jax.experimental import pallas as pl
from jax.experimental.pallas import tpu as pltpu
from jax.sharding import PartitionSpec as P

HEAD_SIZE = 128
KEY_VALUE_HEADS = 2
ADAPTER_RANK = 32
ADAPTER_SCALE = 0.5
MASKED = -1e30
AXES = ("ctx", "head")
SCORE_FACTOR = math.log2(math.e) / math.sqrt(HEAD_SIZE)
VMEM_LIMIT = 24 * 1024 * 1024


def exchange(value, ctx_bit, head_bits):
    ctx_count, head_count = lax.axis_size("ctx"), lax.axis_size("head")
    pairs = [
        (i * head_count + h, (i ^ ctx_bit) * head_count + (h ^ head_bits))
        for i in range(ctx_count)
        for h in range(head_count)
    ]
    return lax.ppermute(value, AXES, pairs)


def gather_patterns(bits):
    patterns = [0]
    for bit in bits:
        patterns += [p ^ bit for p in patterns]
    return patterns


def half_blocks(patterns, ctx, side):
    half_count = len(patterns) // 2
    found = []
    for first in (0, half_count):
        for other in (0, 1):
            for block in range(first, first + half_count):
                half = (side + patterns[block].bit_count() + other) % 2
                found.append((block, half, 2 * (ctx ^ patterns[block]) + half))
    return found


def prologue_kernel(
    patterns,
    hidden_hbm,
    down_hbm,
    key_hbm,
    value_hbm,
    order_hbm,
    frozen_query_hbm,
    query_up_hbm,
    value_up_hbm,
    low_ref,
    kv_ref,
    bias_ref,
    frozen_query_ref,
    query_up_ref,
    value_up_ref,
    hidden_ref,
    down_ref,
    order_ref,
    sems,
    other_sems,
):
    ctx, head = lax.axis_index("ctx"), lax.axis_index("head")
    side = head % 2
    group = head // (lax.axis_size("head") // KEY_VALUE_HEADS)
    tok_dev = hidden_hbm.shape[0]
    span = tok_dev // 2
    rows = pl.ds(pl.multiple_of(side * span, span), span)
    columns = pl.ds(pl.multiple_of(group * HEAD_SIZE, HEAD_SIZE), HEAD_SIZE)
    copies = (
        pltpu.make_async_copy(hidden_hbm, hidden_ref, sems.at[0]),
        pltpu.make_async_copy(down_hbm, down_ref, sems.at[1]),
    )
    for copy in copies:
        copy.start()
    others = [
        pltpu.make_async_copy(*refs, other_sems.at[n])
        for n, refs in enumerate(
            (
                (order_hbm, order_ref),
                (key_hbm.at[rows, columns], kv_ref.at[:, pl.ds(0, HEAD_SIZE)]),
                (value_hbm.at[rows, columns], kv_ref.at[:, pl.ds(HEAD_SIZE, HEAD_SIZE)]),
                (frozen_query_hbm, frozen_query_ref),
                (query_up_hbm, query_up_ref),
                (value_up_hbm.at[:, columns], value_up_ref),
            )
        )
    ]
    for copy in others:
        copy.start()
    others[0].wait()
    row = lax.broadcasted_iota(jnp.int32, (tok_dev, tok_dev), 0)
    lane = lax.broadcasted_iota(jnp.int32, (tok_dev, tok_dev), 1)
    first_row, first_lane = row < span, lane < span
    inner = row % span - lane % span
    query_spans = jnp.where(first_row, order_ref[2 * ctx], order_ref[2 * ctx + 1])
    entries = half_blocks(patterns, ctx, side)
    for tile in range(len(patterns)):
        first, second = order_ref[entries[2 * tile][2]], order_ref[entries[2 * tile + 1][2]]
        ahead = jnp.where(first_lane, first, second) - query_spans
        bias_ref[:, tile * tok_dev : (tile + 1) * tok_dev] = jnp.where(
            ahead * span <= inner, 0.0, MASKED
        )
    for copy in copies:
        copy.wait()
    low_ref[...] = lax.dot_general(
        down_ref[...],
        hidden_ref[...],
        (((1,), (1,)), ((), ())),
        preferred_element_type=jnp.float32,
    ).astype(jnp.bfloat16)
    for copy in others[1:]:
        copy.wait()


def prologue(patterns, hidden, down, keys, values, order, frozen_query, query_up, value_up):
    tok_dev, depth = hidden.shape
    rank = down.shape[0]
    hbm = pl.BlockSpec(memory_space=pltpu.HBM)
    vmem = pl.BlockSpec(memory_space=pltpu.VMEM)
    operands = (hidden, down, keys, values, order, frozen_query, query_up, value_up)
    return pl.pallas_call(
        functools.partial(prologue_kernel, patterns),
        out_shape=(
            jax.ShapeDtypeStruct((rank, tok_dev), jnp.bfloat16),
            jax.ShapeDtypeStruct((tok_dev // 2, 2 * HEAD_SIZE), jnp.bfloat16),
            jax.ShapeDtypeStruct((tok_dev, tok_dev * len(patterns)), jnp.float32),
            jax.ShapeDtypeStruct(frozen_query.shape, jnp.bfloat16),
            jax.ShapeDtypeStruct(query_up.shape, jnp.bfloat16),
            jax.ShapeDtypeStruct((value_up.shape[0], HEAD_SIZE), jnp.bfloat16),
        ),
        in_specs=[hbm] * len(operands),
        out_specs=(vmem,) * 6,
        scratch_shapes=[
            pltpu.VMEM(hidden.shape, jnp.bfloat16),
            pltpu.VMEM(down.shape, jnp.bfloat16),
            pltpu.SMEM(order.shape, jnp.int32),
            pltpu.SemaphoreType.DMA((2,)),
            pltpu.SemaphoreType.DMA((6,)),
        ],
        compiler_params=pltpu.CompilerParams(vmem_limit_bytes=VMEM_LIMIT),
        cost_estimate=pl.CostEstimate(
            flops=2 * tok_dev * depth * rank, bytes_accessed=tok_dev * depth * 4, transcendentals=0
        ),
    )(*(pltpu.with_memory_space_constraint(x, pltpu.HBM) for x in operands))


def fill_values(value_ref, patterns, kv_refs, low_value_ref, value_up_ref):
    span = value_ref.shape[0] // (2 * len(patterns))
    side = lax.axis_index("head") % 2
    value_ref[:, HEAD_SIZE:] = jnp.ones((value_ref.shape[0], HEAD_SIZE), jnp.bfloat16)
    for n, pattern in enumerate(patterns):
        update = ADAPTER_SCALE * lax.dot_general(
            low_value_ref[n * ADAPTER_RANK : (n + 1) * ADAPTER_RANK, :],
            value_up_ref[...],
            (((0,), (0,)), ((), ())),
            preferred_element_type=jnp.float32,
        )
        own_half = (side + pattern.bit_count()) % 2 == 0
        parts = (
            jnp.where(own_half, update[:span], update[span:]),
            jnp.where(own_half, update[span:], update[:span]),
        )
        for other, kv_ref in enumerate(kv_refs):
            at = (other * len(patterns) + n) * span
            value_ref[at : at + span, :HEAD_SIZE] = (
                kv_ref[n * span : (n + 1) * span, HEAD_SIZE:].astype(jnp.float32) + parts[other]
            ).astype(jnp.bfloat16)


def scores_of(queries, kv_ref, bias):
    return (
        lax.dot_general(
            queries,
            kv_ref[:, :HEAD_SIZE],
            (((1,), (1,)), ((), ())),
            preferred_element_type=jnp.float32,
        )
        * SCORE_FACTOR
        + bias
    )


def first_kernel(
    patterns,
    frozen_query_ref,
    low_ref,
    query_up_ref,
    bias_ref,
    kv_ref,
    other_kv_ref,
    low_value_ref,
    value_up_ref,
    queries_ref,
    top_ref,
    sums_ref,
    weights_ref,
    value_ref,
):
    queries_ref[...] = (
        frozen_query_ref[...].astype(jnp.float32)
        + ADAPTER_SCALE
        * lax.dot_general(
            low_ref[:ADAPTER_RANK, :],
            query_up_ref[...],
            (((0,), (0,)), ((), ())),
            preferred_element_type=jnp.float32,
        )
    ).astype(jnp.bfloat16)
    tok_dev, width = queries_ref.shape
    heads = width // HEAD_SIZE
    count = kv_ref.shape[0]
    fill_values(
        value_ref, patterns[: len(patterns) // 2], (kv_ref, other_kv_ref), low_value_ref, value_up_ref
    )
    for head in range(heads):
        columns = slice(head * HEAD_SIZE, (head + 1) * HEAD_SIZE)
        rows = slice(head * tok_dev, (head + 1) * tok_dev)
        scores = [
            scores_of(queries_ref[:, columns], ref, bias_ref[:, n * count : (n + 1) * count])
            for n, ref in enumerate((kv_ref, other_kv_ref))
        ]
        top = jnp.maximum(
            jnp.max(scores[0], axis=1, keepdims=True), jnp.max(scores[1], axis=1, keepdims=True)
        )
        for n in range(2):
            weights_ref[rows, n * count : (n + 1) * count] = jnp.exp2(scores[n] - top).astype(
                jnp.bfloat16
            )
        top_ref[:, columns] = jnp.broadcast_to(top, (tok_dev, HEAD_SIZE))
    for head in range(heads):
        rows = slice(head * tok_dev, (head + 1) * tok_dev)
        sums_ref[rows, :] = jnp.dot(
            weights_ref[rows, :], value_ref[...], preferred_element_type=jnp.float32
        )


def second_kernel(
    patterns, queries_ref, bias_ref, kv_ref, other_kv_ref, first_top_ref, weights_ref, top_ref, scale_ref
):
    tok_dev, width = queries_ref.shape
    count = kv_ref.shape[0]
    before = bias_ref.shape[1] // 2
    for head in range(width // HEAD_SIZE):
        columns = slice(head * HEAD_SIZE, (head + 1) * HEAD_SIZE)
        rows = slice(head * tok_dev, (head + 1) * tok_dev)
        scores = [
            scores_of(
                queries_ref[:, columns],
                ref,
                bias_ref[:, before + n * count : before + (n + 1) * count],
            )
            for n, ref in enumerate((kv_ref, other_kv_ref))
        ]
        new_top = jnp.maximum(
            jnp.max(scores[0], axis=1, keepdims=True), jnp.max(scores[1], axis=1, keepdims=True)
        )
        first_top = first_top_ref[:, columns]
        top = jnp.maximum(first_top, new_top)
        for n in range(2):
            for at in range(0, count, HEAD_SIZE):
                weights_ref[rows, n * count + at : n * count + at + HEAD_SIZE] = jnp.exp2(
                    scores[n][:, at : at + HEAD_SIZE] - top
                ).astype(jnp.bfloat16)
        top_ref[:, columns] = top
        scale_ref[:, columns] = jnp.exp2(first_top - top)


def third_kernel(
    patterns,
    weights_ref,
    top_ref,
    scale_ref,
    first_sums_ref,
    kv_ref,
    other_kv_ref,
    low_value_ref,
    value_up_ref,
    attended_ref,
    normalizer_ref,
    value_ref,
):
    tok_dev, width = top_ref.shape
    fill_values(
        value_ref, patterns[len(patterns) // 2 :], (kv_ref, other_kv_ref), low_value_ref, value_up_ref
    )
    row = lax.broadcasted_iota(jnp.int32, (tok_dev, tok_dev), 0)
    lane = lax.broadcasted_iota(jnp.int32, (tok_dev, tok_dev), 1)
    for head in range(width // HEAD_SIZE):
        columns = slice(head * HEAD_SIZE, (head + 1) * HEAD_SIZE)
        rows = slice(head * tok_dev, (head + 1) * tok_dev)
        sums = jnp.dot(weights_ref[rows, :], value_ref[...], preferred_element_type=jnp.float32)
        scale = scale_ref[:, columns]
        total = first_sums_ref[rows, HEAD_SIZE:] * scale + sums[:, HEAD_SIZE:]
        attended_ref[:, columns] = (
            (first_sums_ref[rows, :HEAD_SIZE] * scale + sums[:, :HEAD_SIZE]) / total
        ).astype(jnp.bfloat16)
        normalizer_ref[head : head + 1, :] = jnp.sum(
            jnp.where(row == lane, top_ref[:, columns] * math.log(2.0) + jnp.log(total), 0.0),
            axis=0,
            keepdims=True,
        )


def call(kernel, patterns, out_shape, scratch_shapes, work, *operands):
    vmem = pl.BlockSpec(memory_space=pltpu.VMEM)
    return pl.pallas_call(
        functools.partial(kernel, patterns),
        out_shape=out_shape,
        in_specs=[vmem] * len(operands),
        out_specs=(vmem,) * len(out_shape),
        scratch_shapes=scratch_shapes,
        compiler_params=pltpu.CompilerParams(vmem_limit_bytes=VMEM_LIMIT),
        cost_estimate=pl.CostEstimate(
            flops=work, bytes_accessed=work // 384, transcendentals=work // 768
        ),
    )(*operands)


def attend_long(patterns, ctx, head, order, frozen_query, low, query_up, kv, low_value, value_up):
    tok_dev, width = frozen_query.shape
    span = tok_dev // 2
    heads = width // HEAD_SIZE
    blocks = len(patterns)
    group = head // (lax.axis_size("head") // KEY_VALUE_HEADS)
    value_up = lax.dynamic_slice_in_dim(value_up, group * HEAD_SIZE, HEAD_SIZE, 1)
    low = low.T
    low_value = low_value.reshape(blocks, ADAPTER_RANK, tok_dev).transpose(0, 2, 1)
    queries = (
        frozen_query.astype(jnp.float32)
        + ADAPTER_SCALE
        * jnp.dot(low[:, :ADAPTER_RANK], query_up, preferred_element_type=jnp.float32)
    ).astype(jnp.bfloat16)
    queries = queries.reshape(tok_dev, heads, HEAD_SIZE).transpose(1, 0, 2).reshape(-1, HEAD_SIZE)
    side = head % 2
    entries = half_blocks(patterns, 0, 0)
    pattern = jnp.array([slot // 2 for _, _, slot in entries], jnp.int32)
    index = jnp.array([block for block, _, _ in entries], jnp.int32)
    half = (jnp.array([half for _, half, _ in entries], jnp.int32) + side) % 2
    key_spans = order[2 * (ctx ^ pattern) + half]
    inner = jnp.arange(span, dtype=jnp.int32)
    key_pos = (key_spans[:, None] * span + inner).reshape(-1)
    query_spans = lax.dynamic_slice_in_dim(order, 2 * ctx, 2)
    query_pos = jnp.tile((query_spans[:, None] * span + inner).reshape(-1), heads)
    low_rows = low_value.reshape(2 * blocks, span, ADAPTER_RANK)[2 * index + half]
    values = (
        kv[:, HEAD_SIZE:].astype(jnp.float32)
        + ADAPTER_SCALE
        * jnp.dot(
            low_rows.reshape(-1, ADAPTER_RANK), value_up, preferred_element_type=jnp.float32
        )
    ).astype(jnp.bfloat16)
    chunk = math.gcd(kv.shape[0], 1024)

    def step(number, state):
        top, total, summed = state
        at = number * chunk
        keys = lax.dynamic_slice_in_dim(kv, at, chunk, 0)[:, :HEAD_SIZE]
        scores = lax.dot_general(
            queries, keys, (((1,), (1,)), ((), ())), preferred_element_type=jnp.float32
        ) * (1.0 / math.sqrt(HEAD_SIZE))
        visible = lax.dynamic_slice_in_dim(key_pos, at, chunk)[None, :] <= query_pos[:, None]
        new_top = jnp.maximum(top, jnp.max(jnp.where(visible, scores, MASKED), axis=1))
        scale = jnp.exp(top - new_top)
        weights = jnp.where(visible, jnp.exp(scores - new_top[:, None]), 0.0)
        summed = summed * scale[:, None] + jnp.dot(
            weights.astype(jnp.bfloat16),
            lax.dynamic_slice_in_dim(values, at, chunk, 0),
            preferred_element_type=jnp.float32,
        )
        return (new_top, total * scale + jnp.sum(weights, axis=1), summed)

    rows = heads * tok_dev
    top, total, summed = lax.fori_loop(
        0,
        kv.shape[0] // chunk,
        step,
        (
            jnp.full((rows,), MASKED, jnp.float32),
            jnp.zeros((rows,), jnp.float32),
            jnp.zeros((rows, HEAD_SIZE), jnp.float32),
        ),
    )
    attended = (summed / total[:, None]).astype(jnp.bfloat16)
    attended = attended.reshape(heads, tok_dev, HEAD_SIZE).transpose(1, 0, 2)
    return attended.reshape(tok_dev, width), (top + jnp.log(total)).reshape(heads, tok_dev)


def local(
    hidden,
    frozen_query_rows,
    frozen_key_rows,
    frozen_value_rows,
    adapter_down_factors,
    query_up_factor,
    value_up_factor,
    slot_span_order,
):
    ctx_count, head_count = lax.axis_size("ctx"), lax.axis_size("head")
    ctx, head = lax.axis_index("ctx"), lax.axis_index("head")
    bits = [ctx_count >> k for k in range(1, ctx_count.bit_length())]
    patterns = gather_patterns(bits)

    low, kv, bias, frozen_query, query_up, value_up = prologue(
        patterns,
        hidden,
        adapter_down_factors.T,
        frozen_key_rows,
        frozen_value_rows,
        slot_span_order,
        frozen_query_rows,
        query_up_factor,
        value_up_factor,
    )
    head_bit = 1
    while head_bit < head_count:
        other = exchange(low, 0, head_bit | 1)
        low = (low.astype(jnp.float32) + other.astype(jnp.float32)).astype(jnp.bfloat16)
        head_bit *= 2
    low_value = low[ADAPTER_RANK:]
    short = hidden.shape[0] * ctx_count <= 1024
    for bit in bits[:-1]:
        cores = 0 if bit == bits[0] else 1
        low_value = jnp.concatenate([low_value, exchange(low_value, bit, cores)], axis=0)
        kv = jnp.concatenate([kv, exchange(kv, bit, 1)], axis=0)
    if short:
        kv, _ = lax.optimization_barrier((kv, low))
    last_low = exchange(low_value, bits[-1], 1)
    last_kv = exchange(kv, bits[-1], 1)
    other_kv = exchange(kv, 0, 1)
    last_other_kv = exchange(last_kv, 0, 1)
    if not short:
        return attend_long(
            patterns,
            ctx,
            head,
            slot_span_order,
            frozen_query_rows,
            low,
            query_up_factor,
            jnp.concatenate([kv, other_kv, last_kv, last_other_kv], axis=0),
            jnp.concatenate([low_value, last_low], axis=0),
            value_up_factor,
        )
    tok_dev, width = frozen_query.shape
    rows = width // HEAD_SIZE * tok_dev
    key_count = 2 * kv.shape[0]
    work = 6 * tok_dev * width * key_count
    wide = jax.ShapeDtypeStruct((tok_dev, width), jnp.float32)
    value_scratch = pltpu.VMEM((key_count, 2 * HEAD_SIZE), jnp.bfloat16)
    queries, first_top, sums = call(
        first_kernel,
        patterns,
        (jax.ShapeDtypeStruct((tok_dev, width), jnp.bfloat16), wide, jax.ShapeDtypeStruct((rows, 2 * HEAD_SIZE), jnp.float32)),
        [pltpu.VMEM((rows, key_count), jnp.bfloat16), value_scratch],
        30 * work,
        frozen_query,
        low,
        query_up,
        bias,
        kv,
        other_kv,
        low_value,
        value_up,
    )
    weights, top, scale = call(
        second_kernel,
        patterns,
        (jax.ShapeDtypeStruct((rows, key_count), jnp.bfloat16), wide, wide),
        [],
        30 * work,
        queries,
        bias,
        last_kv,
        last_other_kv,
        first_top,
    )
    return call(
        third_kernel,
        patterns,
        (
            jax.ShapeDtypeStruct((tok_dev, width), jnp.bfloat16),
            jax.ShapeDtypeStruct((width // HEAD_SIZE, tok_dev), jnp.float32),
        ),
        [value_scratch],
        work,
        weights,
        top,
        scale,
        sums,
        last_kv,
        last_other_kv,
        last_low,
        value_up,
    )


def solution(mesh):
    placed = (
        P("ctx", "head"),
        P("ctx", "head"),
        P("ctx", None),
        P("ctx", None),
        P("head", None),
        P(None, "head"),
        P(),
        P(),
    )
    return jax.shard_map(
        local,
        mesh=mesh,
        in_specs=placed,
        out_specs=(P("ctx", "head"), P("head", "ctx")),
        check_vma=False,
    )
```
